256 devices in a mesh: row: 16 (over z_hi, x), col: 16 (over z_lo, y, core).
Axes of the slice: x: 4, y: 4, z: 8 (z_hi: 4, z_lo: 2; z = z_hi * 2 + z_lo), core: 2. Of those that a mesh axis runs over, the one named last changes fastest.
Arguments:
- features: bfloat16 [196608, 256], P(('row', 'col')), may hold values from -6 to 6
- node_order: int32 [256, 768], P(('row', 'col')), may hold values from 0 to 767, each once within a row
- block_rows: int32 [16, 16, 192], P('row', 'col'), may hold values from 0 to 95
- block_cols: int32 [16, 16, 192], P('row', 'col'), may hold values from 0 to 95
- block_counts: int32 [16, 16], P('row', 'col'), may hold values from 32 to 192, as said below
- adjacency: bfloat16 [16, 16, 192, 128, 128], P('row', 'col'), may hold values from -0.125 to 0.125
- weight_one: bfloat16 [256, 256], replicated, may hold values from -0.375 to 0.375
- weight_two: bfloat16 [256, 256], replicated, may hold values from -0.375 to 0.375
Outputs:
- embeddings: bfloat16 [196608, 256], P(('row', 'col'))
The draws below stay inside these ranges and needn't reach their ends.
Inputs may be any that keep to these rules, and one draw needn't show every extreme that they name: `block_counts`: every tile uses between 32 and 192 slots; some tile uses all 192. `block_rows`: coordinates may repeat within a tile.
All inputs are finite; a program needn't handle non-finite values.
Results may differ from the reference program's by a relative error of at most 0.028.
Values may be sent and summed in bfloat16 or wider, within the bound.
A program may use at most 128 MiB of HBM per device.

```python
import jax
import jax.numpy as jnp
from jax import lax

F = 256
BS = 128
SLAB = 768
NZ_MOST = 192
NODES = 196608
ROWGRP = 12288
COLGRP = 12288
ROWBLK = 96
COLBLK = 96
N_ROW = 16
N_COL = 16


def draw_block_counts(key, part):
    key = jax.random.fold_in(key, 7)
    key_divide, key_choose = jax.random.split(key)
    divisor = jax.random.randint(key_divide, (N_ROW * N_COL,), 1, 7)
    counts = NZ_MOST // divisor
    chosen = jax.random.randint(key_choose, (), 0, N_ROW * N_COL)
    counts = jnp.where(jnp.arange(N_ROW * N_COL) == chosen, NZ_MOST, counts)
    return counts.reshape(N_ROW, N_COL).astype(jnp.int32)


def place_ends(array, stream_key, least, top_value):
    extent = array.shape
    place = [jax.random.randint(jax.random.fold_in(stream_key, axis), (), 0, extent[axis]) for axis in range(len(extent))]
    array = array.at[tuple(place)].set(least)
    longest = extent.index(max(extent))
    place[longest] = (place[longest] + 1) % extent[longest]
    return array.at[tuple(place)].set(top_value)


def level_of(stream_key, dims, shards, low, top_value):
    level, own = 1.0, jax.random.fold_in(stream_key, 6)
    for axis_at, shards_of in shards:
        draws = jnp.exp(jax.random.uniform(jax.random.fold_in(own, axis_at), (shards_of,), jnp.float32, low / len(shards), top_value / len(shards)))
        level = level * jnp.repeat(draws, dims[axis_at] // shards_of).reshape([-1 if axis == axis_at else 1 for axis in range(len(dims))])
    return level


def noise(stream_key, shape, scale, reach, cuts=(), held_as=jnp.bfloat16):
    gain = level_of(stream_key, shape, cuts, -0.22, 0.18) if cuts else 1.0
    entries = jax.random.normal(stream_key, shape, jnp.float32) * scale * gain
    return jnp.minimum(jnp.maximum(entries, -reach), reach).astype(held_as)


def setup_inputs(seed: int = 0) -> dict:
    arg_keys = jax.random.split(jax.random.key(seed), 9)
    return {
        "features": noise(arg_keys[0], (NODES, F), 1.0, 6.0, ((0, 256),)),
        "node_order": jax.vmap(lambda own: jax.random.permutation(own, SLAB))(jax.random.split(arg_keys[1], (N_ROW * N_COL))).reshape((N_ROW * N_COL, SLAB)).astype(jnp.int32),
        "block_rows": place_ends(jax.random.randint(arg_keys[2], (N_ROW, N_COL, NZ_MOST), 0, ROWBLK), jax.random.fold_in(arg_keys[2], 1), 0, ROWBLK - 1).astype(jnp.int32),
        "block_cols": place_ends(jax.random.randint(arg_keys[3], (N_ROW, N_COL, NZ_MOST), 0, COLBLK), jax.random.fold_in(arg_keys[3], 1), 0, COLBLK - 1).astype(jnp.int32),
        "block_counts": draw_block_counts(jax.random.fold_in(arg_keys[8], 71), 0),
        "adjacency": noise(arg_keys[5], (N_ROW, N_COL, NZ_MOST, BS, BS), (BS * BS * NZ_MOST // (2 * SLAB)) ** -0.5, 0.125, ((0, 16), (1, 16))),
        "weight_one": noise(arg_keys[6], (F, F), F ** -0.5, 0.375),
        "weight_two": noise(arg_keys[7], (F, F), F ** -0.5, 0.375),
    }


def block_product(panel_rows, tile_values, source_ids, target_ids, live_count, out_blocks, transposed):
    block_size = tile_values.shape[-1]
    slot_count = tile_values.shape[0]
    stride = min(64, slot_count)
    feature_width = panel_rows.shape[1]
    tile_set = panel_rows.reshape(panel_rows.shape[0] // block_size, block_size, feature_width)
    target_grid = jnp.arange(out_blocks, dtype=jnp.int32)
    pattern = "bji,bjk->bik" if transposed else "bij,bjk->bik"

    def accumulate(round_index, carried):
        offset = round_index * stride
        blocks_now = lax.dynamic_slice_in_dim(tile_values, offset, stride, 0)
        source_now = lax.dynamic_slice_in_dim(source_ids, offset, stride, 0)
        target_now = lax.dynamic_slice_in_dim(target_ids, offset, stride, 0)
        chosen = jnp.take(tile_set, source_now, axis=0)
        product = jnp.einsum(pattern, blocks_now.astype(jnp.float32), chosen.astype(jnp.float32))
        active = (offset + jnp.arange(stride, dtype=jnp.int32)) < live_count
        selector = jnp.where((target_now[None, :] == target_grid[:, None]) & active[None, :], 1.0, 0.0).astype(jnp.float32)
        return carried + jnp.einsum("gb,bik->gik", selector, product)

    summed = lax.fori_loop(0, slot_count // stride, accumulate, jnp.zeros((out_blocks, block_size, feature_width), jnp.float32))
    return summed.reshape(out_blocks * block_size, feature_width)


def rounded(values):
    return lax.optimization_barrier(values.astype(jnp.bfloat16)).astype(jnp.float32)


def reference(features, node_order, block_rows, block_cols, block_counts, adjacency, weight_one, weight_two):
    feature_width = features.shape[1]
    slabs = features.reshape(N_ROW * N_COL, SLAB, feature_width)
    initial = jnp.take_along_axis(slabs, node_order[:, :, None], axis=1).reshape(NODES, feature_width)
    row_panels = initial.reshape(N_ROW, ROWGRP, feature_width)

    def column_total(col_index):
        def add_row(carried, row_index):
            partial_value = block_product(row_panels[row_index], adjacency[row_index, col_index], block_rows[row_index, col_index], block_cols[row_index, col_index], block_counts[row_index, col_index], COLBLK, True)
            return carried + rounded(partial_value), None
        summed, unused = lax.scan(add_row, jnp.zeros((COLGRP, feature_width), jnp.float32), jnp.arange(N_ROW, dtype=jnp.int32))
        return summed

    first = lax.map(column_total, jnp.arange(N_COL, dtype=jnp.int32)).reshape(NODES, feature_width).astype(jnp.bfloat16)
    hidden = jax.nn.relu(jnp.dot(first, weight_one, preferred_element_type=jnp.float32)).astype(jnp.bfloat16)
    column_panels = hidden.reshape(N_COL, COLGRP, feature_width)

    def row_total(row_index):
        def add_column(carried, col_index):
            partial_value = block_product(column_panels[col_index], adjacency[row_index, col_index], block_cols[row_index, col_index], block_rows[row_index, col_index], block_counts[row_index, col_index], ROWBLK, False)
            return carried + rounded(partial_value), None
        summed, unused = lax.scan(add_column, jnp.zeros((ROWGRP, feature_width), jnp.float32), jnp.arange(N_COL, dtype=jnp.int32))
        return summed

    second = lax.map(row_total, jnp.arange(N_ROW, dtype=jnp.int32)).reshape(NODES, feature_width).astype(jnp.bfloat16)
    return jax.nn.relu(jnp.dot(second, weight_two, preferred_element_type=jnp.float32)).astype(jnp.bfloat16)
```

```python
import functools
import jax
import jax.numpy as jnp
from jax import lax
from jax.experimental import pallas as pl
from jax.experimental.pallas import tpu as pltpu
from jax.sharding import PartitionSpec as P

CHUNK = 16


def product_kernel(
    transposed, unroll, source_ref, target_ref, count_ref, panel_hbm, tile_hbm, out_hbm,
    tiles, panel, total, tile_sem, panel_sem, out_sem,
):
    slots, block = tile_hbm.shape[0], tile_hbm.shape[1]
    blocks = panel_hbm.shape[0]
    chunks = slots // CHUNK
    live = count_ref[0, 0]

    def tile_copy(c):
        part = pl.ds(c * CHUNK, CHUNK)
        return pltpu.make_async_copy(tile_hbm.at[part], tiles.at[part], tile_sem.at[c])

    panel_copy = pltpu.make_async_copy(panel_hbm, panel, panel_sem)
    panel_copy.start()
    for c in range(chunks):
        pl.when(c * CHUNK < live)(lambda c=c: tile_copy(c).start())

    @pl.loop(0, blocks)
    def _(g):
        total[g] = jnp.zeros_like(total[g])

    panel_copy.wait()
    dims = (((0,), (0,)), ((), ())) if transposed else (((1,), (0,)), ((), ()))

    def one_chunk(c):
        tile_copy(c).wait()

        @pl.loop(0, CHUNK // unroll)
        def _(step):
            first = c * CHUNK + step * unroll

            @pl.when(first < live)
            def _():
                products, targets = [], []
                for k in range(unroll):
                    slot = first + k
                    products.append(lax.dot_general(
                        tiles[slot], panel[source_ref[0, slot]], dims,
                        preferred_element_type=jnp.float32,
                    ))
                    targets.append(jnp.where(slot < live, target_ref[0, slot], blocks))
                for k in range(unroll):
                    total[targets[k]] += products[k]

    for c in range(chunks):
        pl.when(c * CHUNK < live)(functools.partial(one_chunk, c))

    rounds = 12
    share = blocks // rounds
    copies = []
    for c in range(rounds):
        @pl.loop(c * share, (c + 1) * share)
        def _(g):
            panel[g] = total[g].astype(panel.dtype)
        part = pl.ds(c * share, share)
        copies.append(pltpu.make_async_copy(panel.at[part], out_hbm.at[part], out_sem.at[c]))
        copies[-1].start()
    for copy in copies:
        copy.wait()


def block_product(panel, tiles, source_ids, target_ids, count, transposed, unroll=8):
    slots, block, _ = tiles.shape
    blocks, _, width = panel.shape
    smem = pl.BlockSpec(memory_space=pltpu.SMEM)
    hbm = pl.BlockSpec(memory_space=pl.ANY)
    return pl.pallas_call(
        functools.partial(product_kernel, transposed, unroll),
        out_shape=jax.ShapeDtypeStruct(panel.shape, panel.dtype),
        in_specs=[smem, smem, smem, hbm, hbm],
        out_specs=hbm,
        scratch_shapes=[
            pltpu.VMEM(tiles.shape, tiles.dtype),
            pltpu.VMEM(panel.shape, panel.dtype),
            pltpu.VMEM((blocks + 1, block, width), jnp.float32),
            pltpu.SemaphoreType.DMA((slots // CHUNK,)),
            pltpu.SemaphoreType.DMA,
            pltpu.SemaphoreType.DMA((12,)),
        ],
        compiler_params=pltpu.CompilerParams(vmem_limit_bytes=48 << 20),
        cost_estimate=pl.CostEstimate(
            flops=2 * slots * block * block * width, transcendentals=0,
            bytes_accessed=2 * (tiles.size + 2 * panel.size),
        ),
    )(source_ids, target_ids, count, panel, tiles)


def on_device(
    features, node_order, block_rows, block_cols, block_counts, adjacency, weight_one, weight_two
):
    initial = jnp.take(features, node_order[0], axis=0)
    tiles = adjacency[0, 0]
    rows, cols = block_rows[0], block_cols[0]
    block, width = tiles.shape[-1], features.shape[1]
    row_panel = lax.all_gather(initial, "col", axis=0, tiled=True)
    partial_one = block_product(
        row_panel.reshape(-1, block, width), tiles, rows, cols, block_counts, True
    )
    summed = lax.psum_scatter(
        partial_one.reshape(-1, width), "row", scatter_dimension=0, tiled=True
    )
    hidden = jax.nn.relu(jnp.dot(summed, weight_one, preferred_element_type=jnp.float32)).astype(
        jnp.bfloat16
    )
    col_panel = lax.all_gather(hidden, "row", axis=0, tiled=True)
    partial_two = block_product(
        col_panel.reshape(-1, block, width), tiles, cols, rows, block_counts, False
    )
    second = lax.psum_scatter(
        partial_two.reshape(-1, width), "col", scatter_dimension=0, tiled=True
    )
    return jax.nn.relu(jnp.dot(second, weight_two, preferred_element_type=jnp.float32)).astype(
        jnp.bfloat16
    )


def solution(mesh):
    in_specs = (
        P(("row", "col"), None),
        P(("row", "col"), None),
        P("row", "col", None),
        P("row", "col", None),
        P("row", "col"),
        P("row", "col", None, None, None),
        P(),
        P(),
    )
    out_specs = P(("row", "col"), None)
    return jax.shard_map(
        on_device, mesh=mesh, in_specs=in_specs, out_specs=out_specs, check_vma=False
    )
```

```python
import functools
import jax
import jax.numpy as jnp
from jax import lax
from jax.experimental import pallas as pl
from jax.experimental.pallas import tpu as pltpu
from jax.sharding import PartitionSpec as P

MESH = pl.DeviceIdType.MESH
PARTS = 3


class Mail:
    def __init__(self, send_sem, recv_sem):
        self.send_sem, self.recv_sem, self.sent = send_sem, recv_sem, {}

    def send(self, name, src, dst, device):
        slot = len(self.sent)
        copy = pltpu.make_async_remote_copy(
            src_ref=src, dst_ref=dst, send_sem=self.send_sem.at[slot],
            recv_sem=self.recv_sem.at[slot], device_id=device, device_id_type=MESH,
        )
        copy.start()
        self.sent[name] = copy

    def await_recv(self, *names):
        for name in names:
            self.sent[name].wait_recv()

    def finish(self):
        for copy in self.sent.values():
            copy.wait_send()


def greet(devices):
    barrier = pltpu.get_barrier_semaphore()
    for device in devices:
        pl.semaphore_signal(barrier, inc=1, device_id=device, device_id_type=MESH)
    pl.semaphore_wait(barrier, len(devices))


def add_rows(out, terms):
    rows = out.shape[0]
    step = next(s for s in (64, 48, 32, 16) if rows % s == 0)

    @pl.loop(0, rows // step)
    def _(i):
        at = pl.ds(pl.multiple_of(i * step, step), step)
        total = terms[0][at].astype(jnp.float32)
        for term in terms[1:]:
            total += term[at].astype(jnp.float32)
        out[at] = total.astype(out.dtype)


def dense_relu(out, terms, weight):
    total = terms[0][...].astype(jnp.float32)
    for term in terms[1:]:
        total += term[...].astype(jnp.float32)
    product = jnp.dot(total.astype(jnp.bfloat16), weight[...], preferred_element_type=jnp.float32)
    out[...] = jnp.maximum(product, 0.0).astype(out.dtype)


def row_kernel(
    part, weight, out, own_r, own_l, own_m, x1_l, x1_r, x2_l, x2_r, x3_l, x3_r, xc_r, xc_l, sx,
    z1_l, z1_r, z2_l, z2_r, z3_l, z3_r, zc_r, zc_l, hid, send_sem, recv_sem, local_sem, hid_sem,
):
    slab = part.shape[2]
    n = slab // PARTS
    h = n // 2
    me = lax.axis_index("row")
    z, x = me // 4, me % 4
    xr, xl, xo = (x + 1) % 4, (x + 3) % 4, (x + 2) % 4
    zr, zl, zo = (z + 1) % 4, (z + 3) % 4, (z + 2) % 4
    to_xr, to_xl = {"row": z * 4 + xr}, {"row": z * 4 + xl}
    to_zr, to_zl = {"row": zr * 4 + x}, {"row": zl * 4 + x}
    loads = [
        pltpu.make_async_copy(part.at[:, at], own, local_sem.at[i])
        for i, (at, own) in enumerate(((xr, own_r), (xl, own_l), (x, own_m)))
    ]
    for load in loads:
        load.start()
    greet((to_xr, to_xl, to_zr, to_zl))
    mail = Mail(send_sem, recv_sem)

    def half(p, k):
        return pl.ds(p * n + k * h, h)

    def x12(p):
        a, b = half(p, 0), half(p, 1)
        mail.send(("x1r", p), part.at[:, xo, a], x1_l.at[p], to_xr)
        mail.send(("x1l", p), part.at[:, xo, b], x1_r.at[p], to_xl)
        mail.send(("x2r", p), part.at[:, xr, b], x2_l.at[p], to_xr)
        mail.send(("x2l", p), part.at[:, xl, a], x2_r.at[p], to_xl)

    def x3(p):
        a, b = half(p, 0), half(p, 1)
        if p == 0:
            loads[0].wait()
            loads[1].wait()
        mail.await_recv(("x1r", p))
        for k in range(4):
            add_rows(xc_r.at[p, k], (x1_l.at[p, k], own_r.at[k, a]))
        mail.send(("x3r", p), xc_r.at[p], x3_l.at[p], to_xr)
        mail.await_recv(("x1l", p))
        for k in range(4):
            add_rows(xc_l.at[p, k], (x1_r.at[p, k], own_l.at[k, b]))
        mail.send(("x3l", p), xc_l.at[p], x3_r.at[p], to_xl)

    def x4(p):
        a, b = half(p, 0), half(p, 1)
        if p == 0:
            loads[2].wait()
        mail.await_recv(("x2l", p), ("x3r", p))
        for k in range(4):
            add_rows(sx.at[p, 0, k], (own_m.at[k, a], x3_l.at[p, k], x2_r.at[p, k]))
        mail.send(("z1r", p), sx.at[p, 0, zo], z1_l.at[p], to_zr)
        mail.send(("z2l", p), sx.at[p, 0, zl], z2_r.at[p], to_zl)
        mail.await_recv(("x2r", p), ("x3l", p))
        for k in range(4):
            add_rows(sx.at[p, 1, k], (own_m.at[k, b], x3_r.at[p, k], x2_l.at[p, k]))
        mail.send(("z1l", p), sx.at[p, 1, zo], z1_r.at[p], to_zl)
        mail.send(("z2r", p), sx.at[p, 1, zr], z2_l.at[p], to_zr)

    def z3(p):
        mail.await_recv(("z1r", p))
        add_rows(zc_r.at[p], (z1_l.at[p], sx.at[p, 0, zr]))
        mail.send(("z3r", p), zc_r.at[p], z3_l.at[p], to_zr)
        mail.await_recv(("z1l", p))
        add_rows(zc_l.at[p], (z1_r.at[p], sx.at[p, 1, zl]))
        mail.send(("z3l", p), zc_l.at[p], z3_r.at[p], to_zl)

    def z4(p):
        a, b = half(p, 0), half(p, 1)
        mail.await_recv(("z2l", p), ("z3r", p))
        dense_relu(hid.at[a], (sx.at[p, 0, z], z3_l.at[p], z2_r.at[p]), weight)
        mail.await_recv(("z2r", p), ("z3l", p))
        dense_relu(hid.at[b], (sx.at[p, 1, z], z3_r.at[p], z2_l.at[p]), weight)
        mail.send(("g1ar", p), hid.at[a], out.at[z, x, a], to_zr)
        mail.send(("g1bl", p), hid.at[b], out.at[z, x, b], to_zl)
        mail.send(("g1br", p), hid.at[b], out.at[z, x, b], to_zr)
        mail.send(("g1al", p), hid.at[a], out.at[z, x, a], to_zl)
        whole = pl.ds(p * n, n)
        pltpu.make_async_copy(hid.at[whole], out.at[z, x, whole], hid_sem.at[p]).start()

    def g2(p):
        a, b = half(p, 0), half(p, 1)
        mail.await_recv(("g1ar", p))
        mail.send(("g2r", p), out.at[zl, x, a], out.at[zl, x, a], to_zr)
        mail.await_recv(("g1bl", p))
        mail.send(("g2l", p), out.at[zr, x, b], out.at[zr, x, b], to_zl)

    def g3(p):
        a, b = half(p, 0), half(p, 1)
        mail.await_recv(("g1br", p), ("g1al", p), ("g2r", p), ("g2l", p))
        whole = pl.ds(p * n, n)
        pltpu.make_async_copy(hid.at[whole], out.at[z, x, whole], hid_sem.at[p]).wait()
        for name, rows, to in (("g3ar", a, to_xr), ("g3bl", b, to_xl), ("g3br", b, to_xr), ("g3al", a, to_xl)):
            mail.send((name, p), out.at[:, x, rows], out.at[:, x, rows], to)

    def g4(p):
        a, b = half(p, 0), half(p, 1)
        mail.await_recv(("g3ar", p))
        mail.send(("g4r", p), out.at[:, xl, a], out.at[:, xl, a], to_xr)
        mail.await_recv(("g3bl", p))
        mail.send(("g4l", p), out.at[:, xr, b], out.at[:, xr, b], to_xl)

    def g5(p):
        mail.await_recv(("g3br", p), ("g3al", p), ("g4r", p), ("g4l", p))

    stages = ((x12, 0), (x3, 1), (x4, 2), (z3, 3), (z4, 4), (g2, 5), (g3, 6), (g4, 7), (g5, 8))
    for tick in range(PARTS + len(stages) - 1):
        for stage, lag in stages:
            if 0 <= tick - lag < PARTS:
                stage(tick - lag)
    mail.finish()


def row_exchange(part, weight):
    _, slab, width = part.shape
    h = slab // PARTS // 2
    dt = part.dtype
    hbm = pl.BlockSpec(memory_space=pl.ANY)
    count = 24 * PARTS
    out = pl.pallas_call(
        row_kernel,
        out_shape=jax.ShapeDtypeStruct((4, 4, slab, width), dt),
        in_specs=[hbm, pl.BlockSpec(memory_space=pltpu.VMEM)],
        out_specs=hbm,
        scratch_shapes=(
            [pltpu.VMEM((4, slab, width), dt)] * 3
            + [pltpu.VMEM((PARTS, 4, h, width), dt)] * 8
            + [pltpu.VMEM((PARTS, 2, 4, h, width), dt)]
            + [pltpu.VMEM((PARTS, h, width), dt)] * 8
            + [pltpu.VMEM((slab, width), dt)]
            + [pltpu.SemaphoreType.DMA((count,))] * 2
            + [pltpu.SemaphoreType.DMA((3,)), pltpu.SemaphoreType.DMA((PARTS,))]
        ),
        compiler_params=pltpu.CompilerParams(
            collective_id=1, has_side_effects=True, vmem_limit_bytes=60 << 20
        ),
    )(part.reshape(4, 4, slab, width), weight)
    return out.reshape(16, slab, width)


def gather_kernel(order, features, out, own, send_sem, recv_sem, own_sem):
    slab = features.shape[0]
    h = slab // 2
    me = lax.axis_index("col")
    zp, y, c = me // 8, (me // 2) % 4, me % 2
    yr, yl, yo, zq = (y + 1) % 4, (y + 3) % 4, (y + 2) % 4, 1 - zp
    to_r, to_l = {"col": zp * 8 + yr * 2 + c}, {"col": zp * 8 + yl * 2 + c}
    to_z, to_c = {"col": zq * 8 + y * 2 + c}, {"col": zp * 8 + y * 2 + 1 - c}
    step = 128 if h % 128 == 0 else h

    def place(half):
        @pl.loop(0, h // step)
        def _(i):
            at = pl.ds(pl.multiple_of(half * h + i * step, step), step)
            place_of = order[:, at]
            chosen = lax.broadcasted_iota(jnp.int32, (slab, step), 0) == place_of
            own[at] = lax.dot_general(
                chosen.astype(features.dtype), features[...], (((0,), (0,)), ((), ())),
                preferred_element_type=jnp.float32,
            ).astype(own.dtype)

    place(0)
    greet((to_r, to_l, to_z, to_c))
    mail = Mail(send_sem, recv_sem)
    a, b, whole = pl.ds(0, h), pl.ds(h, h), pl.ds(0, slab)

    def send_own(name, rows, to):
        mail.send(name, own.at[rows], out.at[zp, y, c, rows], to)

    def send_on(name, zs, ys, rows, to):
        mail.send(name, out.at[zs, ys, c, rows], out.at[zs, ys, c, rows], to)

    send_own("ar", a, to_r)
    send_own("za", a, to_z)
    place(1)
    send_own("bl", b, to_l)
    send_own("zb", b, to_z)
    send_own("br", b, to_r)
    send_own("al", a, to_l)
    send_own("c0", whole, to_c)
    own_copy = pltpu.make_async_copy(own, out.at[zp, y, c], own_sem)
    own_copy.start()
    mail.await_recv("ar")
    send_on("fr", zp, yl, a, to_r)
    mail.await_recv("bl")
    send_on("fl", zp, yr, b, to_l)
    mail.await_recv("za")
    send_on("par", zq, y, a, to_r)
    send_on("pal", zq, y, a, to_l)
    mail.await_recv("zb")
    send_on("pbr", zq, y, b, to_r)
    send_on("pbl", zq, y, b, to_l)
    send_on("c1", zq, y, whole, to_c)
    mail.await_recv("br")
    send_on("c2", zp, yl, whole, to_c)
    mail.await_recv("al")
    send_on("c3", zp, yr, whole, to_c)
    mail.await_recv("fr")
    send_on("zoa", zp, yo, a, to_z)
    mail.await_recv("fl")
    send_on("zob", zp, yo, b, to_z)
    send_on("c4", zp, yo, whole, to_c)
    mail.await_recv("par", "pbr")
    send_on("c5", zq, yl, whole, to_c)
    mail.await_recv("pal", "pbl")
    send_on("c6", zq, yr, whole, to_c)
    mail.await_recv("zoa")
    send_on("c7a", zq, yo, a, to_c)
    mail.await_recv("zob")
    send_on("c7b", zq, yo, b, to_c)
    own_copy.wait()
    mail.await_recv("c0", "c1", "c2", "c3", "c4", "c5", "c6", "c7a", "c7b")
    mail.finish()


def col_gather(order, features):
    slab, width = features.shape
    vmem = pl.BlockSpec(memory_space=pltpu.VMEM)
    out = pl.pallas_call(
        gather_kernel,
        out_shape=jax.ShapeDtypeStruct((2, 4, 2, slab, width), features.dtype),
        in_specs=[vmem, vmem],
        out_specs=pl.BlockSpec(memory_space=pl.ANY),
        scratch_shapes=[
            pltpu.VMEM((slab, width), features.dtype),
            pltpu.SemaphoreType.DMA((23,)),
            pltpu.SemaphoreType.DMA((23,)),
            pltpu.SemaphoreType.DMA,
        ],
        compiler_params=pltpu.CompilerParams(
            collective_id=0, has_side_effects=True, vmem_limit_bytes=60 << 20
        ),
    )(order, features)
    return out.reshape(16, slab, width)


def sum_kernel(
    part, weight, out, own, sib, both, z1, s2_l, s2_r, s3_l, s3_r, opp, s4b_l, s4b_r, s4a_l, s4a_r,
    c_r, c_l, via, z2, send_sem, recv_sem, own_sem,
):
    slab = part.shape[3]
    h = slab // 2
    me = lax.axis_index("col")
    zp, y, c = me // 8, (me // 2) % 4, me % 2
    yr, yl, yo, zq, d = (y + 1) % 4, (y + 3) % 4, (y + 2) % 4, 1 - zp, 1 - c
    to_r, to_l = {"col": zp * 8 + yr * 2 + c}, {"col": zp * 8 + yl * 2 + c}
    to_z, to_c = {"col": zq * 8 + y * 2 + c}, {"col": zp * 8 + y * 2 + d}
    a, b = pl.ds(0, h), pl.ds(h, h)
    dests = ((zq, yo), (zq, yr), (zq, yl), (zp, yr), (zp, yl), (zp, yo), (zq, y), (zp, y))
    loads = [
        pltpu.make_async_copy(part.at[zs, ys, c], own.at[i], own_sem.at[i])
        for i, (zs, ys) in enumerate(dests)
    ]
    for load in loads:
        load.start()
    greet((to_r, to_l, to_z, to_c))
    mail = Mail(send_sem, recv_sem)
    for i, (zs, ys) in enumerate(dests):
        mail.send(("c", i), part.at[zs, ys, d], sib.at[i], to_c)

    def join(i):
        loads[i].wait()
        mail.await_recv(("c", i))
        add_rows(both.at[i], (own.at[i], sib.at[i]))

    join(0)
    mail.send("z1", both.at[0], z1, to_z)
    join(1)
    mail.send("s2r", both.at[1], s2_l, to_r)
    join(2)
    mail.send("s2l", both.at[2], s2_r, to_l)
    join(3)
    mail.send("s4br", both.at[3, b], s4b_l, to_r)
    join(4)
    mail.send("s4bl", both.at[4, a], s4b_r, to_l)
    join(5)
    mail.await_recv("z1")
    add_rows(opp, (both.at[5], z1))
    mail.send("s3r", opp.at[a], s3_l, to_r)
    mail.send("s3l", opp.at[b], s3_r, to_l)
    join(6)
    join(7)
    mail.await_recv("s2r", "s2l")
    add_rows(via, (both.at[6], s2_l, s2_r))
    mail.send("z2", via, z2, to_z)
    mail.await_recv("s3r")
    add_rows(c_r, (both.at[3, a], s3_l))
    mail.send("s4ar", c_r, s4a_l, to_r)
    mail.await_recv("s3l")
    add_rows(c_l, (both.at[4, b], s3_r))
    mail.send("s4al", c_l, s4a_r, to_l)
    mail.await_recv("z2", "s4bl", "s4ar")
    dense_relu(out.at[a], (both.at[7, a], s4a_l, s4b_r, z2.at[a]), weight)
    mail.await_recv("s4br", "s4al")
    dense_relu(out.at[b], (both.at[7, b], s4b_l, s4a_r, z2.at[b]), weight)
    mail.finish()


def col_sum(part, weight):
    _, slab, width = part.shape
    dt, h = part.dtype, slab // 2
    vmem = pl.BlockSpec(memory_space=pltpu.VMEM)
    full, half = pltpu.VMEM((slab, width), dt), pltpu.VMEM((h, width), dt)
    return pl.pallas_call(
        sum_kernel,
        out_shape=jax.ShapeDtypeStruct((slab, width), dt),
        in_specs=[pl.BlockSpec(memory_space=pl.ANY), vmem],
        out_specs=vmem,
        scratch_shapes=(
            [pltpu.VMEM((8, slab, width), dt)] * 3
            + [full] * 3 + [half] * 2 + [full] + [half] * 6 + [full] * 2
            + [pltpu.SemaphoreType.DMA((18,))] * 2
            + [pltpu.SemaphoreType.DMA((8,))]
        ),
        compiler_params=pltpu.CompilerParams(
            collective_id=2, has_side_effects=True, vmem_limit_bytes=60 << 20
        ),
    )(part.reshape(2, 4, 2, slab, width), weight)


CHUNK = 16


def product_kernel(
    transposed, unroll, source_ref, target_ref, count_ref, panel_hbm, tile_hbm, out_hbm,
    tiles, panel, total, tile_sem, panel_sem, out_sem,
):
    slots, block = tile_hbm.shape[0], tile_hbm.shape[1]
    blocks = panel_hbm.shape[0]
    chunks = slots // CHUNK
    live = count_ref[0, 0]

    def tile_copy(c):
        part = pl.ds(c * CHUNK, CHUNK)
        return pltpu.make_async_copy(tile_hbm.at[part], tiles.at[part], tile_sem.at[c])

    panel_copy = pltpu.make_async_copy(panel_hbm, panel, panel_sem)
    panel_copy.start()
    for c in range(chunks):
        pl.when(c * CHUNK < live)(lambda c=c: tile_copy(c).start())

    @pl.loop(0, blocks)
    def _(g):
        total[g] = jnp.zeros_like(total[g])

    panel_copy.wait()
    dims = (((0,), (0,)), ((), ())) if transposed else (((1,), (0,)), ((), ()))

    def one_chunk(c):
        tile_copy(c).wait()

        @pl.loop(0, CHUNK // unroll)
        def _(step):
            first = c * CHUNK + step * unroll

            @pl.when(first < live)
            def _():
                products, targets = [], []
                for k in range(unroll):
                    slot = first + k
                    products.append(lax.dot_general(
                        tiles[slot], panel[source_ref[0, slot]], dims,
                        preferred_element_type=jnp.float32,
                    ))
                    targets.append(jnp.where(slot < live, target_ref[0, slot], blocks))
                for k in range(unroll):
                    total[targets[k]] += products[k]

    for c in range(chunks):
        pl.when(c * CHUNK < live)(functools.partial(one_chunk, c))

    rounds = 12
    share = blocks // rounds
    copies = []
    for c in range(rounds):
        @pl.loop(c * share, (c + 1) * share)
        def _(g):
            panel[g] = total[g].astype(panel.dtype)
        part = pl.ds(c * share, share)
        copies.append(pltpu.make_async_copy(panel.at[part], out_hbm.at[part], out_sem.at[c]))
        copies[-1].start()
    for copy in copies:
        copy.wait()


def block_product(panel, tiles, source_ids, target_ids, count, transposed, unroll=8):
    slots, block, _ = tiles.shape
    blocks, _, width = panel.shape
    smem = pl.BlockSpec(memory_space=pltpu.SMEM)
    hbm = pl.BlockSpec(memory_space=pl.ANY)
    return pl.pallas_call(
        functools.partial(product_kernel, transposed, unroll),
        out_shape=jax.ShapeDtypeStruct(panel.shape, panel.dtype),
        in_specs=[smem, smem, smem, hbm, hbm],
        out_specs=hbm,
        scratch_shapes=[
            pltpu.VMEM(tiles.shape, tiles.dtype),
            pltpu.VMEM(panel.shape, panel.dtype),
            pltpu.VMEM((blocks + 1, block, width), jnp.float32),
            pltpu.SemaphoreType.DMA((slots // CHUNK,)),
            pltpu.SemaphoreType.DMA,
            pltpu.SemaphoreType.DMA((12,)),
        ],
        compiler_params=pltpu.CompilerParams(vmem_limit_bytes=60 << 20),
        cost_estimate=pl.CostEstimate(
            flops=2 * slots * block * block * width, transcendentals=0,
            bytes_accessed=2 * (tiles.size + 2 * panel.size),
        ),
    )(source_ids, target_ids, count, panel, tiles)


def on_device(
    features, node_order, block_rows, block_cols, block_counts, adjacency, weight_one, weight_two
):
    tiles = adjacency[0, 0]
    rows, cols = block_rows[0], block_cols[0]
    block, (slab, width) = tiles.shape[-1], features.shape
    row_panel = col_gather(node_order, features)
    partial_one = block_product(
        row_panel.reshape(-1, block, width), tiles, rows, cols, block_counts, True
    )
    col_panel = row_exchange(partial_one.reshape(-1, slab, width), weight_one)
    partial_two = block_product(
        col_panel.reshape(-1, block, width), tiles, cols, rows, block_counts, False
    )
    return col_sum(partial_two.reshape(-1, slab, width), weight_two)


def solution(mesh):
    in_specs = (
        P(("row", "col"), None),
        P(("row", "col"), None),
        P("row", "col", None),
        P("row", "col", None),
        P("row", "col"),
        P("row", "col", None, None, None),
        P(),
        P(),
    )
    out_specs = P(("row", "col"), None)
    return jax.shard_map(
        on_device, mesh=mesh, in_specs=in_specs, out_specs=out_specs, check_vma=False
    )
```

```python
import functools
import jax
import jax.numpy as jnp
from jax import lax
from jax.experimental import pallas as pl
from jax.experimental.pallas import tpu as pltpu
from jax.sharding import PartitionSpec as P

MESH = pl.DeviceIdType.MESH
PARTS = 4
LAGS = dict(r1=0, r2=1, r3=2, r4=3, r5=4, d=5, g2=5, g4=6, g3=6, g3o=6, g5=8, g4o=14, end=15)


class Mail:
    def __init__(self, send_sem, recv_sem):
        self.send_sem, self.recv_sem, self.sent = send_sem, recv_sem, {}

    def send(self, name, src, dst, device):
        slot = len(self.sent)
        copy = pltpu.make_async_remote_copy(
            src_ref=src, dst_ref=dst, send_sem=self.send_sem.at[slot],
            recv_sem=self.recv_sem.at[slot], device_id=device, device_id_type=MESH,
        )
        copy.start()
        self.sent[name] = copy

    def await_recv(self, *names):
        for name in names:
            self.sent[name].wait_recv()

    def finish(self):
        for copy in self.sent.values():
            copy.wait_send()


def greet(devices):
    barrier = pltpu.get_barrier_semaphore()
    for device in devices:
        pl.semaphore_signal(barrier, inc=1, device_id=device, device_id_type=MESH)
    pl.semaphore_wait(barrier, len(devices))


def add_rows(out, terms):
    rows = out.shape[0]
    step = next(s for s in (64, 48, 32, 16) if rows % s == 0)

    @pl.loop(0, rows // step)
    def _(i):
        at = pl.ds(pl.multiple_of(i * step, step), step)
        total = terms[0][at].astype(jnp.float32)
        for term in terms[1:]:
            total += term[at].astype(jnp.float32)
        out[at] = total.astype(out.dtype)


def dense_relu(out, terms, weight):
    total = terms[0][...].astype(jnp.float32)
    for term in terms[1:]:
        total += term[...].astype(jnp.float32)
    product = jnp.dot(total.astype(jnp.bfloat16), weight[...], preferred_element_type=jnp.float32)
    out[...] = jnp.maximum(product, 0.0).astype(out.dtype)


def row_kernel(
    part, weight, out, own, r1_l, r1_r, cz, r2_l, r2_r, r2o_l, r2o_r, cx_r, cx_l, r3m_l, r3m_r,
    r3b_l, r3a_r, r3a_l, r3b_r, sx, r4_l, r4_r, r5b_l, r5a_r, r5a_l, r5b_r, cs_r, cs_l, hid,
    send_sem, recv_sem, own_sem, hid_sem,
):
    slab = part.shape[3]
    n = slab // PARTS
    h = n // 2
    me = lax.axis_index("row")
    z, x = me // 4, me % 4
    xr, xl, xo = (x + 1) % 4, (x + 3) % 4, (x + 2) % 4
    zr, zl, zo = (z + 1) % 4, (z + 3) % 4, (z + 2) % 4
    to_xr, to_xl = {"row": z * 4 + xr}, {"row": z * 4 + xl}
    to_zr, to_zl = {"row": zr * 4 + x}, {"row": zl * 4 + x}
    same, other = z % 2, 1 - z % 2

    def at(ref, zs, xs, rows):
        return ref.at[zs // 2, zs % 2, xs, rows]

    loads = [
        pltpu.make_async_copy(part.at[:, :, xs], own.at[i], own_sem.at[i])
        for i, xs in enumerate((xo, xr, xl, x))
    ]
    for load in loads:
        load.start()
    own_o, own_r, own_l, own_m = (own.at[i] for i in range(4))
    greet((to_xr, to_xl, to_zr, to_zl))
    mail = Mail(send_sem, recv_sem)

    def rows(p):
        return pl.ds(p * n, n), pl.ds(p * n, h), pl.ds(p * n + h, h)

    def r1(p):
        n_, a, b = rows(p)
        mail.send(("r1r", p), at(part, zr, xo, n_), r1_l.at[p], to_zr)
        mail.send(("r1l", p), at(part, zl, xo, n_), r1_r.at[p], to_zl)
        mail.send(("r2or", p), at(part, zo, xo, a), r2o_l.at[p], to_xr)
        mail.send(("r2ol", p), at(part, zo, xo, b), r2o_r.at[p], to_xl)
        mail.send(("r3mr", p), part.at[:, other, xr, n_], r3m_l.at[p], to_xr)
        mail.send(("r3ml", p), part.at[:, other, xl, n_], r3m_r.at[p], to_xl)
        mail.send(("r3br", p), part.at[:, same, xr, b], r3b_l.at[p], to_xr)
        mail.send(("r3al", p), part.at[:, same, xl, a], r3a_r.at[p], to_xl)

    def r2(p):
        n_, a, b = rows(p)
        if p == 0:
            loads[0].wait()
        mail.await_recv(("r1r", p), ("r1l", p))
        add_rows(cz.at[p], (own_o.at[z // 2, same, n_], r1_l.at[p], r1_r.at[p]))
        mail.send(("r2r", p), cz.at[p, pl.ds(0, h)], r2_l.at[p], to_xr)
        mail.send(("r2l", p), cz.at[p, pl.ds(h, h)], r2_r.at[p], to_xl)

    def r3(p):
        n_, a, b = rows(p)
        if p == 0:
            loads[1].wait()
            loads[2].wait()
        mail.await_recv(("r2r", p), ("r2or", p))
        add_rows(cx_r.at[p, z // 2], (own_r.at[z // 2, same, a], r2_l.at[p]))
        add_rows(cx_r.at[p, zo // 2], (own_r.at[zo // 2, same, a], r2o_l.at[p]))
        mail.send(("r3ar", p), cx_r.at[p], r3a_l.at[p], to_xr)
        mail.await_recv(("r2l", p), ("r2ol", p))
        add_rows(cx_l.at[p, z // 2], (own_l.at[z // 2, same, b], r2_r.at[p]))
        add_rows(cx_l.at[p, zo // 2], (own_l.at[zo // 2, same, b], r2o_r.at[p]))
        mail.send(("r3bl", p), cx_l.at[p], r3b_r.at[p], to_xl)

    def r4(p):
        n_, a, b = rows(p)
        first, second = pl.ds(0, h), pl.ds(h, h)
        if p == 0:
            loads[3].wait()
        mail.await_recv(("r3ar", p), ("r3al", p))
        for k in range(2):
            add_rows(sx.at[p, k, same, first], (own_m.at[k, same, a], r3a_l.at[p, k], r3a_r.at[p, k]))
        mail.send(("r4r", p), sx.at[p, zo // 2, same, first], r4_l.at[p], to_zr)
        mail.await_recv(("r3br", p), ("r3bl", p))
        for k in range(2):
            add_rows(sx.at[p, k, same, second], (own_m.at[k, same, b], r3b_l.at[p, k], r3b_r.at[p, k]))
        mail.send(("r4l", p), sx.at[p, zo // 2, same, second], r4_r.at[p], to_zl)
        mail.await_recv(("r3mr", p), ("r3ml", p))
        for k in range(2):
            add_rows(sx.at[p, k, other], (own_m.at[k, other, n_], r3m_l.at[p, k], r3m_r.at[p, k]))
        mail.send(("r5br", p), sx.at[p, zr // 2, other, second], r5b_l.at[p], to_zr)
        mail.send(("r5al", p), sx.at[p, zl // 2, other, first], r5a_r.at[p], to_zl)

    def r5(p):
        mail.await_recv(("r4r", p))
        add_rows(cs_r.at[p], (sx.at[p, zr // 2, other, pl.ds(0, h)], r4_l.at[p]))
        mail.send(("r5ar", p), cs_r.at[p], r5a_l.at[p], to_zr)
        mail.await_recv(("r4l", p))
        add_rows(cs_l.at[p], (sx.at[p, zl // 2, other, pl.ds(h, h)], r4_r.at[p]))
        mail.send(("r5bl", p), cs_l.at[p], r5b_r.at[p], to_zl)

    def dense(p):
        n_, a, b = rows(p)
        mine = sx.at[p, z // 2, same]
        mail.await_recv(("r5ar", p), ("r5al", p))
        dense_relu(hid.at[a], (mine.at[pl.ds(0, h)], r5a_l.at[p], r5a_r.at[p]), weight)
        mail.send(("g1ar", p), hid.at[a], at(out, z, x, a), to_zr)
        mail.send(("g3ar", p), hid.at[a], at(out, z, x, a), to_xr)
        mail.await_recv(("r5br", p), ("r5bl", p))
        dense_relu(hid.at[b], (mine.at[pl.ds(h, h)], r5b_l.at[p], r5b_r.at[p]), weight)
        mail.send(("g1bl", p), hid.at[b], at(out, z, x, b), to_zl)
        mail.send(("g3bl", p), hid.at[b], at(out, z, x, b), to_xl)
        mail.send(("g1br", p), hid.at[b], at(out, z, x, b), to_zr)
        mail.send(("g1al", p), hid.at[a], at(out, z, x, a), to_zl)
        mail.send(("g3br", p), hid.at[b], at(out, z, x, b), to_xr)
        mail.send(("g3al", p), hid.at[a], at(out, z, x, a), to_xl)
        pltpu.make_async_copy(hid.at[n_], at(out, z, x, n_), hid_sem.at[p]).start()

    def pass_on(name, p, zs, xs, rows_, to):
        mail.send((name, p), at(out, zs, xs, rows_), at(out, zs, xs, rows_), to)

    def g2(p):
        n_, a, b = rows(p)
        mail.await_recv(("g1ar", p))
        pass_on("g2r", p, zl, x, a, to_zr)
        mail.await_recv(("g1bl", p))
        pass_on("g2l", p, zr, x, b, to_zl)

    def g4(p):
        n_, a, b = rows(p)
        mail.await_recv(("g3ar", p))
        pass_on("g4r", p, z, xl, a, to_xr)
        mail.await_recv(("g3bl", p))
        pass_on("g4l", p, z, xr, b, to_xl)

    def g5(p):
        n_, a, b = rows(p)
        mail.await_recv(("g4r", p), ("g4l", p))
        pass_on("g5r", p, z, xo, n_, to_zr)
        pass_on("g5l", p, z, xo, n_, to_zl)

    def g3(p):
        n_, a, b = rows(p)
        mail.await_recv(("g1br", p), ("g1al", p))
        both = out.at[:, other, x, n_]
        mail.send(("g3mr", p), both, both, to_xr)
        mail.send(("g3ml", p), both, both, to_xl)

    def g3o(p):
        n_, a, b = rows(p)
        mail.await_recv(("g2r", p))
        pass_on("g3oar", p, zo, x, a, to_xr)
        mail.await_recv(("g2l", p))
        pass_on("g3obl", p, zo, x, b, to_xl)
        pass_on("g3obr", p, zo, x, b, to_xr)
        pass_on("g3oal", p, zo, x, a, to_xl)

    def g4o(p):
        n_, a, b = rows(p)
        mail.await_recv(("g3oar", p))
        pass_on("g4or", p, zo, xl, a, to_xr)
        mail.await_recv(("g3obl", p))
        pass_on("g4ol", p, zo, xr, b, to_xl)

    def end(p):
        n_, a, b = rows(p)
        pltpu.make_async_copy(hid.at[n_], at(out, z, x, n_), hid_sem.at[p]).wait()
        mail.await_recv(*((name, p) for name in (
            "g3br", "g3al", "g3mr", "g3ml", "g3obr", "g3oal", "g4or", "g4ol", "g5r", "g5l"
        )))

    stages = dict(
        r1=r1, r2=r2, r3=r3, r4=r4, r5=r5, d=dense, g2=g2, g4=g4, g5=g5, g3=g3, g3o=g3o, g4o=g4o,
        end=end,
    )
    order = sorted(stages, key=lambda name: -LAGS[name])
    for tick in range(PARTS + max(LAGS.values())):
        for name in order:
            if 0 <= tick - LAGS[name] < PARTS:
                stages[name](tick - LAGS[name])
    mail.finish()


def row_exchange(part, weight):
    _, slab, width = part.shape
    n = slab // PARTS
    h = n // 2
    dt = part.dtype
    hbm = pl.BlockSpec(memory_space=pl.ANY)
    count = 40 * PARTS

    def buf(*lead):
        return [pltpu.VMEM((PARTS, *lead, width), dt)]

    out = pl.pallas_call(
        row_kernel,
        out_shape=jax.ShapeDtypeStruct((2, 2, 4, slab, width), dt),
        in_specs=[hbm, pl.BlockSpec(memory_space=pltpu.VMEM)],
        out_specs=hbm,
        scratch_shapes=(
            [pltpu.VMEM((4, 2, 2, slab, width), dt)]
            + buf(n) * 3 + buf(h) * 4 + buf(2, h) * 2 + buf(2, n) * 2 + buf(2, h) * 4
            + buf(2, 2, n) + buf(h) * 8
            + [pltpu.VMEM((slab, width), dt)]
            + [pltpu.SemaphoreType.DMA((count,))] * 2
            + [pltpu.SemaphoreType.DMA((4,)), pltpu.SemaphoreType.DMA((PARTS,))]
        ),
        compiler_params=pltpu.CompilerParams(
            collective_id=1, has_side_effects=True, vmem_limit_bytes=60 << 20
        ),
    )(part.reshape(2, 2, 4, slab, width), weight)
    return out.reshape(16, slab, width)


def gather_kernel(order, features, out, own, send_sem, recv_sem, own_sem):
    slab = features.shape[0]
    h = slab // 2
    me = lax.axis_index("col")
    zp, y, c = me // 8, (me // 2) % 4, me % 2
    yr, yl, yo, zq = (y + 1) % 4, (y + 3) % 4, (y + 2) % 4, 1 - zp
    to_r, to_l = {"col": zp * 8 + yr * 2 + c}, {"col": zp * 8 + yl * 2 + c}
    to_z, to_c = {"col": zq * 8 + y * 2 + c}, {"col": zp * 8 + y * 2 + 1 - c}
    step = 128 if h % 128 == 0 else h

    def place(half):
        @pl.loop(0, h // step)
        def _(i):
            at = pl.ds(pl.multiple_of(half * h + i * step, step), step)
            place_of = order[:, at]
            chosen = lax.broadcasted_iota(jnp.int32, (slab, step), 0) == place_of
            own[at] = lax.dot_general(
                chosen.astype(features.dtype), features[...], (((0,), (0,)), ((), ())),
                preferred_element_type=jnp.float32,
            ).astype(own.dtype)

    place(0)
    greet((to_r, to_l, to_z, to_c))
    mail = Mail(send_sem, recv_sem)
    a, b, whole = pl.ds(0, h), pl.ds(h, h), pl.ds(0, slab)

    def send_own(name, rows, to):
        mail.send(name, own.at[rows], out.at[zp, y, c, rows], to)

    def send_on(name, zs, ys, rows, to):
        mail.send(name, out.at[zs, ys, c, rows], out.at[zs, ys, c, rows], to)

    send_own("ar", a, to_r)
    send_own("za", a, to_z)
    place(1)
    send_own("bl", b, to_l)
    send_own("zb", b, to_z)
    send_own("br", b, to_r)
    send_own("al", a, to_l)
    send_own("c0", whole, to_c)
    own_copy = pltpu.make_async_copy(own, out.at[zp, y, c], own_sem)
    own_copy.start()
    mail.await_recv("ar")
    send_on("fr", zp, yl, a, to_r)
    mail.await_recv("bl")
    send_on("fl", zp, yr, b, to_l)
    mail.await_recv("za")
    send_on("par", zq, y, a, to_r)
    send_on("pal", zq, y, a, to_l)
    mail.await_recv("zb")
    send_on("pbr", zq, y, b, to_r)
    send_on("pbl", zq, y, b, to_l)
    send_on("c1", zq, y, whole, to_c)
    mail.await_recv("br")
    send_on("c2", zp, yl, whole, to_c)
    mail.await_recv("al")
    send_on("c3", zp, yr, whole, to_c)
    mail.await_recv("fr")
    send_on("zoa", zp, yo, a, to_z)
    mail.await_recv("fl")
    send_on("zob", zp, yo, b, to_z)
    send_on("c4", zp, yo, whole, to_c)
    mail.await_recv("par", "pbr")
    send_on("c5", zq, yl, whole, to_c)
    mail.await_recv("pal", "pbl")
    send_on("c6", zq, yr, whole, to_c)
    mail.await_recv("zoa")
    send_on("c7a", zq, yo, a, to_c)
    mail.await_recv("zob")
    send_on("c7b", zq, yo, b, to_c)
    own_copy.wait()
    mail.await_recv("c0", "c1", "c2", "c3", "c4", "c5", "c6", "c7a", "c7b")
    mail.finish()


def col_gather(order, features):
    slab, width = features.shape
    vmem = pl.BlockSpec(memory_space=pltpu.VMEM)
    out = pl.pallas_call(
        gather_kernel,
        out_shape=jax.ShapeDtypeStruct((2, 4, 2, slab, width), features.dtype),
        in_specs=[vmem, vmem],
        out_specs=pl.BlockSpec(memory_space=pl.ANY),
        scratch_shapes=[
            pltpu.VMEM((slab, width), features.dtype),
            pltpu.SemaphoreType.DMA((23,)),
            pltpu.SemaphoreType.DMA((23,)),
            pltpu.SemaphoreType.DMA,
        ],
        compiler_params=pltpu.CompilerParams(
            collective_id=0, has_side_effects=True, vmem_limit_bytes=60 << 20
        ),
    )(order, features)
    return out.reshape(16, slab, width)


def sum_kernel(
    part, weight, out, own, sib, both, z1, s2_l, s2_r, s3_l, s3_r, opp, s4b_l, s4b_r, s4a_l, s4a_r,
    c_r, c_l, via, z2, send_sem, recv_sem, own_sem,
):
    slab = part.shape[3]
    h = slab // 2
    me = lax.axis_index("col")
    zp, y, c = me // 8, (me // 2) % 4, me % 2
    yr, yl, yo, zq, d = (y + 1) % 4, (y + 3) % 4, (y + 2) % 4, 1 - zp, 1 - c
    to_r, to_l = {"col": zp * 8 + yr * 2 + c}, {"col": zp * 8 + yl * 2 + c}
    to_z, to_c = {"col": zq * 8 + y * 2 + c}, {"col": zp * 8 + y * 2 + d}
    a, b = pl.ds(0, h), pl.ds(h, h)
    dests = ((zq, yo), (zq, yr), (zq, yl), (zp, yr), (zp, yl), (zp, yo), (zq, y), (zp, y))
    loads = [
        pltpu.make_async_copy(part.at[zs, ys, c], own.at[i], own_sem.at[i])
        for i, (zs, ys) in enumerate(dests)
    ]
    for load in loads:
        load.start()
    greet((to_r, to_l, to_z, to_c))
    mail = Mail(send_sem, recv_sem)
    for i, (zs, ys) in enumerate(dests):
        mail.send(("c", i), part.at[zs, ys, d], sib.at[i], to_c)

    def join(i):
        loads[i].wait()
        mail.await_recv(("c", i))
        add_rows(both.at[i], (own.at[i], sib.at[i]))

    join(0)
    mail.send("z1", both.at[0], z1, to_z)
    join(1)
    mail.send("s2r", both.at[1], s2_l, to_r)
    join(2)
    mail.send("s2l", both.at[2], s2_r, to_l)
    join(3)
    mail.send("s4br", both.at[3, b], s4b_l, to_r)
    join(4)
    mail.send("s4bl", both.at[4, a], s4b_r, to_l)
    join(5)
    mail.await_recv("z1")
    add_rows(opp, (both.at[5], z1))
    mail.send("s3r", opp.at[a], s3_l, to_r)
    mail.send("s3l", opp.at[b], s3_r, to_l)
    join(6)
    join(7)
    mail.await_recv("s2r", "s2l")
    add_rows(via, (both.at[6], s2_l, s2_r))
    mail.send("z2", via, z2, to_z)
    mail.await_recv("s3r")
    add_rows(c_r, (both.at[3, a], s3_l))
    mail.send("s4ar", c_r, s4a_l, to_r)
    mail.await_recv("s3l")
    add_rows(c_l, (both.at[4, b], s3_r))
    mail.send("s4al", c_l, s4a_r, to_l)
    mail.await_recv("z2", "s4bl", "s4ar")
    dense_relu(out.at[a], (both.at[7, a], s4a_l, s4b_r, z2.at[a]), weight)
    mail.await_recv("s4br", "s4al")
    dense_relu(out.at[b], (both.at[7, b], s4b_l, s4a_r, z2.at[b]), weight)
    mail.finish()


def col_sum(part, weight):
    _, slab, width = part.shape
    dt, h = part.dtype, slab // 2
    vmem = pl.BlockSpec(memory_space=pltpu.VMEM)
    full, half = pltpu.VMEM((slab, width), dt), pltpu.VMEM((h, width), dt)
    return pl.pallas_call(
        sum_kernel,
        out_shape=jax.ShapeDtypeStruct((slab, width), dt),
        in_specs=[pl.BlockSpec(memory_space=pl.ANY), vmem],
        out_specs=vmem,
        scratch_shapes=(
            [pltpu.VMEM((8, slab, width), dt)] * 3
            + [full] * 3 + [half] * 2 + [full] + [half] * 6 + [full] * 2
            + [pltpu.SemaphoreType.DMA((18,))] * 2
            + [pltpu.SemaphoreType.DMA((8,))]
        ),
        compiler_params=pltpu.CompilerParams(
            collective_id=2, has_side_effects=True, vmem_limit_bytes=60 << 20
        ),
    )(part.reshape(2, 4, 2, slab, width), weight)


CHUNK = 16


def product_kernel(
    transposed, unroll, source_ref, target_ref, count_ref, panel_hbm, tile_hbm, out_hbm,
    tiles, panel, total, tile_sem, panel_sem, out_sem,
):
    slots, block = tile_hbm.shape[0], tile_hbm.shape[1]
    blocks = panel_hbm.shape[0]
    chunks = slots // CHUNK
    live = count_ref[0, 0]

    def tile_copy(c):
        part = pl.ds(c * CHUNK, CHUNK)
        return pltpu.make_async_copy(tile_hbm.at[part], tiles.at[part], tile_sem.at[c])

    panel_copy = pltpu.make_async_copy(panel_hbm, panel, panel_sem)
    panel_copy.start()
    for c in range(chunks):
        pl.when(c * CHUNK < live)(lambda c=c: tile_copy(c).start())

    @pl.loop(0, blocks)
    def _(g):
        total[g] = jnp.zeros_like(total[g])

    panel_copy.wait()
    dims = (((0,), (0,)), ((), ())) if transposed else (((1,), (0,)), ((), ()))

    def one_chunk(c):
        tile_copy(c).wait()

        @pl.loop(0, CHUNK // unroll)
        def _(step):
            first = c * CHUNK + step * unroll

            @pl.when(first < live)
            def _():
                products, targets = [], []
                for k in range(unroll):
                    slot = first + k
                    products.append(lax.dot_general(
                        tiles[slot], panel[source_ref[0, slot]], dims,
                        preferred_element_type=jnp.float32,
                    ))
                    targets.append(jnp.where(slot < live, target_ref[0, slot], blocks))
                for k in range(unroll):
                    total[targets[k]] += products[k]

    for c in range(chunks):
        pl.when(c * CHUNK < live)(functools.partial(one_chunk, c))

    rounds = 12
    share = blocks // rounds
    copies = []
    for c in range(rounds):
        @pl.loop(c * share, (c + 1) * share)
        def _(g):
            panel[g] = total[g].astype(panel.dtype)
        part = pl.ds(c * share, share)
        copies.append(pltpu.make_async_copy(panel.at[part], out_hbm.at[part], out_sem.at[c]))
        copies[-1].start()
    for copy in copies:
        copy.wait()


def block_product(panel, tiles, source_ids, target_ids, count, transposed, unroll=8):
    slots, block, _ = tiles.shape
    blocks, _, width = panel.shape
    smem = pl.BlockSpec(memory_space=pltpu.SMEM)
    hbm = pl.BlockSpec(memory_space=pl.ANY)
    return pl.pallas_call(
        functools.partial(product_kernel, transposed, unroll),
        out_shape=jax.ShapeDtypeStruct(panel.shape, panel.dtype),
        in_specs=[smem, smem, smem, hbm, hbm],
        out_specs=hbm,
        scratch_shapes=[
            pltpu.VMEM(tiles.shape, tiles.dtype),
            pltpu.VMEM(panel.shape, panel.dtype),
            pltpu.VMEM((blocks + 1, block, width), jnp.float32),
            pltpu.SemaphoreType.DMA((slots // CHUNK,)),
            pltpu.SemaphoreType.DMA,
            pltpu.SemaphoreType.DMA((12,)),
        ],
        compiler_params=pltpu.CompilerParams(vmem_limit_bytes=60 << 20),
        cost_estimate=pl.CostEstimate(
            flops=2 * slots * block * block * width, transcendentals=0,
            bytes_accessed=2 * (tiles.size + 2 * panel.size),
        ),
    )(source_ids, target_ids, count, panel, tiles)


def on_device(
    features, node_order, block_rows, block_cols, block_counts, adjacency, weight_one, weight_two
):
    tiles = adjacency[0, 0]
    rows, cols = block_rows[0], block_cols[0]
    block, (slab, width) = tiles.shape[-1], features.shape
    row_panel = col_gather(node_order, features)
    partial_one = block_product(
        row_panel.reshape(-1, block, width), tiles, rows, cols, block_counts, True
    )
    col_panel = row_exchange(partial_one.reshape(-1, slab, width), weight_one)
    partial_two = block_product(
        col_panel.reshape(-1, block, width), tiles, cols, rows, block_counts, False
    )
    return col_sum(partial_two.reshape(-1, slab, width), weight_two)


def solution(mesh):
    in_specs = (
        P(("row", "col"), None),
        P(("row", "col"), None),
        P("row", "col", None),
        P("row", "col", None),
        P("row", "col"),
        P("row", "col", None, None, None),
        P(),
        P(),
    )
    out_specs = P(("row", "col"), None)
    return jax.shard_map(
        on_device, mesh=mesh, in_specs=in_specs, out_specs=out_specs, check_vma=False
    )
```

```python
import functools
import jax
import jax.numpy as jnp
from jax import lax
from jax.experimental import pallas as pl
from jax.experimental.pallas import tpu as pltpu
from jax.sharding import PartitionSpec as P

MESH = pl.DeviceIdType.MESH
PARTS = 4
LAGS = dict(r1=0, r2=1, r3=2, r4=3, r5=4, d=5, g2=5, g4=6, g3=6, g3o=6, g5=8, g4o=14, end=15)


class Mail:
    def __init__(self, send_sem, recv_sem):
        self.send_sem, self.recv_sem, self.sent = send_sem, recv_sem, {}

    def send(self, name, src, dst, device):
        slot = len(self.sent)
        copy = pltpu.make_async_remote_copy(
            src_ref=src, dst_ref=dst, send_sem=self.send_sem.at[slot],
            recv_sem=self.recv_sem.at[slot], device_id=device, device_id_type=MESH,
        )
        copy.start()
        self.sent[name] = copy

    def await_recv(self, *names):
        for name in names:
            self.sent[name].wait_recv()

    def finish(self):
        for copy in self.sent.values():
            copy.wait_send()


def greet(devices):
    barrier = pltpu.get_barrier_semaphore()
    for device in devices:
        pl.semaphore_signal(barrier, inc=1, device_id=device, device_id_type=MESH)
    pl.semaphore_wait(barrier, len(devices))


def add_rows(out, terms):
    rows = out.shape[0]
    step = next(s for s in (64, 48, 32, 16) if rows % s == 0)

    @pl.loop(0, rows // step)
    def _(i):
        at = pl.ds(pl.multiple_of(i * step, step), step)
        total = terms[0][at].astype(jnp.float32)
        for term in terms[1:]:
            total += term[at].astype(jnp.float32)
        out[at] = total.astype(out.dtype)


def dense_relu(out, terms, weight):
    total = terms[0][...].astype(jnp.float32)
    for term in terms[1:]:
        total += term[...].astype(jnp.float32)
    product = jnp.dot(total.astype(jnp.bfloat16), weight[...], preferred_element_type=jnp.float32)
    out[...] = jnp.maximum(product, 0.0).astype(out.dtype)


def row_kernel(
    part, weight, out, r1_l, r1_r, cz, r2_l, r2_r, r2o_l, r2o_r, cx_r, cx_l, r3m_l, r3m_r,
    r3b_l, r3a_r, r3a_l, r3b_r, sx, r4_l, r4_r, r5b_l, r5a_r, r5a_l, r5b_r, cs_r, cs_l, hid,
    send_sem, recv_sem, hid_sem,
):
    slab = part.shape[3]
    n = slab // PARTS
    h = n // 2
    me = lax.axis_index("row")
    z, x = me // 4, me % 4
    xr, xl, xo = (x + 1) % 4, (x + 3) % 4, (x + 2) % 4
    zr, zl, zo = (z + 1) % 4, (z + 3) % 4, (z + 2) % 4
    to_xr, to_xl = {"row": z * 4 + xr}, {"row": z * 4 + xl}
    to_zr, to_zl = {"row": zr * 4 + x}, {"row": zl * 4 + x}
    same, other = z % 2, 1 - z % 2

    def at(ref, zs, xs, rows):
        return ref.at[zs // 2, zs % 2, xs, rows]

    greet((to_xr, to_xl, to_zr, to_zl))
    mail = Mail(send_sem, recv_sem)

    def rows(p):
        return pl.ds(p * n, n), pl.ds(p * n, h), pl.ds(p * n + h, h)

    def r1(p):
        n_, a, b = rows(p)
        mail.send(("r1r", p), at(part, zr, xo, n_), r1_l.at[p], to_zr)
        mail.send(("r1l", p), at(part, zl, xo, n_), r1_r.at[p], to_zl)
        mail.send(("r2or", p), at(part, zo, xo, a), r2o_l.at[p], to_xr)
        mail.send(("r2ol", p), at(part, zo, xo, b), r2o_r.at[p], to_xl)
        mail.send(("r3mr", p), part.at[:, other, xr, n_], r3m_l.at[p], to_xr)
        mail.send(("r3ml", p), part.at[:, other, xl, n_], r3m_r.at[p], to_xl)
        mail.send(("r3br", p), part.at[:, same, xr, b], r3b_l.at[p], to_xr)
        mail.send(("r3al", p), part.at[:, same, xl, a], r3a_r.at[p], to_xl)

    def r2(p):
        n_, a, b = rows(p)
        mail.await_recv(("r1r", p), ("r1l", p))
        add_rows(cz.at[p], (part.at[z // 2, same, xo, n_], r1_l.at[p], r1_r.at[p]))
        mail.send(("r2r", p), cz.at[p, pl.ds(0, h)], r2_l.at[p], to_xr)
        mail.send(("r2l", p), cz.at[p, pl.ds(h, h)], r2_r.at[p], to_xl)

    def r3(p):
        n_, a, b = rows(p)
        mail.await_recv(("r2r", p), ("r2or", p))
        add_rows(cx_r.at[p, z // 2], (part.at[z // 2, same, xr, a], r2_l.at[p]))
        add_rows(cx_r.at[p, zo // 2], (part.at[zo // 2, same, xr, a], r2o_l.at[p]))
        mail.send(("r3ar", p), cx_r.at[p], r3a_l.at[p], to_xr)
        mail.await_recv(("r2l", p), ("r2ol", p))
        add_rows(cx_l.at[p, z // 2], (part.at[z // 2, same, xl, b], r2_r.at[p]))
        add_rows(cx_l.at[p, zo // 2], (part.at[zo // 2, same, xl, b], r2o_r.at[p]))
        mail.send(("r3bl", p), cx_l.at[p], r3b_r.at[p], to_xl)

    def r4(p):
        n_, a, b = rows(p)
        first, second = pl.ds(0, h), pl.ds(h, h)
        mail.await_recv(("r3ar", p), ("r3al", p))
        for k in range(2):
            add_rows(sx.at[p, k, same, first], (part.at[k, same, x, a], r3a_l.at[p, k], r3a_r.at[p, k]))
        mail.send(("r4r", p), sx.at[p, zo // 2, same, first], r4_l.at[p], to_zr)
        mail.await_recv(("r3br", p), ("r3bl", p))
        for k in range(2):
            add_rows(sx.at[p, k, same, second], (part.at[k, same, x, b], r3b_l.at[p, k], r3b_r.at[p, k]))
        mail.send(("r4l", p), sx.at[p, zo // 2, same, second], r4_r.at[p], to_zl)
        mail.await_recv(("r3mr", p), ("r3ml", p))
        for k in range(2):
            add_rows(sx.at[p, k, other], (part.at[k, other, x, n_], r3m_l.at[p, k], r3m_r.at[p, k]))
        mail.send(("r5br", p), sx.at[p, zr // 2, other, second], r5b_l.at[p], to_zr)
        mail.send(("r5al", p), sx.at[p, zl // 2, other, first], r5a_r.at[p], to_zl)

    def r5(p):
        mail.await_recv(("r4r", p))
        add_rows(cs_r.at[p], (sx.at[p, zr // 2, other, pl.ds(0, h)], r4_l.at[p]))
        mail.send(("r5ar", p), cs_r.at[p], r5a_l.at[p], to_zr)
        mail.await_recv(("r4l", p))
        add_rows(cs_l.at[p], (sx.at[p, zl // 2, other, pl.ds(h, h)], r4_r.at[p]))
        mail.send(("r5bl", p), cs_l.at[p], r5b_r.at[p], to_zl)

    def dense(p):
        n_, a, b = rows(p)
        mine = sx.at[p, z // 2, same]
        mail.await_recv(("r5ar", p), ("r5al", p))
        dense_relu(hid.at[a], (mine.at[pl.ds(0, h)], r5a_l.at[p], r5a_r.at[p]), weight)
        mail.send(("g1ar", p), hid.at[a], at(out, z, x, a), to_zr)
        mail.send(("g3ar", p), hid.at[a], at(out, z, x, a), to_xr)
        mail.await_recv(("r5br", p), ("r5bl", p))
        dense_relu(hid.at[b], (mine.at[pl.ds(h, h)], r5b_l.at[p], r5b_r.at[p]), weight)
        mail.send(("g1bl", p), hid.at[b], at(out, z, x, b), to_zl)
        mail.send(("g3bl", p), hid.at[b], at(out, z, x, b), to_xl)
        mail.send(("g1br", p), hid.at[b], at(out, z, x, b), to_zr)
        mail.send(("g1al", p), hid.at[a], at(out, z, x, a), to_zl)
        mail.send(("g3br", p), hid.at[b], at(out, z, x, b), to_xr)
        mail.send(("g3al", p), hid.at[a], at(out, z, x, a), to_xl)
        pltpu.make_async_copy(hid.at[n_], at(out, z, x, n_), hid_sem.at[p]).start()

    def pass_on(name, p, zs, xs, rows_, to):
        mail.send((name, p), at(out, zs, xs, rows_), at(out, zs, xs, rows_), to)

    def g2(p):
        n_, a, b = rows(p)
        mail.await_recv(("g1ar", p))
        pass_on("g2r", p, zl, x, a, to_zr)
        mail.await_recv(("g1bl", p))
        pass_on("g2l", p, zr, x, b, to_zl)

    def g4(p):
        n_, a, b = rows(p)
        mail.await_recv(("g3ar", p))
        pass_on("g4r", p, z, xl, a, to_xr)
        mail.await_recv(("g3bl", p))
        pass_on("g4l", p, z, xr, b, to_xl)

    def g5(p):
        n_, a, b = rows(p)
        mail.await_recv(("g4r", p), ("g4l", p))
        pass_on("g5r", p, z, xo, n_, to_zr)
        pass_on("g5l", p, z, xo, n_, to_zl)

    def g3(p):
        n_, a, b = rows(p)
        mail.await_recv(("g1br", p), ("g1al", p))
        both = out.at[:, other, x, n_]
        mail.send(("g3mr", p), both, both, to_xr)
        mail.send(("g3ml", p), both, both, to_xl)

    def g3o(p):
        n_, a, b = rows(p)
        mail.await_recv(("g2r", p))
        pass_on("g3oar", p, zo, x, a, to_xr)
        mail.await_recv(("g2l", p))
        pass_on("g3obl", p, zo, x, b, to_xl)
        pass_on("g3obr", p, zo, x, b, to_xr)
        pass_on("g3oal", p, zo, x, a, to_xl)

    def g4o(p):
        n_, a, b = rows(p)
        mail.await_recv(("g3oar", p))
        pass_on("g4or", p, zo, xl, a, to_xr)
        mail.await_recv(("g3obl", p))
        pass_on("g4ol", p, zo, xr, b, to_xl)

    def end(p):
        n_, a, b = rows(p)
        pltpu.make_async_copy(hid.at[n_], at(out, z, x, n_), hid_sem.at[p]).wait()
        mail.await_recv(*((name, p) for name in (
            "g3br", "g3al", "g3mr", "g3ml", "g3obr", "g3oal", "g4or", "g4ol", "g5r", "g5l"
        )))

    stages = dict(
        r1=r1, r2=r2, r3=r3, r4=r4, r5=r5, d=dense, g2=g2, g4=g4, g5=g5, g3=g3, g3o=g3o, g4o=g4o,
        end=end,
    )
    order = sorted(stages, key=lambda name: -LAGS[name])
    for tick in range(PARTS + max(LAGS.values())):
        for name in order:
            if 0 <= tick - LAGS[name] < PARTS:
                stages[name](tick - LAGS[name])
    mail.finish()


def row_exchange(part, weight):
    _, slab, width = part.shape
    n = slab // PARTS
    h = n // 2
    dt = part.dtype
    vmem = pl.BlockSpec(memory_space=pltpu.VMEM)
    count = 40 * PARTS

    def buf(*lead):
        return [pltpu.VMEM((PARTS, *lead, width), dt)]

    out = pl.pallas_call(
        row_kernel,
        out_shape=jax.ShapeDtypeStruct((2, 2, 4, slab, width), dt),
        in_specs=[vmem, vmem],
        out_specs=vmem,
        scratch_shapes=(
            buf(n) * 3 + buf(h) * 4 + buf(2, h) * 2 + buf(2, n) * 2 + buf(2, h) * 4
            + buf(2, 2, n) + buf(h) * 8
            + [pltpu.VMEM((slab, width), dt)]
            + [pltpu.SemaphoreType.DMA((count,))] * 2
            + [pltpu.SemaphoreType.DMA((PARTS,))]
        ),
        compiler_params=pltpu.CompilerParams(
            collective_id=1, has_side_effects=True, vmem_limit_bytes=28 << 20
        ),
    )(part.reshape(2, 2, 4, slab, width), weight)
    return out.reshape(16, slab, width)


def gather_kernel(order, features, out, own, send_sem, recv_sem, own_sem):
    slab = features.shape[0]
    h = slab // 4
    me = lax.axis_index("col")
    zp, y, c = me // 8, (me // 2) % 4, me % 2
    yr, yl, yo, zq = (y + 1) % 4, (y + 3) % 4, (y + 2) % 4, 1 - zp
    to_r, to_l = {"col": zp * 8 + yr * 2 + c}, {"col": zp * 8 + yl * 2 + c}
    to_z, to_c = {"col": zq * 8 + y * 2 + c}, {"col": zp * 8 + y * 2 + 1 - c}

    def place(q):
        at = pl.ds(q * h, h)
        chosen = lax.broadcasted_iota(jnp.int32, (slab, h), 0) == order[:, at]
        own[at] = lax.dot_general(
            chosen.astype(features.dtype), features[...], (((0,), (0,)), ((), ())),
            preferred_element_type=jnp.float32,
        ).astype(own.dtype)

    for q in (0, 2):
        place(q)
    greet((to_r, to_l, to_z, to_c))
    mail = Mail(send_sem, recv_sem)
    whole, lower, upper = pl.ds(0, slab), pl.ds(0, 2 * h), pl.ds(2 * h, 2 * h)

    def send_own(name, q, to):
        rows = pl.ds(q * h, h)
        mail.send((name, q), own.at[rows], out.at[zp, y, c, rows], to)

    def send_on(name, zs, ys, rows, to):
        mail.send(name, out.at[zs, ys, c, rows], out.at[zs, ys, c, rows], to)

    def quarter(q):
        return pl.ds(q * h, h)

    for q in (0, 2):
        send_own("r" if q == 0 else "l", q, to_r if q == 0 else to_l)
        send_own("z", q, to_z)
    for q in (1, 3):
        place(q)
        send_own("r" if q == 1 else "l", q, to_r if q == 1 else to_l)
        send_own("z", q, to_z)
    send_own("r", 2, to_r)
    send_own("l", 0, to_l)
    mail.send("c0", own, out.at[zp, y, c], to_c)
    own_copy = pltpu.make_async_copy(own, out.at[zp, y, c], own_sem)
    own_copy.start()
    mail.await_recv(("r", 0))
    send_on(("fr", 0), zp, yl, quarter(0), to_r)
    mail.await_recv(("l", 2))
    send_on(("fl", 2), zp, yr, quarter(2), to_l)
    send_own("r", 3, to_r)
    send_own("l", 1, to_l)
    mail.await_recv(("r", 1))
    send_on(("fr", 1), zp, yl, quarter(1), to_r)
    mail.await_recv(("l", 3))
    send_on(("fl", 3), zp, yr, quarter(3), to_l)
    for q in (0, 2):
        mail.await_recv(("z", q))
        send_on(("pr", q), zq, y, quarter(q), to_r)
        send_on(("pl", q), zq, y, quarter(q), to_l)
    mail.await_recv(("fr", 0))
    send_on(("zo", 0), zp, yo, quarter(0), to_z)
    mail.await_recv(("fl", 2))
    send_on(("zo", 2), zp, yo, quarter(2), to_z)
    for q in (1, 3):
        mail.await_recv(("z", q))
        send_on(("pr", q), zq, y, quarter(q), to_r)
        send_on(("pl", q), zq, y, quarter(q), to_l)
    send_on("c1", zq, y, whole, to_c)
    mail.await_recv(("r", 2), ("r", 3), ("l", 0), ("l", 1))
    send_on("c2", zp, yl, whole, to_c)
    send_on("c3", zp, yr, whole, to_c)
    mail.await_recv(("fr", 1))
    send_on(("zo", 1), zp, yo, quarter(1), to_z)
    mail.await_recv(("fl", 3))
    send_on(("zo", 3), zp, yo, quarter(3), to_z)
    send_on("c4", zp, yo, whole, to_c)
    last = []
    for q in (0, 2, 1, 3):
        for name, zs, ys in (("pr", zq, yl), ("pl", zq, yr), ("zo", zq, yo)):
            mail.await_recv((name, q))
            last.append(("c" + name, q))
            send_on(last[-1], zs, ys, quarter(q), to_c)
    own_copy.wait()
    mail.await_recv("c0", "c1", "c2", "c3", "c4", *last)
    mail.finish()


def col_gather(order, features):
    slab, width = features.shape
    vmem = pl.BlockSpec(memory_space=pltpu.VMEM)
    out = pl.pallas_call(
        gather_kernel,
        out_shape=jax.ShapeDtypeStruct((2, 4, 2, slab, width), features.dtype),
        in_specs=[vmem, vmem],
        out_specs=vmem,
        scratch_shapes=[
            pltpu.VMEM((slab, width), features.dtype),
            pltpu.SemaphoreType.DMA((45,)),
            pltpu.SemaphoreType.DMA((45,)),
            pltpu.SemaphoreType.DMA,
        ],
        compiler_params=pltpu.CompilerParams(
            collective_id=0, has_side_effects=True, vmem_limit_bytes=16 << 20
        ),
    )(order, features)
    return out.reshape(16, slab, width)


def sum_kernel(
    part, weight, out, sib, both, z1, s2_l, s2_r, s3_l, s3_r, opp, s4b_l, s4b_r, s4a_l, s4a_r,
    c_r, c_l, via, z2, send_sem, recv_sem,
):
    slab = part.shape[3]
    h = slab // 2
    me = lax.axis_index("col")
    zp, y, c = me // 8, (me // 2) % 4, me % 2
    yr, yl, yo, zq, d = (y + 1) % 4, (y + 3) % 4, (y + 2) % 4, 1 - zp, 1 - c
    to_r, to_l = {"col": zp * 8 + yr * 2 + c}, {"col": zp * 8 + yl * 2 + c}
    to_z, to_c = {"col": zq * 8 + y * 2 + c}, {"col": zp * 8 + y * 2 + d}
    a, b = pl.ds(0, h), pl.ds(h, h)
    dests = ((zq, yo), (zq, yr), (zq, yl), (zp, yr), (zp, yl), (zp, yo), (zq, y), (zp, y))
    greet((to_r, to_l, to_z, to_c))
    mail = Mail(send_sem, recv_sem)
    for i, (zs, ys) in enumerate(dests):
        mail.send(("c", i), part.at[zs, ys, d], sib.at[i], to_c)

    def join(i):
        zs, ys = dests[i]
        mail.await_recv(("c", i))
        add_rows(both.at[i], (part.at[zs, ys, c], sib.at[i]))

    join(0)
    mail.send("z1", both.at[0], z1, to_z)
    join(1)
    mail.send("s2r", both.at[1], s2_l, to_r)
    join(2)
    mail.send("s2l", both.at[2], s2_r, to_l)
    join(3)
    mail.send("s4br", both.at[3, b], s4b_l, to_r)
    join(4)
    mail.send("s4bl", both.at[4, a], s4b_r, to_l)
    join(5)
    mail.await_recv("z1")
    add_rows(opp, (both.at[5], z1))
    mail.send("s3r", opp.at[a], s3_l, to_r)
    mail.send("s3l", opp.at[b], s3_r, to_l)
    join(6)
    join(7)
    mail.await_recv("s2r", "s2l")
    add_rows(via, (both.at[6], s2_l, s2_r))
    mail.send("z2", via, z2, to_z)
    mail.await_recv("s3r")
    add_rows(c_r, (both.at[3, a], s3_l))
    mail.send("s4ar", c_r, s4a_l, to_r)
    mail.await_recv("s3l")
    add_rows(c_l, (both.at[4, b], s3_r))
    mail.send("s4al", c_l, s4a_r, to_l)
    mail.await_recv("z2", "s4bl", "s4ar")
    dense_relu(out.at[a], (both.at[7, a], s4a_l, s4b_r, z2.at[a]), weight)
    mail.await_recv("s4br", "s4al")
    dense_relu(out.at[b], (both.at[7, b], s4b_l, s4a_r, z2.at[b]), weight)
    mail.finish()


def col_sum(part, weight):
    _, slab, width = part.shape
    dt, h = part.dtype, slab // 2
    vmem = pl.BlockSpec(memory_space=pltpu.VMEM)
    full, half = pltpu.VMEM((slab, width), dt), pltpu.VMEM((h, width), dt)
    return pl.pallas_call(
        sum_kernel,
        out_shape=jax.ShapeDtypeStruct((slab, width), dt),
        in_specs=[vmem, vmem],
        out_specs=vmem,
        scratch_shapes=(
            [pltpu.VMEM((8, slab, width), dt)] * 2
            + [full] * 3 + [half] * 2 + [full] + [half] * 6 + [full] * 2
            + [pltpu.SemaphoreType.DMA((18,))] * 2
        ),
        compiler_params=pltpu.CompilerParams(
            collective_id=2, has_side_effects=True, vmem_limit_bytes=28 << 20
        ),
    )(part.reshape(2, 4, 2, slab, width), weight)


CHUNK = 16


def product_kernel(
    transposed, unroll, source_ref, target_ref, count_ref, panel, tile_hbm, out,
    tiles, total, tile_sem,
):
    slots = tile_hbm.shape[0]
    blocks = panel.shape[0]
    chunks = slots // CHUNK
    live = count_ref[0, 0]

    def tile_copy(c):
        part = pl.ds(c * CHUNK, CHUNK)
        return pltpu.make_async_copy(tile_hbm.at[part], tiles.at[part], tile_sem.at[c])

    for c in range(chunks):
        pl.when(c * CHUNK < live)(lambda c=c: tile_copy(c).start())

    @pl.loop(0, blocks)
    def _(g):
        total[g] = jnp.zeros_like(total[g])

    dims = (((0,), (0,)), ((), ())) if transposed else (((1,), (0,)), ((), ()))

    def some_slots(first):
        products, targets = [], []
        for k in range(unroll):
            slot = first + k
            products.append(lax.dot_general(
                tiles[slot], panel[source_ref[0, slot]], dims, preferred_element_type=jnp.float32
            ))
            targets.append(jnp.where(slot < live, target_ref[0, slot], blocks))
        for k in range(unroll):
            total[targets[k]] += products[k]

    def one_chunk(c):
        tile_copy(c).wait()
        if unroll == CHUNK:
            some_slots(c * CHUNK)
        else:
            @pl.loop(0, CHUNK // unroll)
            def _(step):
                first = c * CHUNK + step * unroll
                pl.when(first < live)(lambda: some_slots(first))

    @pl.loop(0, chunks)
    def _(c):
        pl.when(c * CHUNK < live)(lambda: one_chunk(c))

    @pl.loop(0, blocks)
    def _(g):
        out[g] = total[g].astype(out.dtype)


def block_product(panel, tiles, source_ids, target_ids, count, transposed, unroll=16):
    slots, block, _ = tiles.shape
    blocks, _, width = panel.shape
    smem = pl.BlockSpec(memory_space=pltpu.SMEM)
    vmem = pl.BlockSpec(memory_space=pltpu.VMEM)
    return pl.pallas_call(
        functools.partial(product_kernel, transposed, unroll),
        out_shape=jax.ShapeDtypeStruct(panel.shape, panel.dtype),
        in_specs=[smem, smem, smem, vmem, pl.BlockSpec(memory_space=pl.ANY)],
        out_specs=vmem,
        scratch_shapes=[
            pltpu.VMEM(tiles.shape, tiles.dtype),
            pltpu.VMEM((blocks + 1, block, width), jnp.float32),
            pltpu.SemaphoreType.DMA((slots // CHUNK,)),
        ],
        compiler_params=pltpu.CompilerParams(vmem_limit_bytes=36 << 20),
        cost_estimate=pl.CostEstimate(
            flops=2 * slots * block * block * width, transcendentals=0,
            bytes_accessed=2 * (tiles.size + 2 * panel.size),
        ),
    )(source_ids, target_ids, count, panel, tiles)


def on_device(
    features, node_order, block_rows, block_cols, block_counts, adjacency, weight_one, weight_two
):
    tiles = adjacency[0, 0]
    rows, cols = block_rows[0], block_cols[0]
    block, (slab, width) = tiles.shape[-1], features.shape
    row_panel = col_gather(node_order, features)
    partial_one = block_product(
        row_panel.reshape(-1, block, width), tiles, rows, cols, block_counts, True
    )
    col_panel = row_exchange(partial_one.reshape(-1, slab, width), weight_one)
    partial_two = block_product(
        col_panel.reshape(-1, block, width), tiles, cols, rows, block_counts, False
    )
    return col_sum(partial_two.reshape(-1, slab, width), weight_two)


def solution(mesh):
    in_specs = (
        P(("row", "col"), None),
        P(("row", "col"), None),
        P("row", "col", None),
        P("row", "col", None),
        P("row", "col"),
        P("row", "col", None, None, None),
        P(),
        P(),
    )
    out_specs = P(("row", "col"), None)
    return jax.shard_map(
        on_device, mesh=mesh, in_specs=in_specs, out_specs=out_specs, check_vma=False
    )
```

```python
import functools
import jax
import jax.numpy as jnp
from jax import lax
from jax.experimental import pallas as pl
from jax.experimental.pallas import tpu as pltpu
from jax.sharding import PartitionSpec as P

MESH = pl.DeviceIdType.MESH
PARTS = 4
LAGS = dict(r1=0, r2=1, r3=2, r4=3, r5=4, d=5, g2=6, g4=6, g5=8, g3=7, g3o=7, g4o=9, end=12)


class Mail:
    def __init__(self, send_sem, recv_sem):
        self.send_sem, self.recv_sem, self.sent = send_sem, recv_sem, {}

    def send(self, name, src, dst, device):
        slot = len(self.sent)
        copy = pltpu.make_async_remote_copy(
            src_ref=src, dst_ref=dst, send_sem=self.send_sem.at[slot],
            recv_sem=self.recv_sem.at[slot], device_id=device, device_id_type=MESH,
        )
        copy.start()
        self.sent[name] = copy

    def await_recv(self, *names):
        for name in names:
            self.sent[name].wait_recv()

    def finish(self):
        for copy in self.sent.values():
            copy.wait_send()


def greet(devices, meanwhile=None):
    barrier = pltpu.get_barrier_semaphore()
    for device in devices:
        pl.semaphore_signal(barrier, inc=1, device_id=device, device_id_type=MESH)
    if meanwhile is not None:
        meanwhile()
    pl.semaphore_wait(barrier, len(devices))


def add_rows(out, terms):
    rows = out.shape[0]
    step = next(s for s in (64, 48, 32, 16) if rows % s == 0)

    @pl.loop(0, rows // step)
    def _(i):
        at = pl.ds(pl.multiple_of(i * step, step), step)
        total = terms[0][at].astype(jnp.float32)
        for term in terms[1:]:
            total += term[at].astype(jnp.float32)
        out[at] = total.astype(out.dtype)


def dense_relu(out, terms, weight):
    total = terms[0][...].astype(jnp.float32)
    for term in terms[1:]:
        total += term[...].astype(jnp.float32)
    product = jnp.dot(total.astype(jnp.bfloat16), weight[...], preferred_element_type=jnp.float32)
    out[...] = jnp.maximum(product, 0.0).astype(out.dtype)


def row_kernel(
    part, weight, out, r1_l, r1_r, cz, r2_l, r2_r, r2o_l, r2o_r, cx_r, cx_l, r3m_l, r3m_r,
    r3b_l, r3a_r, r3a_l, r3b_r, sx, r4_l, r4_r, r5b_l, r5a_r, r5a_l, r5b_r, cs_r, cs_l, hid,
    send_sem, recv_sem, hid_sem,
):
    slab = part.shape[3]
    n = slab // PARTS
    h = n // 2
    me = lax.axis_index("row")
    z, x = me // 4, me % 4
    xr, xl, xo = (x + 1) % 4, (x + 3) % 4, (x + 2) % 4
    zr, zl, zo = (z + 1) % 4, (z + 3) % 4, (z + 2) % 4
    to_xr, to_xl = {"row": z * 4 + xr}, {"row": z * 4 + xl}
    to_zr, to_zl = {"row": zr * 4 + x}, {"row": zl * 4 + x}
    same, other = z % 2, 1 - z % 2

    def at(ref, zs, xs, rows):
        return ref.at[zs // 2, zs % 2, xs, rows]

    greet((to_xr, to_xl, to_zr, to_zl))
    mail = Mail(send_sem, recv_sem)

    def rows(p):
        return pl.ds(p * n, n), pl.ds(p * n, h), pl.ds(p * n + h, h)

    def r1(p):
        n_, a, b = rows(p)
        mail.send(("r1r", p), at(part, zr, xo, n_), r1_l.at[p], to_zr)
        mail.send(("r1l", p), at(part, zl, xo, n_), r1_r.at[p], to_zl)
        mail.send(("r2or", p), at(part, zo, xo, a), r2o_l.at[p], to_xr)
        mail.send(("r2ol", p), at(part, zo, xo, b), r2o_r.at[p], to_xl)
        mail.send(("r3mr", p), part.at[:, other, xr, n_], r3m_l.at[p], to_xr)
        mail.send(("r3ml", p), part.at[:, other, xl, n_], r3m_r.at[p], to_xl)
        mail.send(("r3br", p), part.at[:, same, xr, b], r3b_l.at[p], to_xr)
        mail.send(("r3al", p), part.at[:, same, xl, a], r3a_r.at[p], to_xl)

    def r2(p):
        n_, a, b = rows(p)
        mail.await_recv(("r1r", p), ("r1l", p))
        add_rows(cz.at[p], (part.at[z // 2, same, xo, n_], r1_l.at[p], r1_r.at[p]))
        mail.send(("r2r", p), cz.at[p, pl.ds(0, h)], r2_l.at[p], to_xr)
        mail.send(("r2l", p), cz.at[p, pl.ds(h, h)], r2_r.at[p], to_xl)

    def r3(p):
        n_, a, b = rows(p)
        mail.await_recv(("r2r", p), ("r2or", p))
        add_rows(cx_r.at[p, z // 2], (part.at[z // 2, same, xr, a], r2_l.at[p]))
        add_rows(cx_r.at[p, zo // 2], (part.at[zo // 2, same, xr, a], r2o_l.at[p]))
        mail.send(("r3ar", p), cx_r.at[p], r3a_l.at[p], to_xr)
        mail.await_recv(("r2l", p), ("r2ol", p))
        add_rows(cx_l.at[p, z // 2], (part.at[z // 2, same, xl, b], r2_r.at[p]))
        add_rows(cx_l.at[p, zo // 2], (part.at[zo // 2, same, xl, b], r2o_r.at[p]))
        mail.send(("r3bl", p), cx_l.at[p], r3b_r.at[p], to_xl)

    def r4(p):
        n_, a, b = rows(p)
        first, second = pl.ds(0, h), pl.ds(h, h)
        mail.await_recv(("r3ar", p), ("r3al", p))
        for k in range(2):
            add_rows(sx.at[p, k, same, first], (part.at[k, same, x, a], r3a_l.at[p, k], r3a_r.at[p, k]))
        mail.send(("r4r", p), sx.at[p, zo // 2, same, first], r4_l.at[p], to_zr)
        mail.await_recv(("r3br", p), ("r3bl", p))
        for k in range(2):
            add_rows(sx.at[p, k, same, second], (part.at[k, same, x, b], r3b_l.at[p, k], r3b_r.at[p, k]))
        mail.send(("r4l", p), sx.at[p, zo // 2, same, second], r4_r.at[p], to_zl)
        mail.await_recv(("r3mr", p), ("r3ml", p))
        for k in range(2):
            add_rows(sx.at[p, k, other], (part.at[k, other, x, n_], r3m_l.at[p, k], r3m_r.at[p, k]))
        mail.send(("r5br", p), sx.at[p, zr // 2, other, second], r5b_l.at[p], to_zr)
        mail.send(("r5al", p), sx.at[p, zl // 2, other, first], r5a_r.at[p], to_zl)

    def r5(p):
        mail.await_recv(("r4r", p))
        add_rows(cs_r.at[p], (sx.at[p, zr // 2, other, pl.ds(0, h)], r4_l.at[p]))
        mail.send(("r5ar", p), cs_r.at[p], r5a_l.at[p], to_zr)
        mail.await_recv(("r4l", p))
        add_rows(cs_l.at[p], (sx.at[p, zl // 2, other, pl.ds(h, h)], r4_r.at[p]))
        mail.send(("r5bl", p), cs_l.at[p], r5b_r.at[p], to_zl)

    def dense(p):
        n_, a, b = rows(p)
        mine = sx.at[p, z // 2, same]
        mail.await_recv(("r5ar", p), ("r5al", p))
        dense_relu(hid.at[a], (mine.at[pl.ds(0, h)], r5a_l.at[p], r5a_r.at[p]), weight)
        mail.send(("g1ar", p), hid.at[a], at(out, z, x, a), to_zr)
        mail.send(("g3ar", p), hid.at[a], at(out, z, x, a), to_xr)
        mail.await_recv(("r5br", p), ("r5bl", p))
        dense_relu(hid.at[b], (mine.at[pl.ds(h, h)], r5b_l.at[p], r5b_r.at[p]), weight)
        mail.send(("g1bl", p), hid.at[b], at(out, z, x, b), to_zl)
        mail.send(("g3bl", p), hid.at[b], at(out, z, x, b), to_xl)
        mail.send(("g1br", p), hid.at[b], at(out, z, x, b), to_zr)
        mail.send(("g1al", p), hid.at[a], at(out, z, x, a), to_zl)
        mail.send(("g3br", p), hid.at[b], at(out, z, x, b), to_xr)
        mail.send(("g3al", p), hid.at[a], at(out, z, x, a), to_xl)
        pltpu.make_async_copy(hid.at[n_], at(out, z, x, n_), hid_sem.at[p]).start()

    def pass_on(name, p, zs, xs, rows_, to):
        mail.send((name, p), at(out, zs, xs, rows_), at(out, zs, xs, rows_), to)

    def g2(p):
        n_, a, b = rows(p)
        mail.await_recv(("g1ar", p))
        pass_on("g2r", p, zl, x, a, to_zr)
        mail.await_recv(("g1bl", p))
        pass_on("g2l", p, zr, x, b, to_zl)

    def g4(p):
        n_, a, b = rows(p)
        mail.await_recv(("g3ar", p))
        pass_on("g4r", p, z, xl, a, to_xr)
        mail.await_recv(("g3bl", p))
        pass_on("g4l", p, z, xr, b, to_xl)

    def g5(p):
        n_, a, b = rows(p)
        mail.await_recv(("g4r", p), ("g4l", p))
        pass_on("g5r", p, z, xo, n_, to_zr)
        pass_on("g5l", p, z, xo, n_, to_zl)

    def g3(p):
        n_, a, b = rows(p)
        mail.await_recv(("g1br", p), ("g1al", p))
        both = out.at[:, other, x, n_]
        mail.send(("g3mr", p), both, both, to_xr)
        mail.send(("g3ml", p), both, both, to_xl)

    def g3o(p):
        n_, a, b = rows(p)
        mail.await_recv(("g2r", p))
        pass_on("g3oar", p, zo, x, a, to_xr)
        mail.await_recv(("g2l", p))
        pass_on("g3obl", p, zo, x, b, to_xl)
        pass_on("g3obr", p, zo, x, b, to_xr)
        pass_on("g3oal", p, zo, x, a, to_xl)

    def g4o(p):
        n_, a, b = rows(p)
        mail.await_recv(("g3oar", p))
        pass_on("g4or", p, zo, xl, a, to_xr)
        mail.await_recv(("g3obl", p))
        pass_on("g4ol", p, zo, xr, b, to_xl)

    def end(p):
        n_, a, b = rows(p)
        pltpu.make_async_copy(hid.at[n_], at(out, z, x, n_), hid_sem.at[p]).wait()
        mail.await_recv(*((name, p) for name in (
            "g3br", "g3al", "g3mr", "g3ml", "g3obr", "g3oal", "g4or", "g4ol", "g5r", "g5l"
        )))

    stages = dict(
        r1=r1, r2=r2, r3=r3, r4=r4, r5=r5, d=dense, g2=g2, g4=g4, g5=g5, g3=g3, g3o=g3o, g4o=g4o,
        end=end,
    )
    order = sorted(stages, key=lambda name: -LAGS[name])
    for tick in range(PARTS + max(LAGS.values())):
        for name in order:
            if 0 <= tick - LAGS[name] < PARTS:
                stages[name](tick - LAGS[name])
    mail.finish()


def row_exchange(part, weight):
    _, slab, width = part.shape
    n = slab // PARTS
    h = n // 2
    dt = part.dtype
    vmem = pl.BlockSpec(memory_space=pltpu.VMEM)
    count = 40 * PARTS

    def buf(*lead):
        return [pltpu.VMEM((PARTS, *lead, width), dt)]

    out = pl.pallas_call(
        row_kernel,
        out_shape=jax.ShapeDtypeStruct((2, 2, 4, slab, width), dt),
        in_specs=[vmem, vmem],
        out_specs=vmem,
        scratch_shapes=(
            buf(n) * 3 + buf(h) * 4 + buf(2, h) * 2 + buf(2, n) * 2 + buf(2, h) * 4
            + buf(2, 2, n) + buf(h) * 8
            + [pltpu.VMEM((slab, width), dt)]
            + [pltpu.SemaphoreType.DMA((count,))] * 2
            + [pltpu.SemaphoreType.DMA((PARTS,))]
        ),
        compiler_params=pltpu.CompilerParams(
            collective_id=1, has_side_effects=True, vmem_limit_bytes=28 << 20
        ),
    )(part.reshape(2, 2, 4, slab, width), weight)
    return out.reshape(16, slab, width)


def gather_kernel(
    order_hbm, features_hbm, out, order, features, own, send_sem, recv_sem, own_sem, load_sem
):
    slab = features.shape[0]
    h = slab // 4
    me = lax.axis_index("col")
    zp, y, c = me // 8, (me // 2) % 4, me % 2
    yr, yl, yo, zq = (y + 1) % 4, (y + 3) % 4, (y + 2) % 4, 1 - zp
    to_r, to_l = {"col": zp * 8 + yr * 2 + c}, {"col": zp * 8 + yl * 2 + c}
    to_z, to_c = {"col": zq * 8 + y * 2 + c}, {"col": zp * 8 + y * 2 + 1 - c}

    def place(q):
        at = pl.ds(q * h, h)
        chosen = lax.broadcasted_iota(jnp.int32, (slab, h), 0) == order[:, at]
        own[at] = lax.dot_general(
            chosen.astype(features.dtype), features[...], (((0,), (0,)), ((), ())),
            preferred_element_type=jnp.float32,
        ).astype(own.dtype)

    def begin():
        loads = (
            pltpu.make_async_copy(features_hbm, features, load_sem.at[0]),
            pltpu.make_async_copy(order_hbm, order, load_sem.at[1]),
        )
        for load in loads:
            load.start()
        for load in loads:
            load.wait()
        for q in (0, 2):
            place(q)

    greet((to_r, to_l, to_z, to_c), begin)
    mail = Mail(send_sem, recv_sem)
    whole, lower, upper = pl.ds(0, slab), pl.ds(0, 2 * h), pl.ds(2 * h, 2 * h)

    def send_own(name, q, to):
        rows = pl.ds(q * h, h)
        mail.send((name, q), own.at[rows], out.at[zp, y, c, rows], to)

    def send_on(name, zs, ys, rows, to):
        mail.send(name, out.at[zs, ys, c, rows], out.at[zs, ys, c, rows], to)

    def quarter(q):
        return pl.ds(q * h, h)

    for q in (0, 2):
        send_own("r" if q == 0 else "l", q, to_r if q == 0 else to_l)
        send_own("z", q, to_z)
    for q in (1, 3):
        place(q)
        send_own("r" if q == 1 else "l", q, to_r if q == 1 else to_l)
        send_own("z", q, to_z)
    send_own("r", 2, to_r)
    send_own("l", 0, to_l)
    mail.send("c0", own, out.at[zp, y, c], to_c)
    own_copy = pltpu.make_async_copy(own, out.at[zp, y, c], own_sem)
    own_copy.start()
    mail.await_recv(("r", 0))
    send_on(("fr", 0), zp, yl, quarter(0), to_r)
    mail.await_recv(("l", 2))
    send_on(("fl", 2), zp, yr, quarter(2), to_l)
    send_own("r", 3, to_r)
    send_own("l", 1, to_l)
    mail.await_recv(("r", 1))
    send_on(("fr", 1), zp, yl, quarter(1), to_r)
    mail.await_recv(("l", 3))
    send_on(("fl", 3), zp, yr, quarter(3), to_l)
    for q in (0, 2):
        mail.await_recv(("z", q))
        send_on(("pr", q), zq, y, quarter(q), to_r)
        send_on(("pl", q), zq, y, quarter(q), to_l)
    mail.await_recv(("fr", 0))
    send_on(("zo", 0), zp, yo, quarter(0), to_z)
    mail.await_recv(("fl", 2))
    send_on(("zo", 2), zp, yo, quarter(2), to_z)
    for q in (1, 3):
        mail.await_recv(("z", q))
        send_on(("pr", q), zq, y, quarter(q), to_r)
        send_on(("pl", q), zq, y, quarter(q), to_l)
    send_on("c1", zq, y, whole, to_c)
    mail.await_recv(("r", 2), ("r", 3), ("l", 0), ("l", 1))
    send_on("c2", zp, yl, whole, to_c)
    send_on("c3", zp, yr, whole, to_c)
    mail.await_recv(("fr", 1))
    send_on(("zo", 1), zp, yo, quarter(1), to_z)
    mail.await_recv(("fl", 3))
    send_on(("zo", 3), zp, yo, quarter(3), to_z)
    send_on("c4", zp, yo, whole, to_c)
    last = []
    for q in (0, 2, 1, 3):
        for name, zs, ys in (("pr", zq, yl), ("pl", zq, yr), ("zo", zq, yo)):
            mail.await_recv((name, q))
            last.append(("c" + name, q))
            send_on(last[-1], zs, ys, quarter(q), to_c)
    own_copy.wait()
    mail.await_recv("c0", "c1", "c2", "c3", "c4", *last)
    mail.finish()


def col_gather(order, features):
    slab, width = features.shape
    hbm = pl.BlockSpec(memory_space=pltpu.HBM)
    out = pl.pallas_call(
        gather_kernel,
        out_shape=jax.ShapeDtypeStruct((2, 4, 2, slab, width), features.dtype),
        in_specs=[hbm, hbm],
        out_specs=pl.BlockSpec(memory_space=pltpu.VMEM),
        scratch_shapes=[
            pltpu.VMEM(order.shape, order.dtype),
            pltpu.VMEM((slab, width), features.dtype),
            pltpu.VMEM((slab, width), features.dtype),
            pltpu.SemaphoreType.DMA((45,)),
            pltpu.SemaphoreType.DMA((45,)),
            pltpu.SemaphoreType.DMA,
            pltpu.SemaphoreType.DMA((2,)),
        ],
        compiler_params=pltpu.CompilerParams(
            collective_id=0, has_side_effects=True, vmem_limit_bytes=16 << 20
        ),
    )(order, features)
    return out.reshape(16, slab, width)


def sum_kernel(
    part, weight, out, sib, both, z1, s2_l, s2_r, s3_l, s3_r, opp, s4b_l, s4b_r, s4a_l, s4a_r,
    c_r, c_l, via, z2, send_sem, recv_sem,
):
    slab = part.shape[3]
    h = slab // 2
    me = lax.axis_index("col")
    zp, y, c = me // 8, (me // 2) % 4, me % 2
    yr, yl, yo, zq, d = (y + 1) % 4, (y + 3) % 4, (y + 2) % 4, 1 - zp, 1 - c
    to_r, to_l = {"col": zp * 8 + yr * 2 + c}, {"col": zp * 8 + yl * 2 + c}
    to_z, to_c = {"col": zq * 8 + y * 2 + c}, {"col": zp * 8 + y * 2 + d}
    a, b = pl.ds(0, h), pl.ds(h, h)
    dests = ((zq, yo), (zq, yr), (zq, yl), (zp, yr), (zp, yl), (zp, yo), (zq, y), (zp, y))
    greet((to_r, to_l, to_z, to_c))
    mail = Mail(send_sem, recv_sem)
    for i, (zs, ys) in enumerate(dests):
        mail.send(("c", i), part.at[zs, ys, d], sib.at[i], to_c)

    def join(i):
        zs, ys = dests[i]
        mail.await_recv(("c", i))
        add_rows(both.at[i], (part.at[zs, ys, c], sib.at[i]))

    join(0)
    mail.send("z1", both.at[0], z1, to_z)
    join(1)
    mail.send("s2r", both.at[1], s2_l, to_r)
    join(2)
    mail.send("s2l", both.at[2], s2_r, to_l)
    join(3)
    mail.send("s4br", both.at[3, b], s4b_l, to_r)
    join(4)
    mail.send("s4bl", both.at[4, a], s4b_r, to_l)
    join(5)
    mail.await_recv("z1")
    add_rows(opp, (both.at[5], z1))
    mail.send("s3r", opp.at[a], s3_l, to_r)
    mail.send("s3l", opp.at[b], s3_r, to_l)
    join(6)
    join(7)
    mail.await_recv("s2r", "s2l")
    add_rows(via, (both.at[6], s2_l, s2_r))
    mail.send("z2", via, z2, to_z)
    mail.await_recv("s3r")
    add_rows(c_r, (both.at[3, a], s3_l))
    mail.send("s4ar", c_r, s4a_l, to_r)
    mail.await_recv("s3l")
    add_rows(c_l, (both.at[4, b], s3_r))
    mail.send("s4al", c_l, s4a_r, to_l)
    mail.await_recv("z2", "s4bl", "s4ar")
    dense_relu(out.at[a], (both.at[7, a], s4a_l, s4b_r, z2.at[a]), weight)
    mail.await_recv("s4br", "s4al")
    dense_relu(out.at[b], (both.at[7, b], s4b_l, s4a_r, z2.at[b]), weight)
    mail.finish()


def col_sum(part, weight):
    _, slab, width = part.shape
    dt, h = part.dtype, slab // 2
    vmem = pl.BlockSpec(memory_space=pltpu.VMEM)
    full, half = pltpu.VMEM((slab, width), dt), pltpu.VMEM((h, width), dt)
    return pl.pallas_call(
        sum_kernel,
        out_shape=jax.ShapeDtypeStruct((slab, width), dt),
        in_specs=[vmem, vmem],
        out_specs=vmem,
        scratch_shapes=(
            [pltpu.VMEM((8, slab, width), dt)] * 2
            + [full] * 3 + [half] * 2 + [full] + [half] * 6 + [full] * 2
            + [pltpu.SemaphoreType.DMA((18,))] * 2
        ),
        compiler_params=pltpu.CompilerParams(
            collective_id=2, has_side_effects=True, vmem_limit_bytes=28 << 20
        ),
    )(part.reshape(2, 4, 2, slab, width), weight)


CHUNK = 16


def product_kernel(
    transposed, unroll, source_ref, target_ref, count_ref, panel, tile_hbm, out,
    tiles, total, tile_sem,
):
    slots = tile_hbm.shape[0]
    blocks = panel.shape[0]
    chunks = slots // CHUNK
    live = count_ref[0, 0]

    def tile_copy(c):
        part = pl.ds(c * CHUNK, CHUNK)
        return pltpu.make_async_copy(tile_hbm.at[part], tiles.at[part], tile_sem.at[c])

    for c in range(chunks):
        pl.when(c * CHUNK < live)(lambda c=c: tile_copy(c).start())

    @pl.loop(0, blocks)
    def _(g):
        total[g] = jnp.zeros_like(total[g])

    dims = (((0,), (0,)), ((), ())) if transposed else (((1,), (0,)), ((), ()))

    def some_slots(first):
        products, targets = [], []
        for k in range(unroll):
            slot = first + k
            products.append(lax.dot_general(
                tiles[slot], panel[source_ref[0, slot]], dims, preferred_element_type=jnp.float32
            ))
            targets.append(jnp.where(slot < live, target_ref[0, slot], blocks))
        for k in range(unroll):
            total[targets[k]] += products[k]

    def one_chunk(c):
        tile_copy(c).wait()
        if unroll == CHUNK:
            some_slots(c * CHUNK)
        else:
            @pl.loop(0, CHUNK // unroll)
            def _(step):
                first = c * CHUNK + step * unroll
                pl.when(first < live)(lambda: some_slots(first))

    @pl.loop(0, chunks)
    def _(c):
        pl.when(c * CHUNK < live)(lambda: one_chunk(c))

    @pl.loop(0, blocks)
    def _(g):
        out[g] = total[g].astype(out.dtype)


def block_product(panel, tiles, source_ids, target_ids, count, transposed, unroll=16):
    slots, block, _ = tiles.shape
    blocks, _, width = panel.shape
    smem = pl.BlockSpec(memory_space=pltpu.SMEM)
    vmem = pl.BlockSpec(memory_space=pltpu.VMEM)
    return pl.pallas_call(
        functools.partial(product_kernel, transposed, unroll),
        out_shape=jax.ShapeDtypeStruct(panel.shape, panel.dtype),
        in_specs=[smem, smem, smem, vmem, pl.BlockSpec(memory_space=pl.ANY)],
        out_specs=vmem,
        scratch_shapes=[
            pltpu.VMEM(tiles.shape, tiles.dtype),
            pltpu.VMEM((blocks + 1, block, width), jnp.float32),
            pltpu.SemaphoreType.DMA((slots // CHUNK,)),
        ],
        compiler_params=pltpu.CompilerParams(vmem_limit_bytes=36 << 20),
        cost_estimate=pl.CostEstimate(
            flops=2 * slots * block * block * width, transcendentals=0,
            bytes_accessed=2 * (tiles.size + 2 * panel.size),
        ),
    )(source_ids, target_ids, count, panel, tiles)


def on_device(
    features, node_order, block_rows, block_cols, block_counts, adjacency, weight_one, weight_two
):
    tiles = adjacency[0, 0]
    rows, cols = block_rows[0], block_cols[0]
    block, (slab, width) = tiles.shape[-1], features.shape
    row_panel = col_gather(node_order, features)
    partial_one = block_product(
        row_panel.reshape(-1, block, width), tiles, rows, cols, block_counts, True
    )
    col_panel = row_exchange(partial_one.reshape(-1, slab, width), weight_one)
    partial_two = block_product(
        col_panel.reshape(-1, block, width), tiles, cols, rows, block_counts, False
    )
    return col_sum(partial_two.reshape(-1, slab, width), weight_two)


def solution(mesh):
    in_specs = (
        P(("row", "col"), None),
        P(("row", "col"), None),
        P("row", "col", None),
        P("row", "col", None),
        P("row", "col"),
        P("row", "col", None, None, None),
        P(),
        P(),
    )
    out_specs = P(("row", "col"), None)
    return jax.shard_map(
        on_device, mesh=mesh, in_specs=in_specs, out_specs=out_specs, check_vma=False
    )
```

```python
import functools
import jax
import jax.numpy as jnp
from jax import lax
from jax.experimental import pallas as pl
from jax.experimental.pallas import tpu as pltpu
from jax.sharding import PartitionSpec as P

MESH = pl.DeviceIdType.MESH
PARTS = 4
LAGS = dict(r1=0, r2=1, r3=2, r4=3, r5=4, d=5, g2=6, g4=6, g5=8, g3=7, g3o=7, g4o=9, end=12)


class Mail:
    def __init__(self, send_sem, recv_sem):
        self.send_sem, self.recv_sem, self.sent = send_sem, recv_sem, {}

    def send(self, name, src, dst, device):
        slot = len(self.sent)
        copy = pltpu.make_async_remote_copy(
            src_ref=src, dst_ref=dst, send_sem=self.send_sem.at[slot],
            recv_sem=self.recv_sem.at[slot], device_id=device, device_id_type=MESH,
        )
        copy.start()
        self.sent[name] = copy

    def await_recv(self, *names):
        for name in names:
            self.sent[name].wait_recv()

    def finish(self):
        for copy in self.sent.values():
            copy.wait_send()


def greet(devices, meanwhile=None):
    barrier = pltpu.get_barrier_semaphore()
    for device in devices:
        pl.semaphore_signal(barrier, inc=1, device_id=device, device_id_type=MESH)
    if meanwhile is not None:
        meanwhile()
    pl.semaphore_wait(barrier, len(devices))


def add_rows(out, terms):
    rows = out.shape[0]
    step = next(s for s in (64, 48, 32, 16) if rows % s == 0)

    @pl.loop(0, rows // step)
    def _(i):
        at = pl.ds(pl.multiple_of(i * step, step), step)
        total = terms[0][at].astype(jnp.float32)
        for term in terms[1:]:
            total += term[at].astype(jnp.float32)
        out[at] = total.astype(out.dtype)


def dense_relu(out, terms, weight):
    total = terms[0][...].astype(jnp.float32)
    for term in terms[1:]:
        total += term[...].astype(jnp.float32)
    product = jnp.dot(total.astype(jnp.bfloat16), weight[...], preferred_element_type=jnp.float32)
    out[...] = jnp.maximum(product, 0.0).astype(out.dtype)


def row_kernel(
    part, weight, out, r1_l, r1_r, cz, r2_l, r2_r, r2o_l, r2o_r, cx_r, cx_l, r3m_l, r3m_r,
    r3b_l, r3a_r, r3a_l, r3b_r, sx, r4_l, r4_r, r5b_l, r5a_r, r5a_l, r5b_r, cs_r, cs_l, hid,
    send_sem, recv_sem, hid_sem,
):
    slab = part.shape[3]
    n = slab // PARTS
    h = n // 2
    me = lax.axis_index("row")
    z, x = me // 4, me % 4
    xr, xl, xo = (x + 1) % 4, (x + 3) % 4, (x + 2) % 4
    zr, zl, zo = (z + 1) % 4, (z + 3) % 4, (z + 2) % 4
    to_xr, to_xl = {"row": z * 4 + xr}, {"row": z * 4 + xl}
    to_zr, to_zl = {"row": zr * 4 + x}, {"row": zl * 4 + x}
    same, other = z % 2, 1 - z % 2

    def at(ref, zs, xs, rows):
        return ref.at[zs // 2, zs % 2, xs, rows]

    greet((to_xr, to_xl, to_zr, to_zl))
    mail = Mail(send_sem, recv_sem)

    def rows(p):
        return pl.ds(p * n, n), pl.ds(p * n, h), pl.ds(p * n + h, h)

    def r1(p):
        n_, a, b = rows(p)
        mail.send(("r1r", p), at(part, zr, xo, n_), r1_l.at[p], to_zr)
        mail.send(("r1l", p), at(part, zl, xo, n_), r1_r.at[p], to_zl)
        mail.send(("r2or", p), at(part, zo, xo, a), r2o_l.at[p], to_xr)
        mail.send(("r2ol", p), at(part, zo, xo, b), r2o_r.at[p], to_xl)
        mail.send(("r3mr", p), part.at[:, other, xr, n_], r3m_l.at[p], to_xr)
        mail.send(("r3ml", p), part.at[:, other, xl, n_], r3m_r.at[p], to_xl)
        mail.send(("r3br", p), part.at[:, same, xr, b], r3b_l.at[p], to_xr)
        mail.send(("r3al", p), part.at[:, same, xl, a], r3a_r.at[p], to_xl)

    def r2(p):
        n_, a, b = rows(p)
        mail.await_recv(("r1r", p), ("r1l", p))
        add_rows(cz.at[p], (part.at[z // 2, same, xo, n_], r1_l.at[p], r1_r.at[p]))
        mail.send(("r2r", p), cz.at[p, pl.ds(0, h)], r2_l.at[p], to_xr)
        mail.send(("r2l", p), cz.at[p, pl.ds(h, h)], r2_r.at[p], to_xl)

    def r3(p):
        n_, a, b = rows(p)
        mail.await_recv(("r2r", p), ("r2or", p))
        add_rows(cx_r.at[p, z // 2], (part.at[z // 2, same, xr, a], r2_l.at[p]))
        add_rows(cx_r.at[p, zo // 2], (part.at[zo // 2, same, xr, a], r2o_l.at[p]))
        mail.send(("r3ar", p), cx_r.at[p], r3a_l.at[p], to_xr)
        mail.await_recv(("r2l", p), ("r2ol", p))
        add_rows(cx_l.at[p, z // 2], (part.at[z // 2, same, xl, b], r2_r.at[p]))
        add_rows(cx_l.at[p, zo // 2], (part.at[zo // 2, same, xl, b], r2o_r.at[p]))
        mail.send(("r3bl", p), cx_l.at[p], r3b_r.at[p], to_xl)

    def r4(p):
        n_, a, b = rows(p)
        first, second = pl.ds(0, h), pl.ds(h, h)
        mail.await_recv(("r3ar", p), ("r3al", p))
        for k in range(2):
            add_rows(sx.at[p, k, same, first], (part.at[k, same, x, a], r3a_l.at[p, k], r3a_r.at[p, k]))
        mail.send(("r4r", p), sx.at[p, zo // 2, same, first], r4_l.at[p], to_zr)
        mail.await_recv(("r3br", p), ("r3bl", p))
        for k in range(2):
            add_rows(sx.at[p, k, same, second], (part.at[k, same, x, b], r3b_l.at[p, k], r3b_r.at[p, k]))
        mail.send(("r4l", p), sx.at[p, zo // 2, same, second], r4_r.at[p], to_zl)
        mail.await_recv(("r3mr", p), ("r3ml", p))
        for k in range(2):
            add_rows(sx.at[p, k, other], (part.at[k, other, x, n_], r3m_l.at[p, k], r3m_r.at[p, k]))
        mail.send(("r5br", p), sx.at[p, zr // 2, other, second], r5b_l.at[p], to_zr)
        mail.send(("r5al", p), sx.at[p, zl // 2, other, first], r5a_r.at[p], to_zl)

    def r5(p):
        mail.await_recv(("r4r", p))
        add_rows(cs_r.at[p], (sx.at[p, zr // 2, other, pl.ds(0, h)], r4_l.at[p]))
        mail.send(("r5ar", p), cs_r.at[p], r5a_l.at[p], to_zr)
        mail.await_recv(("r4l", p))
        add_rows(cs_l.at[p], (sx.at[p, zl // 2, other, pl.ds(h, h)], r4_r.at[p]))
        mail.send(("r5bl", p), cs_l.at[p], r5b_r.at[p], to_zl)

    def dense(p):
        n_, a, b = rows(p)
        mine = sx.at[p, z // 2, same]
        mail.await_recv(("r5ar", p), ("r5al", p))
        dense_relu(hid.at[a], (mine.at[pl.ds(0, h)], r5a_l.at[p], r5a_r.at[p]), weight)
        mail.send(("g1ar", p), hid.at[a], at(out, z, x, a), to_zr)
        mail.send(("g3ar", p), hid.at[a], at(out, z, x, a), to_xr)
        mail.await_recv(("r5br", p), ("r5bl", p))
        dense_relu(hid.at[b], (mine.at[pl.ds(h, h)], r5b_l.at[p], r5b_r.at[p]), weight)
        mail.send(("g1bl", p), hid.at[b], at(out, z, x, b), to_zl)
        mail.send(("g3bl", p), hid.at[b], at(out, z, x, b), to_xl)
        mail.send(("g1br", p), hid.at[b], at(out, z, x, b), to_zr)
        mail.send(("g1al", p), hid.at[a], at(out, z, x, a), to_zl)
        mail.send(("g3br", p), hid.at[b], at(out, z, x, b), to_xr)
        mail.send(("g3al", p), hid.at[a], at(out, z, x, a), to_xl)
        pltpu.make_async_copy(hid.at[n_], at(out, z, x, n_), hid_sem.at[p]).start()

    def pass_on(name, p, zs, xs, rows_, to):
        mail.send((name, p), at(out, zs, xs, rows_), at(out, zs, xs, rows_), to)

    def g2(p):
        n_, a, b = rows(p)
        mail.await_recv(("g1ar", p))
        pass_on("g2r", p, zl, x, a, to_zr)
        mail.await_recv(("g1bl", p))
        pass_on("g2l", p, zr, x, b, to_zl)

    def g4(p):
        n_, a, b = rows(p)
        mail.await_recv(("g3ar", p))
        pass_on("g4r", p, z, xl, a, to_xr)
        mail.await_recv(("g3bl", p))
        pass_on("g4l", p, z, xr, b, to_xl)

    def g5(p):
        n_, a, b = rows(p)
        mail.await_recv(("g4r", p), ("g4l", p))
        pass_on("g5r", p, z, xo, n_, to_zr)
        pass_on("g5l", p, z, xo, n_, to_zl)

    def g3(p):
        n_, a, b = rows(p)
        mail.await_recv(("g1br", p), ("g1al", p))
        both = out.at[:, other, x, n_]
        mail.send(("g3mr", p), both, both, to_xr)
        mail.send(("g3ml", p), both, both, to_xl)

    def g3o(p):
        n_, a, b = rows(p)
        mail.await_recv(("g2r", p))
        pass_on("g3oar", p, zo, x, a, to_xr)
        mail.await_recv(("g2l", p))
        pass_on("g3obl", p, zo, x, b, to_xl)
        pass_on("g3obr", p, zo, x, b, to_xr)
        pass_on("g3oal", p, zo, x, a, to_xl)

    def g4o(p):
        n_, a, b = rows(p)
        mail.await_recv(("g3oar", p))
        pass_on("g4or", p, zo, xl, a, to_xr)
        mail.await_recv(("g3obl", p))
        pass_on("g4ol", p, zo, xr, b, to_xl)

    def end(p):
        n_, a, b = rows(p)
        pltpu.make_async_copy(hid.at[n_], at(out, z, x, n_), hid_sem.at[p]).wait()
        mail.await_recv(*((name, p) for name in (
            "g3br", "g3al", "g3mr", "g3ml", "g3obr", "g3oal", "g4or", "g4ol", "g5r", "g5l"
        )))

    stages = dict(
        r1=r1, r2=r2, r3=r3, r4=r4, r5=r5, d=dense, g2=g2, g4=g4, g5=g5, g3=g3, g3o=g3o, g4o=g4o,
        end=end,
    )
    order = sorted(stages, key=lambda name: -LAGS[name])
    for tick in range(PARTS + max(LAGS.values())):
        for name in order:
            if 0 <= tick - LAGS[name] < PARTS:
                stages[name](tick - LAGS[name])
    mail.finish()


def row_exchange(part, weight):
    _, slab, width = part.shape
    n = slab // PARTS
    h = n // 2
    dt = part.dtype
    vmem = pl.BlockSpec(memory_space=pltpu.VMEM)
    count = 40 * PARTS

    def buf(*lead):
        return [pltpu.VMEM((PARTS, *lead, width), dt)]

    out = pl.pallas_call(
        row_kernel,
        out_shape=jax.ShapeDtypeStruct((2, 2, 4, slab, width), dt),
        in_specs=[vmem, vmem],
        out_specs=vmem,
        scratch_shapes=(
            buf(n) * 3 + buf(h) * 4 + buf(2, h) * 2 + buf(2, n) * 2 + buf(2, h) * 4
            + buf(2, 2, n) + buf(h) * 8
            + [pltpu.VMEM((slab, width), dt)]
            + [pltpu.SemaphoreType.DMA((count,))] * 2
            + [pltpu.SemaphoreType.DMA((PARTS,))]
        ),
        compiler_params=pltpu.CompilerParams(
            collective_id=1, has_side_effects=True, vmem_limit_bytes=28 << 20
        ),
    )(part.reshape(2, 2, 4, slab, width), weight)
    return out.reshape(16, slab, width)


def tail_rows(slab):
    return max(slab // 96, 1) * 16


def gather_kernel(
    order_hbm, features_hbm, out, order, features, own, send_sem, recv_sem, own_sem, load_sem
):
    slab = features.shape[0]
    h = slab // 4
    me = lax.axis_index("col")
    zp, y, c = me // 8, (me // 2) % 4, me % 2
    yr, yl, yo, zq = (y + 1) % 4, (y + 3) % 4, (y + 2) % 4, 1 - zp
    to_r, to_l = {"col": zp * 8 + yr * 2 + c}, {"col": zp * 8 + yl * 2 + c}
    to_z, to_c = {"col": zq * 8 + y * 2 + c}, {"col": zp * 8 + y * 2 + 1 - c}

    def place(q):
        at = pl.ds(q * h, h)
        chosen = lax.broadcasted_iota(jnp.int32, (slab, h), 0) == order[:, at]
        own[at] = lax.dot_general(
            chosen.astype(features.dtype), features[...], (((0,), (0,)), ((), ())),
            preferred_element_type=jnp.float32,
        ).astype(own.dtype)

    def begin():
        loads = (
            pltpu.make_async_copy(features_hbm, features, load_sem.at[0]),
            pltpu.make_async_copy(order_hbm, order, load_sem.at[1]),
        )
        for load in loads:
            load.start()
        for load in loads:
            load.wait()
        for q in (0, 2):
            place(q)

    greet((to_r, to_l, to_z, to_c), begin)
    mail = Mail(send_sem, recv_sem)
    whole, cut = pl.ds(0, slab), tail_rows(slab)
    tail = pl.ds(slab - cut, cut)

    def send_own(name, q, to):
        rows = pl.ds(q * h, h)
        mail.send((name, q), own.at[rows], out.at[zp, y, c, rows], to)

    def send_on(name, zs, ys, rows, to):
        mail.send(name, out.at[zs, ys, c, rows], out.at[zs, ys, c, rows], to)

    def quarter(q):
        return pl.ds(q * h, h)

    def short(q):
        return pl.ds(q * h, h - cut if q == 3 else h)

    for q in (0, 2):
        send_own("r" if q == 0 else "l", q, to_r if q == 0 else to_l)
        send_own("z", q, to_z)
    for q in (1, 3):
        place(q)
        send_own("r" if q == 1 else "l", q, to_r if q == 1 else to_l)
        send_own("z", q, to_z)
    send_own("r", 2, to_r)
    send_own("l", 0, to_l)
    mail.send("c0", own, out.at[zp, y, c], to_c)
    own_copy = pltpu.make_async_copy(own, out.at[zp, y, c], own_sem)
    own_copy.start()
    mail.await_recv(("r", 0))
    send_on(("fr", 0), zp, yl, quarter(0), to_r)
    mail.await_recv(("l", 2))
    send_on(("fl", 2), zp, yr, quarter(2), to_l)
    send_own("r", 3, to_r)
    send_own("l", 1, to_l)
    mail.await_recv(("r", 1))
    send_on(("fr", 1), zp, yl, quarter(1), to_r)
    mail.await_recv(("l", 3))
    send_on(("fl", 3), zp, yr, quarter(3), to_l)
    send_on("tr", zp, yr, tail, to_z)
    for q in (0, 2):
        mail.await_recv(("z", q))
        send_on(("pr", q), zq, y, short(q), to_r)
        send_on(("pl", q), zq, y, short(q), to_l)
    mail.await_recv(("fr", 0))
    send_on(("zo", 0), zp, yo, quarter(0), to_z)
    mail.await_recv(("fl", 2))
    send_on(("zo", 2), zp, yo, quarter(2), to_z)
    for q in (1, 3):
        mail.await_recv(("z", q))
        send_on(("pr", q), zq, y, short(q), to_r)
        send_on(("pl", q), zq, y, short(q), to_l)
    send_on("c1", zq, y, whole, to_c)
    mail.await_recv(("r", 2), ("r", 3), ("l", 0), ("l", 1))
    send_on("tl", zp, yl, tail, to_z)
    send_on("c2", zp, yl, whole, to_c)
    send_on("c3", zp, yr, whole, to_c)
    mail.await_recv(("fr", 1))
    send_on(("zo", 1), zp, yo, quarter(1), to_z)
    mail.await_recv(("fl", 3))
    send_on(("zo", 3), zp, yo, quarter(3), to_z)
    send_on("c4", zp, yo, whole, to_c)
    last = []
    for q in (0, 2, 1, 3):
        for name, zs, ys in (("pr", zq, yl), ("pl", zq, yr), ("zo", zq, yo)):
            mail.await_recv((name, q))
            last.append(("c" + name, q))
            send_on(last[-1], zs, ys, quarter(q) if name == "zo" else short(q), to_c)
        if q == 1:
            for name, ys in (("tr", yr), ("tl", yl)):
                mail.await_recv(name)
                last.append("c" + name)
                send_on(last[-1], zq, ys, tail, to_c)
    own_copy.wait()
    mail.await_recv("c0", "c1", "c2", "c3", "c4", *last)
    mail.finish()


def col_gather(order, features):
    slab, width = features.shape
    hbm = pl.BlockSpec(memory_space=pltpu.HBM)
    out = pl.pallas_call(
        gather_kernel,
        out_shape=jax.ShapeDtypeStruct((2, 4, 2, slab, width), features.dtype),
        in_specs=[hbm, hbm],
        out_specs=pl.BlockSpec(memory_space=pltpu.VMEM),
        scratch_shapes=[
            pltpu.VMEM(order.shape, order.dtype),
            pltpu.VMEM((slab, width), features.dtype),
            pltpu.VMEM((slab, width), features.dtype),
            pltpu.SemaphoreType.DMA((49,)),
            pltpu.SemaphoreType.DMA((49,)),
            pltpu.SemaphoreType.DMA,
            pltpu.SemaphoreType.DMA((2,)),
        ],
        compiler_params=pltpu.CompilerParams(
            collective_id=0, has_side_effects=True, vmem_limit_bytes=16 << 20
        ),
    )(order, features)
    return out.reshape(16, slab, width)


def sum_kernel(
    part, weight, out, sib, both, z1, s2_l, s2_r, s3_l, s3_r, opp, s4b_l, s4b_r, s4a_l, s4a_r,
    c_r, c_l, z2, t_r, t_l, send_sem, recv_sem,
):
    slab = part.shape[3]
    h = slab // 2
    me = lax.axis_index("col")
    zp, y, c = me // 8, (me // 2) % 4, me % 2
    yr, yl, yo, zq, d = (y + 1) % 4, (y + 3) % 4, (y + 2) % 4, 1 - zp, 1 - c
    to_r, to_l = {"col": zp * 8 + yr * 2 + c}, {"col": zp * 8 + yl * 2 + c}
    to_z, to_c = {"col": zq * 8 + y * 2 + c}, {"col": zp * 8 + y * 2 + d}
    a, b = pl.ds(0, h), pl.ds(h, h)
    cut = tail_rows(slab)
    head, tail = pl.ds(0, slab - cut), pl.ds(slab - cut, cut)
    dests = ((zq, yo), (zq, yr), (zq, yl), (zp, yr), (zp, yl), (zp, yo), (zq, y), (zp, y))
    greet((to_r, to_l, to_z, to_c))
    mail = Mail(send_sem, recv_sem)
    quarters = [pl.ds(q * (h // 2), h // 2) for q in range(4)]
    turns = (0, 2, 1, 3)
    for q in turns:
        mail.send(("c0", q), part.at[zq, yo, d, quarters[q]], sib.at[0, quarters[q]], to_c)
    for i, (zs, ys) in enumerate(dests[1:], 1):
        mail.send(("c", i), part.at[zs, ys, d], sib.at[i], to_c)

    def join(i):
        zs, ys = dests[i]
        mail.await_recv(("c", i))
        add_rows(both.at[i], (part.at[zs, ys, c], sib.at[i]))

    for q in turns:
        rows = quarters[q]
        mail.await_recv(("c0", q))
        add_rows(both.at[0, rows], (part.at[zq, yo, c, rows], sib.at[0, rows]))
        mail.send(("z1", q), both.at[0, rows], z1.at[rows], to_z)
    join(1)
    mail.send("s2r", both.at[1, head], s2_l, to_r)
    join(2)
    mail.send("s2l", both.at[2, head], s2_r, to_l)
    mail.send("tr", both.at[1, tail], t_r, to_z)
    mail.send("tl", both.at[2, tail], t_l, to_z)
    for i in (5, 3, 4, 6, 7):
        join(i)
    for q in turns:
        rows, half = quarters[q], quarters[q % 2]
        mail.await_recv(("z1", q))
        add_rows(opp.at[rows], (both.at[5, rows], z1.at[rows]))
        if q < 2:
            mail.send(("s3r", q), opp.at[rows], s3_l.at[half], to_r)
        else:
            mail.send(("s3l", q), opp.at[rows], s3_r.at[half], to_l)
    mail.await_recv("tr", "tl")
    add_rows(both.at[3, tail], (both.at[3, tail], t_r))
    add_rows(both.at[4, tail], (both.at[4, tail], t_l))
    mail.send("s4br", both.at[3, b], s4b_l, to_r)
    mail.send("s4bl", both.at[4, a], s4b_r, to_l)
    mail.await_recv("s2r", "s2l")
    add_rows(both.at[6, head], (both.at[6, head], s2_l, s2_r))
    mail.send("z2", both.at[6], z2, to_z)
    for q in turns:
        rows, half = quarters[q], quarters[q % 2]
        if q < 2:
            mail.await_recv(("s3r", q))
            add_rows(c_r.at[half], (both.at[3, rows], s3_l.at[half]))
            mail.send(("s4ar", q), c_r.at[half], s4a_l.at[half], to_r)
        else:
            mail.await_recv(("s3l", q))
            add_rows(c_l.at[half], (both.at[4, rows], s3_r.at[half]))
            mail.send(("s4al", q), c_l.at[half], s4a_r.at[half], to_l)
    mail.await_recv("z2", "s4bl", ("s4ar", 0), ("s4ar", 1))
    dense_relu(out.at[a], (both.at[7, a], s4a_l, s4b_r, z2.at[a]), weight)
    mail.await_recv("s4br", ("s4al", 2), ("s4al", 3))
    dense_relu(out.at[b], (both.at[7, b], s4b_l, s4a_r, z2.at[b]), weight)
    mail.finish()


def col_sum(part, weight):
    _, slab, width = part.shape
    dt, h, cut = part.dtype, slab // 2, tail_rows(slab)
    vmem = pl.BlockSpec(memory_space=pltpu.VMEM)
    full, half = pltpu.VMEM((slab, width), dt), pltpu.VMEM((h, width), dt)
    return pl.pallas_call(
        sum_kernel,
        out_shape=jax.ShapeDtypeStruct((slab, width), dt),
        in_specs=[vmem, vmem],
        out_specs=vmem,
        scratch_shapes=(
            [pltpu.VMEM((8, slab, width), dt)] * 2
            + [full] + [pltpu.VMEM((slab - cut, width), dt)] * 2 + [half] * 2 + [full] + [half] * 6
            + [full] + [pltpu.VMEM((cut, width), dt)] * 2
            + [pltpu.SemaphoreType.DMA((30,))] * 2
        ),
        compiler_params=pltpu.CompilerParams(
            collective_id=2, has_side_effects=True, vmem_limit_bytes=28 << 20
        ),
    )(part.reshape(2, 4, 2, slab, width), weight)


CHUNK = 32


def product_kernel(
    transposed, unroll, source_ref, target_ref, count_ref, panel, tile_hbm, out,
    tiles, total, tile_sem,
):
    slots = tile_hbm.shape[0]
    blocks = panel.shape[0]
    chunks = slots // CHUNK
    live = count_ref[0, 0]

    def tile_copy(c):
        part = pl.ds(c * CHUNK, CHUNK)
        return pltpu.make_async_copy(tile_hbm.at[part], tiles.at[part], tile_sem.at[c])

    for c in range(chunks):
        pl.when(c * CHUNK < live)(lambda c=c: tile_copy(c).start())

    @pl.loop(0, blocks)
    def _(g):
        total[g] = jnp.zeros_like(total[g])

    dims = (((0,), (0,)), ((), ())) if transposed else (((1,), (0,)), ((), ()))

    def some_slots(first):
        products, targets = [], []
        for k in range(unroll):
            slot = first + k
            products.append(lax.dot_general(
                tiles[slot], panel[source_ref[0, slot]], dims, preferred_element_type=jnp.float32
            ))
            targets.append(jnp.where(slot < live, target_ref[0, slot], blocks))
        for k in range(unroll):
            total[targets[k]] += products[k]

    def one_chunk(c):
        tile_copy(c).wait()
        if unroll == CHUNK:
            some_slots(c * CHUNK)
        else:
            @pl.loop(0, CHUNK // unroll)
            def _(step):
                first = c * CHUNK + step * unroll
                pl.when(first < live)(lambda: some_slots(first))

    @pl.loop(0, chunks)
    def _(c):
        pl.when(c * CHUNK < live)(lambda: one_chunk(c))

    @pl.loop(0, blocks)
    def _(g):
        out[g] = total[g].astype(out.dtype)


def block_product(panel, tiles, source_ids, target_ids, count, transposed, unroll=32):
    slots, block, _ = tiles.shape
    blocks, _, width = panel.shape
    smem = pl.BlockSpec(memory_space=pltpu.SMEM)
    vmem = pl.BlockSpec(memory_space=pltpu.VMEM)
    return pl.pallas_call(
        functools.partial(product_kernel, transposed, unroll),
        out_shape=jax.ShapeDtypeStruct(panel.shape, panel.dtype),
        in_specs=[smem, smem, smem, vmem, pl.BlockSpec(memory_space=pl.ANY)],
        out_specs=vmem,
        scratch_shapes=[
            pltpu.VMEM(tiles.shape, tiles.dtype),
            pltpu.VMEM((blocks + 1, block, width), jnp.float32),
            pltpu.SemaphoreType.DMA((slots // CHUNK,)),
        ],
        compiler_params=pltpu.CompilerParams(vmem_limit_bytes=36 << 20),
        cost_estimate=pl.CostEstimate(
            flops=2 * slots * block * block * width, transcendentals=0,
            bytes_accessed=2 * (tiles.size + 2 * panel.size),
        ),
    )(source_ids, target_ids, count, panel, tiles)


def on_device(
    features, node_order, block_rows, block_cols, block_counts, adjacency, weight_one, weight_two
):
    tiles = adjacency[0, 0]
    rows, cols = block_rows[0], block_cols[0]
    block, (slab, width) = tiles.shape[-1], features.shape
    row_panel = col_gather(node_order, features)
    partial_one = block_product(
        row_panel.reshape(-1, block, width), tiles, rows, cols, block_counts, True
    )
    col_panel = row_exchange(partial_one.reshape(-1, slab, width), weight_one)
    partial_two = block_product(
        col_panel.reshape(-1, block, width), tiles, cols, rows, block_counts, False
    )
    return col_sum(partial_two.reshape(-1, slab, width), weight_two)


def solution(mesh):
    in_specs = (
        P(("row", "col"), None),
        P(("row", "col"), None),
        P("row", "col", None),
        P("row", "col", None),
        P("row", "col"),
        P("row", "col", None, None, None),
        P(),
        P(),
    )
    out_specs = P(("row", "col"), None)
    return jax.shard_map(
        on_device, mesh=mesh, in_specs=in_specs, out_specs=out_specs, check_vma=False
    )
```

```python
import functools
import jax
import jax.numpy as jnp
from jax import lax
from jax.experimental import pallas as pl
from jax.experimental.pallas import tpu as pltpu
from jax.sharding import PartitionSpec as P

MESH = pl.DeviceIdType.MESH
PARTS = 4
ORDER = (
    ("r1z", 0), ("r1o", 0), ("r1z", 2), ("r1z", 3), ("r1x", 0), ("r2", 0), ("r1o", 3), ("r1o", 2),
    ("r2", 2), ("r3", 0), ("r1z", 1), ("r1x", 2), ("r3", 2), ("r4", 0), ("r2", 3), ("r1o", 1),
    ("r1x", 3), ("r5", 0), ("r2", 1), ("r4", 2), ("r3", 3), ("d", 0), ("r5", 2), ("r1x", 1),
    ("r3", 1), ("g2", 0), ("r4", 3), ("d", 2), ("g3o", 0), ("r5", 3), ("g2", 2), ("g4", 2),
    ("r4", 1), ("g4", 0), ("g4o", 0), ("g3", 0), ("d", 3), ("g3o", 2), ("r5", 1), ("g2", 3),
    ("g3", 2), ("g4", 3), ("g5", 2), ("d", 1), ("g3o", 3), ("g5", 3), ("g3", 3), ("g2", 1),
    ("g4", 1), ("g5", 0), ("g3", 1), ("g4o", 2), ("g3o", 1), ("g5", 1), ("g4o", 3), ("g4o", 1),
)


class Mail:
    def __init__(self, send_sem, recv_sem):
        self.send_sem, self.recv_sem, self.sent = send_sem, recv_sem, {}

    def send(self, name, src, dst, device):
        slot = len(self.sent)
        copy = pltpu.make_async_remote_copy(
            src_ref=src, dst_ref=dst, send_sem=self.send_sem.at[slot],
            recv_sem=self.recv_sem.at[slot], device_id=device, device_id_type=MESH,
        )
        copy.start()
        self.sent[name] = copy

    def await_recv(self, *names):
        for name in names:
            self.sent[name].wait_recv()

    def finish(self):
        for copy in self.sent.values():
            copy.wait_send()


def greet(devices, meanwhile=None):
    barrier = pltpu.get_barrier_semaphore()
    for device in devices:
        pl.semaphore_signal(barrier, inc=1, device_id=device, device_id_type=MESH)
    if meanwhile is not None:
        meanwhile()
    pl.semaphore_wait(barrier, len(devices))


def add_rows(out, terms):
    rows = out.shape[0]
    step = next(s for s in (64, 48, 32, 16) if rows % s == 0)

    @pl.loop(0, rows // step)
    def _(i):
        at = pl.ds(pl.multiple_of(i * step, step), step)
        total = terms[0][at].astype(jnp.float32)
        for term in terms[1:]:
            total += term[at].astype(jnp.float32)
        out[at] = total.astype(out.dtype)


def dense_relu(out, terms, weight):
    total = terms[0][...].astype(jnp.float32)
    for term in terms[1:]:
        total += term[...].astype(jnp.float32)
    product = jnp.dot(total.astype(jnp.bfloat16), weight[...], preferred_element_type=jnp.float32)
    out[...] = jnp.maximum(product, 0.0).astype(out.dtype)


def row_kernel(
    part, weight, out, r1_l, r1_r, cz, r2_l, r2_r, r2o_l, r2o_r, cx_r, cx_l, r3m_l, r3m_r,
    r3b_l, r3a_r, r3a_l, r3b_r, sx, r4_l, r4_r, r5b_l, r5a_r, r5a_l, r5b_r, cs_r, cs_l, hid,
    send_sem, recv_sem, hid_sem,
):
    slab = part.shape[3]
    n = slab // PARTS
    h = n // 2
    me = lax.axis_index("row")
    z, x = me // 4, me % 4
    xr, xl, xo = (x + 1) % 4, (x + 3) % 4, (x + 2) % 4
    zr, zl, zo = (z + 1) % 4, (z + 3) % 4, (z + 2) % 4
    to_xr, to_xl = {"row": z * 4 + xr}, {"row": z * 4 + xl}
    to_zr, to_zl = {"row": zr * 4 + x}, {"row": zl * 4 + x}
    same, other = z % 2, 1 - z % 2

    def at(ref, zs, xs, rows):
        return ref.at[zs // 2, zs % 2, xs, rows]

    greet((to_xr, to_xl, to_zr, to_zl))
    mail = Mail(send_sem, recv_sem)

    def rows(p):
        return pl.ds(p * n, n), pl.ds(p * n, h), pl.ds(p * n + h, h)

    def r1z(p):
        n_, a, b = rows(p)
        mail.send(("r1r", p), at(part, zr, xo, n_), r1_l.at[p], to_zr)
        mail.send(("r1l", p), at(part, zl, xo, n_), r1_r.at[p], to_zl)

    def r1o(p):
        n_, a, b = rows(p)
        mail.send(("r2or", p), at(part, zo, xo, a), r2o_l.at[p], to_xr)
        mail.send(("r2ol", p), at(part, zo, xo, b), r2o_r.at[p], to_xl)

    def r1x(p):
        n_, a, b = rows(p)
        mail.send(("r3mr", p), part.at[:, other, xr, n_], r3m_l.at[p], to_xr)
        mail.send(("r3ml", p), part.at[:, other, xl, n_], r3m_r.at[p], to_xl)
        mail.send(("r3br", p), part.at[:, same, xr, b], r3b_l.at[p], to_xr)
        mail.send(("r3al", p), part.at[:, same, xl, a], r3a_r.at[p], to_xl)

    def r2(p):
        n_, a, b = rows(p)
        mail.await_recv(("r1r", p), ("r1l", p))
        add_rows(cz.at[p], (part.at[z // 2, same, xo, n_], r1_l.at[p], r1_r.at[p]))
        mail.send(("r2r", p), cz.at[p, pl.ds(0, h)], r2_l.at[p], to_xr)
        mail.send(("r2l", p), cz.at[p, pl.ds(h, h)], r2_r.at[p], to_xl)

    def r3(p):
        n_, a, b = rows(p)
        mail.await_recv(("r2r", p), ("r2or", p))
        add_rows(cx_r.at[p, z // 2], (part.at[z // 2, same, xr, a], r2_l.at[p]))
        add_rows(cx_r.at[p, zo // 2], (part.at[zo // 2, same, xr, a], r2o_l.at[p]))
        mail.send(("r3ar", p), cx_r.at[p], r3a_l.at[p], to_xr)
        mail.await_recv(("r2l", p), ("r2ol", p))
        add_rows(cx_l.at[p, z // 2], (part.at[z // 2, same, xl, b], r2_r.at[p]))
        add_rows(cx_l.at[p, zo // 2], (part.at[zo // 2, same, xl, b], r2o_r.at[p]))
        mail.send(("r3bl", p), cx_l.at[p], r3b_r.at[p], to_xl)

    def r4(p):
        n_, a, b = rows(p)
        first, second = pl.ds(0, h), pl.ds(h, h)
        mail.await_recv(("r3ar", p), ("r3al", p))
        for k in range(2):
            add_rows(sx.at[p, k, same, first], (part.at[k, same, x, a], r3a_l.at[p, k], r3a_r.at[p, k]))
        mail.send(("r4r", p), sx.at[p, zo // 2, same, first], r4_l.at[p], to_zr)
        mail.await_recv(("r3br", p), ("r3bl", p))
        for k in range(2):
            add_rows(sx.at[p, k, same, second], (part.at[k, same, x, b], r3b_l.at[p, k], r3b_r.at[p, k]))
        mail.send(("r4l", p), sx.at[p, zo // 2, same, second], r4_r.at[p], to_zl)
        mail.await_recv(("r3mr", p), ("r3ml", p))
        for k in range(2):
            add_rows(sx.at[p, k, other], (part.at[k, other, x, n_], r3m_l.at[p, k], r3m_r.at[p, k]))
        mail.send(("r5br", p), sx.at[p, zr // 2, other, second], r5b_l.at[p], to_zr)
        mail.send(("r5al", p), sx.at[p, zl // 2, other, first], r5a_r.at[p], to_zl)

    def r5(p):
        mail.await_recv(("r4r", p))
        add_rows(cs_r.at[p], (sx.at[p, zr // 2, other, pl.ds(0, h)], r4_l.at[p]))
        mail.send(("r5ar", p), cs_r.at[p], r5a_l.at[p], to_zr)
        mail.await_recv(("r4l", p))
        add_rows(cs_l.at[p], (sx.at[p, zl // 2, other, pl.ds(h, h)], r4_r.at[p]))
        mail.send(("r5bl", p), cs_l.at[p], r5b_r.at[p], to_zl)

    def dense(p):
        n_, a, b = rows(p)
        mine = sx.at[p, z // 2, same]
        mail.await_recv(("r5ar", p), ("r5al", p))
        dense_relu(hid.at[a], (mine.at[pl.ds(0, h)], r5a_l.at[p], r5a_r.at[p]), weight)
        mail.send(("g1ar", p), hid.at[a], at(out, z, x, a), to_zr)
        mail.send(("g3ar", p), hid.at[a], at(out, z, x, a), to_xr)
        mail.await_recv(("r5br", p), ("r5bl", p))
        dense_relu(hid.at[b], (mine.at[pl.ds(h, h)], r5b_l.at[p], r5b_r.at[p]), weight)
        mail.send(("g1bl", p), hid.at[b], at(out, z, x, b), to_zl)
        mail.send(("g3bl", p), hid.at[b], at(out, z, x, b), to_xl)
        mail.send(("g1br", p), hid.at[b], at(out, z, x, b), to_zr)
        mail.send(("g1al", p), hid.at[a], at(out, z, x, a), to_zl)
        mail.send(("g3br", p), hid.at[b], at(out, z, x, b), to_xr)
        mail.send(("g3al", p), hid.at[a], at(out, z, x, a), to_xl)
        pltpu.make_async_copy(hid.at[n_], at(out, z, x, n_), hid_sem.at[p]).start()

    def pass_on(name, p, zs, xs, rows_, to):
        mail.send((name, p), at(out, zs, xs, rows_), at(out, zs, xs, rows_), to)

    def g2(p):
        n_, a, b = rows(p)
        mail.await_recv(("g1ar", p))
        pass_on("g2r", p, zl, x, a, to_zr)
        mail.await_recv(("g1bl", p))
        pass_on("g2l", p, zr, x, b, to_zl)

    def g4(p):
        n_, a, b = rows(p)
        mail.await_recv(("g3ar", p))
        pass_on("g4r", p, z, xl, a, to_xr)
        mail.await_recv(("g3bl", p))
        pass_on("g4l", p, z, xr, b, to_xl)

    def g5(p):
        n_, a, b = rows(p)
        mail.await_recv(("g4r", p), ("g4l", p))
        pass_on("g5r", p, z, xo, n_, to_zr)
        pass_on("g5l", p, z, xo, n_, to_zl)

    def g3(p):
        n_, a, b = rows(p)
        mail.await_recv(("g1br", p), ("g1al", p))
        both = out.at[:, other, x, n_]
        mail.send(("g3mr", p), both, both, to_xr)
        mail.send(("g3ml", p), both, both, to_xl)

    def g3o(p):
        n_, a, b = rows(p)
        mail.await_recv(("g2r", p))
        pass_on("g3oar", p, zo, x, a, to_xr)
        mail.await_recv(("g2l", p))
        pass_on("g3obl", p, zo, x, b, to_xl)
        pass_on("g3obr", p, zo, x, b, to_xr)
        pass_on("g3oal", p, zo, x, a, to_xl)

    def g4o(p):
        n_, a, b = rows(p)
        mail.await_recv(("g3oar", p))
        pass_on("g4or", p, zo, xl, a, to_xr)
        mail.await_recv(("g3obl", p))
        pass_on("g4ol", p, zo, xr, b, to_xl)

    def end(p):
        n_, a, b = rows(p)
        pltpu.make_async_copy(hid.at[n_], at(out, z, x, n_), hid_sem.at[p]).wait()
        mail.await_recv(*((name, p) for name in (
            "g3br", "g3al", "g3mr", "g3ml", "g3obr", "g3oal", "g4or", "g4ol", "g5r", "g5l"
        )))

    stages = dict(
        r1z=r1z, r1o=r1o, r1x=r1x, r2=r2, r3=r3, r4=r4, r5=r5, d=dense, g2=g2, g4=g4, g5=g5, g3=g3,
        g3o=g3o, g4o=g4o,
    )
    for name, p in ORDER:
        stages[name](p)
    for p in range(PARTS):
        end(p)
    mail.finish()


def row_exchange(part, weight):
    _, slab, width = part.shape
    n = slab // PARTS
    h = n // 2
    dt = part.dtype
    vmem = pl.BlockSpec(memory_space=pltpu.VMEM)
    count = 40 * PARTS

    def buf(*lead):
        return [pltpu.VMEM((PARTS, *lead, width), dt)]

    out = pl.pallas_call(
        row_kernel,
        out_shape=jax.ShapeDtypeStruct((2, 2, 4, slab, width), dt),
        in_specs=[vmem, vmem],
        out_specs=vmem,
        scratch_shapes=(
            buf(n) * 3 + buf(h) * 4 + buf(2, h) * 2 + buf(2, n) * 2 + buf(2, h) * 4
            + buf(2, 2, n) + buf(h) * 8
            + [pltpu.VMEM((slab, width), dt)]
            + [pltpu.SemaphoreType.DMA((count,))] * 2
            + [pltpu.SemaphoreType.DMA((PARTS,))]
        ),
        compiler_params=pltpu.CompilerParams(
            collective_id=1, has_side_effects=True, vmem_limit_bytes=28 << 20
        ),
    )(part.reshape(2, 2, 4, slab, width), weight)
    return out.reshape(16, slab, width)


def tail_rows(slab):
    return max(slab // 96, 1) * 16


def gather_kernel(
    order_hbm, features_hbm, out, order, features, own, send_sem, recv_sem, own_sem, load_sem
):
    slab = features.shape[0]
    h = slab // 4
    me = lax.axis_index("col")
    zp, y, c = me // 8, (me // 2) % 4, me % 2
    yr, yl, yo, zq = (y + 1) % 4, (y + 3) % 4, (y + 2) % 4, 1 - zp
    to_r, to_l = {"col": zp * 8 + yr * 2 + c}, {"col": zp * 8 + yl * 2 + c}
    to_z, to_c = {"col": zq * 8 + y * 2 + c}, {"col": zp * 8 + y * 2 + 1 - c}

    def place(q):
        at = pl.ds(q * h, h)
        chosen = lax.broadcasted_iota(jnp.int32, (slab, h), 0) == order[:, at]
        own[at] = lax.dot_general(
            chosen.astype(features.dtype), features[...], (((0,), (0,)), ((), ())),
            preferred_element_type=jnp.float32,
        ).astype(own.dtype)

    def begin():
        loads = (
            pltpu.make_async_copy(features_hbm, features, load_sem.at[0]),
            pltpu.make_async_copy(order_hbm, order, load_sem.at[1]),
        )
        for load in loads:
            load.start()
        for load in loads:
            load.wait()
        for q in (0, 2):
            place(q)

    greet((to_r, to_l, to_z, to_c), begin)
    mail = Mail(send_sem, recv_sem)
    whole, cut = pl.ds(0, slab), tail_rows(slab)
    tail = pl.ds(slab - cut, cut)

    def send_own(name, q, to):
        rows = pl.ds(q * h, h)
        mail.send((name, q), own.at[rows], out.at[zp, y, c, rows], to)

    def send_on(name, zs, ys, rows, to):
        mail.send(name, out.at[zs, ys, c, rows], out.at[zs, ys, c, rows], to)

    def quarter(q):
        return pl.ds(q * h, h)

    def short(q):
        return pl.ds(q * h, h - cut if q == 3 else h)

    for q in (0, 2):
        send_own("r" if q == 0 else "l", q, to_r if q == 0 else to_l)
        send_own("z", q, to_z)
    for q in (1, 3):
        place(q)
        send_own("r" if q == 1 else "l", q, to_r if q == 1 else to_l)
        send_own("z", q, to_z)
    send_own("r", 2, to_r)
    send_own("l", 0, to_l)
    mail.send("c0", own, out.at[zp, y, c], to_c)
    own_copy = pltpu.make_async_copy(own, out.at[zp, y, c], own_sem)
    own_copy.start()
    mail.await_recv(("r", 0))
    send_on(("fr", 0), zp, yl, quarter(0), to_r)
    mail.await_recv(("l", 2))
    send_on(("fl", 2), zp, yr, quarter(2), to_l)
    send_own("r", 3, to_r)
    send_own("l", 1, to_l)
    mail.await_recv(("r", 1))
    send_on(("fr", 1), zp, yl, quarter(1), to_r)
    mail.await_recv(("l", 3))
    send_on(("fl", 3), zp, yr, quarter(3), to_l)
    send_on("tr", zp, yr, tail, to_z)
    for q in (0, 2):
        mail.await_recv(("z", q))
        send_on(("pr", q), zq, y, short(q), to_r)
        send_on(("pl", q), zq, y, short(q), to_l)
    mail.await_recv(("fr", 0))
    send_on(("zo", 0), zp, yo, quarter(0), to_z)
    mail.await_recv(("fl", 2))
    send_on(("zo", 2), zp, yo, quarter(2), to_z)
    for q in (1, 3):
        mail.await_recv(("z", q))
        send_on(("pr", q), zq, y, short(q), to_r)
        send_on(("pl", q), zq, y, short(q), to_l)
    send_on("c1", zq, y, whole, to_c)
    mail.await_recv(("r", 2), ("r", 3), ("l", 0), ("l", 1))
    send_on("tl", zp, yl, tail, to_z)
    send_on("c2", zp, yl, whole, to_c)
    send_on("c3", zp, yr, whole, to_c)
    mail.await_recv(("fr", 1))
    send_on(("zo", 1), zp, yo, quarter(1), to_z)
    mail.await_recv(("fl", 3))
    send_on(("zo", 3), zp, yo, quarter(3), to_z)
    send_on("c4", zp, yo, whole, to_c)
    last = []
    for q in (0, 2, 1, 3):
        for name, zs, ys in (("pr", zq, yl), ("pl", zq, yr), ("zo", zq, yo)):
            mail.await_recv((name, q))
            last.append(("c" + name, q))
            send_on(last[-1], zs, ys, quarter(q) if name == "zo" else short(q), to_c)
        if q == 1:
            for name, ys in (("tr", yr), ("tl", yl)):
                mail.await_recv(name)
                last.append("c" + name)
                send_on(last[-1], zq, ys, tail, to_c)
    own_copy.wait()
    mail.await_recv("c0", "c1", "c2", "c3", "c4", *last)
    mail.finish()


def col_gather(order, features):
    slab, width = features.shape
    hbm = pl.BlockSpec(memory_space=pltpu.HBM)
    out = pl.pallas_call(
        gather_kernel,
        out_shape=jax.ShapeDtypeStruct((2, 4, 2, slab, width), features.dtype),
        in_specs=[hbm, hbm],
        out_specs=pl.BlockSpec(memory_space=pltpu.VMEM),
        scratch_shapes=[
            pltpu.VMEM(order.shape, order.dtype),
            pltpu.VMEM((slab, width), features.dtype),
            pltpu.VMEM((slab, width), features.dtype),
            pltpu.SemaphoreType.DMA((49,)),
            pltpu.SemaphoreType.DMA((49,)),
            pltpu.SemaphoreType.DMA,
            pltpu.SemaphoreType.DMA((2,)),
        ],
        compiler_params=pltpu.CompilerParams(
            collective_id=0, has_side_effects=True, vmem_limit_bytes=16 << 20
        ),
    )(order, features)
    return out.reshape(16, slab, width)


def sum_kernel(
    part, weight, out, sib, both, z1, s2_l, s2_r, s3_l, s3_r, opp, s4b_l, s4b_r, s4a_l, s4a_r,
    c_r, c_l, z2, t_r, t_l, send_sem, recv_sem,
):
    slab = part.shape[3]
    h = slab // 2
    me = lax.axis_index("col")
    zp, y, c = me // 8, (me // 2) % 4, me % 2
    yr, yl, yo, zq, d = (y + 1) % 4, (y + 3) % 4, (y + 2) % 4, 1 - zp, 1 - c
    to_r, to_l = {"col": zp * 8 + yr * 2 + c}, {"col": zp * 8 + yl * 2 + c}
    to_z, to_c = {"col": zq * 8 + y * 2 + c}, {"col": zp * 8 + y * 2 + d}
    a, b = pl.ds(0, h), pl.ds(h, h)
    cut = tail_rows(slab)
    head, tail = pl.ds(0, slab - cut), pl.ds(slab - cut, cut)
    dests = ((zq, yo), (zq, yr), (zq, yl), (zp, yr), (zp, yl), (zp, yo), (zq, y), (zp, y))
    greet((to_r, to_l, to_z, to_c))
    mail = Mail(send_sem, recv_sem)
    quarters = [pl.ds(q * (h // 2), h // 2) for q in range(4)]
    turns = (0, 2, 1, 3)
    for q in turns:
        mail.send(("c0", q), part.at[zq, yo, d, quarters[q]], sib.at[0, quarters[q]], to_c)
    for i, (zs, ys) in enumerate(dests[1:], 1):
        mail.send(("c", i), part.at[zs, ys, d], sib.at[i], to_c)

    def join(i):
        zs, ys = dests[i]
        mail.await_recv(("c", i))
        add_rows(both.at[i], (part.at[zs, ys, c], sib.at[i]))

    for q in turns:
        rows = quarters[q]
        mail.await_recv(("c0", q))
        add_rows(both.at[0, rows], (part.at[zq, yo, c, rows], sib.at[0, rows]))
        mail.send(("z1", q), both.at[0, rows], z1.at[rows], to_z)
    join(1)
    mail.send("s2r", both.at[1, head], s2_l, to_r)
    join(2)
    mail.send("s2l", both.at[2, head], s2_r, to_l)
    mail.send("tr", both.at[1, tail], t_r, to_z)
    mail.send("tl", both.at[2, tail], t_l, to_z)
    for i in (5, 3, 4, 6, 7):
        join(i)
    for q in turns:
        rows, half = quarters[q], quarters[q % 2]
        mail.await_recv(("z1", q))
        add_rows(opp.at[rows], (both.at[5, rows], z1.at[rows]))
        if q < 2:
            mail.send(("s3r", q), opp.at[rows], s3_l.at[half], to_r)
        else:
            mail.send(("s3l", q), opp.at[rows], s3_r.at[half], to_l)
    mail.await_recv("tr", "tl")
    add_rows(both.at[3, tail], (both.at[3, tail], t_r))
    add_rows(both.at[4, tail], (both.at[4, tail], t_l))
    mail.send("s4br", both.at[3, b], s4b_l, to_r)
    mail.send("s4bl", both.at[4, a], s4b_r, to_l)
    mail.await_recv("s2r", "s2l")
    add_rows(both.at[6, head], (both.at[6, head], s2_l, s2_r))
    mail.send("z2", both.at[6], z2, to_z)
    for q in turns:
        rows, half = quarters[q], quarters[q % 2]
        if q < 2:
            mail.await_recv(("s3r", q))
            add_rows(c_r.at[half], (both.at[3, rows], s3_l.at[half]))
            mail.send(("s4ar", q), c_r.at[half], s4a_l.at[half], to_r)
        else:
            mail.await_recv(("s3l", q))
            add_rows(c_l.at[half], (both.at[4, rows], s3_r.at[half]))
            mail.send(("s4al", q), c_l.at[half], s4a_r.at[half], to_l)
    mail.await_recv("z2", "s4bl", ("s4ar", 0), ("s4ar", 1))
    dense_relu(out.at[a], (both.at[7, a], s4a_l, s4b_r, z2.at[a]), weight)
    mail.await_recv("s4br", ("s4al", 2), ("s4al", 3))
    dense_relu(out.at[b], (both.at[7, b], s4b_l, s4a_r, z2.at[b]), weight)
    mail.finish()


def col_sum(part, weight):
    _, slab, width = part.shape
    dt, h, cut = part.dtype, slab // 2, tail_rows(slab)
    vmem = pl.BlockSpec(memory_space=pltpu.VMEM)
    full, half = pltpu.VMEM((slab, width), dt), pltpu.VMEM((h, width), dt)
    return pl.pallas_call(
        sum_kernel,
        out_shape=jax.ShapeDtypeStruct((slab, width), dt),
        in_specs=[vmem, vmem],
        out_specs=vmem,
        scratch_shapes=(
            [pltpu.VMEM((8, slab, width), dt)] * 2
            + [full] + [pltpu.VMEM((slab - cut, width), dt)] * 2 + [half] * 2 + [full] + [half] * 6
            + [full] + [pltpu.VMEM((cut, width), dt)] * 2
            + [pltpu.SemaphoreType.DMA((30,))] * 2
        ),
        compiler_params=pltpu.CompilerParams(
            collective_id=2, has_side_effects=True, vmem_limit_bytes=28 << 20
        ),
    )(part.reshape(2, 4, 2, slab, width), weight)


CHUNK = 32


def product_kernel(
    transposed, unroll, source_ref, target_ref, count_ref, panel, tile_hbm, out,
    tiles, total, tile_sem,
):
    slots = tile_hbm.shape[0]
    blocks = panel.shape[0]
    chunks = slots // CHUNK
    live = count_ref[0, 0]

    def tile_copy(c):
        part = pl.ds(c * CHUNK, CHUNK)
        return pltpu.make_async_copy(tile_hbm.at[part], tiles.at[part], tile_sem.at[c])

    for c in range(chunks):
        pl.when(c * CHUNK < live)(lambda c=c: tile_copy(c).start())

    @pl.loop(0, blocks)
    def _(g):
        total[g] = jnp.zeros_like(total[g])

    dims = (((0,), (0,)), ((), ())) if transposed else (((1,), (0,)), ((), ()))

    def some_slots(first):
        products, targets = [], []
        for k in range(unroll):
            slot = first + k
            products.append(lax.dot_general(
                tiles[slot], panel[source_ref[0, slot]], dims, preferred_element_type=jnp.float32
            ))
            targets.append(jnp.where(slot < live, target_ref[0, slot], blocks))
        for k in range(unroll):
            total[targets[k]] += products[k]

    def one_chunk(c):
        tile_copy(c).wait()
        if unroll == CHUNK:
            some_slots(c * CHUNK)
        else:
            @pl.loop(0, CHUNK // unroll)
            def _(step):
                first = c * CHUNK + step * unroll
                pl.when(first < live)(lambda: some_slots(first))

    @pl.loop(0, chunks)
    def _(c):
        pl.when(c * CHUNK < live)(lambda: one_chunk(c))

    @pl.loop(0, blocks)
    def _(g):
        out[g] = total[g].astype(out.dtype)


def block_product(panel, tiles, source_ids, target_ids, count, transposed, unroll=32):
    slots, block, _ = tiles.shape
    blocks, _, width = panel.shape
    smem = pl.BlockSpec(memory_space=pltpu.SMEM)
    vmem = pl.BlockSpec(memory_space=pltpu.VMEM)
    return pl.pallas_call(
        functools.partial(product_kernel, transposed, unroll),
        out_shape=jax.ShapeDtypeStruct(panel.shape, panel.dtype),
        in_specs=[smem, smem, smem, vmem, pl.BlockSpec(memory_space=pl.ANY)],
        out_specs=vmem,
        scratch_shapes=[
            pltpu.VMEM(tiles.shape, tiles.dtype),
            pltpu.VMEM((blocks + 1, block, width), jnp.float32),
            pltpu.SemaphoreType.DMA((slots // CHUNK,)),
        ],
        compiler_params=pltpu.CompilerParams(vmem_limit_bytes=36 << 20),
        cost_estimate=pl.CostEstimate(
            flops=2 * slots * block * block * width, transcendentals=0,
            bytes_accessed=2 * (tiles.size + 2 * panel.size),
        ),
    )(source_ids, target_ids, count, panel, tiles)


def on_device(
    features, node_order, block_rows, block_cols, block_counts, adjacency, weight_one, weight_two
):
    tiles = adjacency[0, 0]
    rows, cols = block_rows[0], block_cols[0]
    block, (slab, width) = tiles.shape[-1], features.shape
    row_panel = col_gather(node_order, features)
    partial_one = block_product(
        row_panel.reshape(-1, block, width), tiles, rows, cols, block_counts, True
    )
    col_panel = row_exchange(partial_one.reshape(-1, slab, width), weight_one)
    partial_two = block_product(
        col_panel.reshape(-1, block, width), tiles, cols, rows, block_counts, False
    )
    return col_sum(partial_two.reshape(-1, slab, width), weight_two)


def solution(mesh):
    in_specs = (
        P(("row", "col"), None),
        P(("row", "col"), None),
        P("row", "col", None),
        P("row", "col", None),
        P("row", "col"),
        P("row", "col", None, None, None),
        P(),
        P(),
    )
    out_specs = P(("row", "col"), None)
    return jax.shard_map(
        on_device, mesh=mesh, in_specs=in_specs, out_specs=out_specs, check_vma=False
    )
```

```python
import functools
import jax
import jax.numpy as jnp
from jax import lax
from jax.experimental import pallas as pl
from jax.experimental.pallas import tpu as pltpu
from jax.sharding import PartitionSpec as P

MESH = pl.DeviceIdType.MESH
PARTS = 4
ORDER = (
    ("r1z", 0), ("r1o", 0), ("r1z", 2), ("r1z", 3), ("r1x", 0), ("r2", 0), ("r1o", 3), ("r1o", 2),
    ("r2", 2), ("r3", 0), ("r1z", 1), ("r1x", 2), ("r3", 2), ("r4", 0), ("r2", 3), ("r1o", 1),
    ("r1x", 3), ("r5", 0), ("r2", 1), ("r4", 2), ("r3", 3), ("d", 0), ("r5", 2), ("r1x", 1),
    ("r3", 1), ("g2", 0), ("r4", 3), ("d", 2), ("g3o", 0), ("r5", 3), ("g2", 2), ("g4", 2),
    ("r4", 1), ("g4", 0), ("g4o", 0), ("g3", 0), ("d", 3), ("g3o", 2), ("r5", 1), ("g2", 3),
    ("g3", 2), ("g4", 3), ("g5", 2), ("d", 1), ("g3o", 3), ("g5", 3), ("g3", 3), ("g2", 1),
    ("g4", 1), ("g5", 0), ("g3", 1), ("g4o", 2), ("g3o", 1), ("g5", 1), ("g4o", 3), ("g4o", 1),
)


class Mail:
    def __init__(self, send_sem, recv_sem):
        self.send_sem, self.recv_sem, self.sent = send_sem, recv_sem, {}

    def send(self, name, src, dst, device):
        slot = len(self.sent)
        copy = pltpu.make_async_remote_copy(
            src_ref=src, dst_ref=dst, send_sem=self.send_sem.at[slot],
            recv_sem=self.recv_sem.at[slot], device_id=device, device_id_type=MESH,
        )
        copy.start()
        self.sent[name] = copy

    def await_recv(self, *names):
        for name in names:
            self.sent[name].wait_recv()

    def finish(self):
        for copy in self.sent.values():
            copy.wait_send()


def greet(devices, meanwhile=None):
    barrier = pltpu.get_barrier_semaphore()
    for device in devices:
        pl.semaphore_signal(barrier, inc=1, device_id=device, device_id_type=MESH)
    if meanwhile is not None:
        meanwhile()
    pl.semaphore_wait(barrier, len(devices))


def add_rows(out, terms):
    rows = out.shape[0]
    step = next(s for s in (64, 48, 32, 16) if rows % s == 0)

    @pl.loop(0, rows // step)
    def _(i):
        at = pl.ds(pl.multiple_of(i * step, step), step)
        total = terms[0][at].astype(jnp.float32)
        for term in terms[1:]:
            total += term[at].astype(jnp.float32)
        out[at] = total.astype(out.dtype)


def round_slab(out, total, slab):
    block = total.shape[1]
    count = out.shape[0] // block

    @pl.loop(0, count)
    def _(j):
        at = pl.ds(pl.multiple_of(j * block, block), block)
        out[at] = total[slab * count + j].astype(out.dtype)


def dense_relu(out, terms, weight):
    total = terms[0][...].astype(jnp.float32)
    for term in terms[1:]:
        total += term[...].astype(jnp.float32)
    product = jnp.dot(total.astype(jnp.bfloat16), weight[...], preferred_element_type=jnp.float32)
    out[...] = jnp.maximum(product, 0.0).astype(out.dtype)


def row_kernel(
    total, weight, out, part, r1_l, r1_r, cz, r2_l, r2_r, r2o_l, r2o_r, cx_r, cx_l, r3m_l, r3m_r,
    r3b_l, r3a_r, r3a_l, r3b_r, sx, r4_l, r4_r, r5b_l, r5a_r, r5a_l, r5b_r, cs_r, cs_l, hid,
    send_sem, recv_sem, hid_sem,
):
    slab = part.shape[3]
    n = slab // PARTS
    h = n // 2
    me = lax.axis_index("row")
    z, x = me // 4, me % 4
    xr, xl, xo = (x + 1) % 4, (x + 3) % 4, (x + 2) % 4
    zr, zl, zo = (z + 1) % 4, (z + 3) % 4, (z + 2) % 4
    to_xr, to_xl = {"row": z * 4 + xr}, {"row": z * 4 + xl}
    to_zr, to_zl = {"row": zr * 4 + x}, {"row": zl * 4 + x}
    same, other = z % 2, 1 - z % 2

    def at(ref, zs, xs, rows):
        return ref.at[zs // 2, zs % 2, xs, rows]


    def round_x(*xs):
        for zs in (zr, zl, zo, z):
            for x_ in xs:
                round_slab(part.at[zs // 2, zs % 2, x_], total, zs * 4 + x_)

    greet((to_xr, to_xl, to_zr, to_zl), lambda: round_x(xo))
    mail = Mail(send_sem, recv_sem)

    def rows(p):
        return pl.ds(p * n, n), pl.ds(p * n, h), pl.ds(p * n + h, h)

    def r1z(p):
        n_, a, b = rows(p)
        mail.send(("r1r", p), at(part, zr, xo, n_), r1_l.at[p], to_zr)
        mail.send(("r1l", p), at(part, zl, xo, n_), r1_r.at[p], to_zl)

    def r1o(p):
        n_, a, b = rows(p)
        mail.send(("r2or", p), at(part, zo, xo, a), r2o_l.at[p], to_xr)
        mail.send(("r2ol", p), at(part, zo, xo, b), r2o_r.at[p], to_xl)

    def r1x(p):
        n_, a, b = rows(p)
        mail.send(("r3mr", p), part.at[:, other, xr, n_], r3m_l.at[p], to_xr)
        mail.send(("r3ml", p), part.at[:, other, xl, n_], r3m_r.at[p], to_xl)
        mail.send(("r3br", p), part.at[:, same, xr, b], r3b_l.at[p], to_xr)
        mail.send(("r3al", p), part.at[:, same, xl, a], r3a_r.at[p], to_xl)

    def r2(p):
        n_, a, b = rows(p)
        mail.await_recv(("r1r", p), ("r1l", p))
        add_rows(cz.at[p], (part.at[z // 2, same, xo, n_], r1_l.at[p], r1_r.at[p]))
        mail.send(("r2r", p), cz.at[p, pl.ds(0, h)], r2_l.at[p], to_xr)
        mail.send(("r2l", p), cz.at[p, pl.ds(h, h)], r2_r.at[p], to_xl)

    def r3(p):
        n_, a, b = rows(p)
        mail.await_recv(("r2r", p), ("r2or", p))
        add_rows(cx_r.at[p, z // 2], (part.at[z // 2, same, xr, a], r2_l.at[p]))
        add_rows(cx_r.at[p, zo // 2], (part.at[zo // 2, same, xr, a], r2o_l.at[p]))
        mail.send(("r3ar", p), cx_r.at[p], r3a_l.at[p], to_xr)
        mail.await_recv(("r2l", p), ("r2ol", p))
        add_rows(cx_l.at[p, z // 2], (part.at[z // 2, same, xl, b], r2_r.at[p]))
        add_rows(cx_l.at[p, zo // 2], (part.at[zo // 2, same, xl, b], r2o_r.at[p]))
        mail.send(("r3bl", p), cx_l.at[p], r3b_r.at[p], to_xl)

    def r4(p):
        n_, a, b = rows(p)
        first, second = pl.ds(0, h), pl.ds(h, h)
        mail.await_recv(("r3ar", p), ("r3al", p))
        for k in range(2):
            add_rows(sx.at[p, k, same, first], (part.at[k, same, x, a], r3a_l.at[p, k], r3a_r.at[p, k]))
        mail.send(("r4r", p), sx.at[p, zo // 2, same, first], r4_l.at[p], to_zr)
        mail.await_recv(("r3br", p), ("r3bl", p))
        for k in range(2):
            add_rows(sx.at[p, k, same, second], (part.at[k, same, x, b], r3b_l.at[p, k], r3b_r.at[p, k]))
        mail.send(("r4l", p), sx.at[p, zo // 2, same, second], r4_r.at[p], to_zl)
        mail.await_recv(("r3mr", p), ("r3ml", p))
        for k in range(2):
            add_rows(sx.at[p, k, other], (part.at[k, other, x, n_], r3m_l.at[p, k], r3m_r.at[p, k]))
        mail.send(("r5br", p), sx.at[p, zr // 2, other, second], r5b_l.at[p], to_zr)
        mail.send(("r5al", p), sx.at[p, zl // 2, other, first], r5a_r.at[p], to_zl)

    def r5(p):
        mail.await_recv(("r4r", p))
        add_rows(cs_r.at[p], (sx.at[p, zr // 2, other, pl.ds(0, h)], r4_l.at[p]))
        mail.send(("r5ar", p), cs_r.at[p], r5a_l.at[p], to_zr)
        mail.await_recv(("r4l", p))
        add_rows(cs_l.at[p], (sx.at[p, zl // 2, other, pl.ds(h, h)], r4_r.at[p]))
        mail.send(("r5bl", p), cs_l.at[p], r5b_r.at[p], to_zl)

    def dense(p):
        n_, a, b = rows(p)
        mine = sx.at[p, z // 2, same]
        mail.await_recv(("r5ar", p), ("r5al", p))
        dense_relu(hid.at[a], (mine.at[pl.ds(0, h)], r5a_l.at[p], r5a_r.at[p]), weight)
        mail.send(("g1ar", p), hid.at[a], at(out, z, x, a), to_zr)
        mail.send(("g3ar", p), hid.at[a], at(out, z, x, a), to_xr)
        mail.await_recv(("r5br", p), ("r5bl", p))
        dense_relu(hid.at[b], (mine.at[pl.ds(h, h)], r5b_l.at[p], r5b_r.at[p]), weight)
        mail.send(("g1bl", p), hid.at[b], at(out, z, x, b), to_zl)
        mail.send(("g3bl", p), hid.at[b], at(out, z, x, b), to_xl)
        mail.send(("g1br", p), hid.at[b], at(out, z, x, b), to_zr)
        mail.send(("g1al", p), hid.at[a], at(out, z, x, a), to_zl)
        mail.send(("g3br", p), hid.at[b], at(out, z, x, b), to_xr)
        mail.send(("g3al", p), hid.at[a], at(out, z, x, a), to_xl)
        pltpu.make_async_copy(hid.at[n_], at(out, z, x, n_), hid_sem.at[p]).start()

    def pass_on(name, p, zs, xs, rows_, to):
        mail.send((name, p), at(out, zs, xs, rows_), at(out, zs, xs, rows_), to)

    def g2(p):
        n_, a, b = rows(p)
        mail.await_recv(("g1ar", p))
        pass_on("g2r", p, zl, x, a, to_zr)
        mail.await_recv(("g1bl", p))
        pass_on("g2l", p, zr, x, b, to_zl)

    def g4(p):
        n_, a, b = rows(p)
        mail.await_recv(("g3ar", p))
        pass_on("g4r", p, z, xl, a, to_xr)
        mail.await_recv(("g3bl", p))
        pass_on("g4l", p, z, xr, b, to_xl)

    def g5(p):
        n_, a, b = rows(p)
        mail.await_recv(("g4r", p), ("g4l", p))
        pass_on("g5r", p, z, xo, n_, to_zr)
        pass_on("g5l", p, z, xo, n_, to_zl)

    def g3(p):
        n_, a, b = rows(p)
        mail.await_recv(("g1br", p), ("g1al", p))
        both = out.at[:, other, x, n_]
        mail.send(("g3mr", p), both, both, to_xr)
        mail.send(("g3ml", p), both, both, to_xl)

    def g3o(p):
        n_, a, b = rows(p)
        mail.await_recv(("g2r", p))
        pass_on("g3oar", p, zo, x, a, to_xr)
        mail.await_recv(("g2l", p))
        pass_on("g3obl", p, zo, x, b, to_xl)
        pass_on("g3obr", p, zo, x, b, to_xr)
        pass_on("g3oal", p, zo, x, a, to_xl)

    def g4o(p):
        n_, a, b = rows(p)
        mail.await_recv(("g3oar", p))
        pass_on("g4or", p, zo, xl, a, to_xr)
        mail.await_recv(("g3obl", p))
        pass_on("g4ol", p, zo, xr, b, to_xl)

    def end(p):
        n_, a, b = rows(p)
        pltpu.make_async_copy(hid.at[n_], at(out, z, x, n_), hid_sem.at[p]).wait()
        mail.await_recv(*((name, p) for name in (
            "g3br", "g3al", "g3mr", "g3ml", "g3obr", "g3oal", "g4or", "g4ol", "g5r", "g5l"
        )))

    stages = dict(
        r1z=r1z, r1o=r1o, r1x=r1x, r2=r2, r3=r3, r4=r4, r5=r5, d=dense, g2=g2, g4=g4, g5=g5, g3=g3,
        g3o=g3o, g4o=g4o,
    )
    first_x = next(i for i, (name, _) in enumerate(ORDER) if name == "r1x")
    for i, (name, p) in enumerate(ORDER):
        if i == first_x:
            round_x(xr, xl)
        stages[name](p)
        if i == first_x:
            round_x(x)
    for p in range(PARTS):
        end(p)
    mail.finish()


def row_exchange(total, weight, slab):
    width = total.shape[2]
    n = slab // PARTS
    h = n // 2
    dt = weight.dtype
    vmem = pl.BlockSpec(memory_space=pltpu.VMEM)
    count = 40 * PARTS

    def buf(*lead):
        return [pltpu.VMEM((PARTS, *lead, width), dt)]

    out = pl.pallas_call(
        row_kernel,
        out_shape=jax.ShapeDtypeStruct((2, 2, 4, slab, width), dt),
        in_specs=[vmem, vmem],
        out_specs=vmem,
        scratch_shapes=(
            [pltpu.VMEM((2, 2, 4, slab, width), dt)]
            + buf(n) * 3 + buf(h) * 4 + buf(2, h) * 2 + buf(2, n) * 2 + buf(2, h) * 4
            + buf(2, 2, n) + buf(h) * 8
            + [pltpu.VMEM((slab, width), dt)]
            + [pltpu.SemaphoreType.DMA((count,))] * 2
            + [pltpu.SemaphoreType.DMA((PARTS,))]
        ),
        compiler_params=pltpu.CompilerParams(
            collective_id=1, has_side_effects=True, vmem_limit_bytes=20 << 20
        ),
    )(total, weight)
    return out.reshape(16, slab, width)


def tail_rows(slab):
    return max(slab // 96, 1) * 16


def gather_kernel(order, features, out, own, send_sem, recv_sem, own_sem):
    slab = features.shape[0]
    h = slab // 4
    me = lax.axis_index("col")
    zp, y, c = me // 8, (me // 2) % 4, me % 2
    yr, yl, yo, zq = (y + 1) % 4, (y + 3) % 4, (y + 2) % 4, 1 - zp
    to_r, to_l = {"col": zp * 8 + yr * 2 + c}, {"col": zp * 8 + yl * 2 + c}
    to_z, to_c = {"col": zq * 8 + y * 2 + c}, {"col": zp * 8 + y * 2 + 1 - c}

    def place(q):
        at = pl.ds(q * h, h)
        chosen = lax.broadcasted_iota(jnp.int32, (slab, h), 0) == order[:, at]
        own[at] = lax.dot_general(
            chosen.astype(features.dtype), features[...], (((0,), (0,)), ((), ())),
            preferred_element_type=jnp.float32,
        ).astype(own.dtype)

    def begin():
        for q in (0, 2):
            place(q)

    greet((to_r, to_l, to_z, to_c), begin)
    mail = Mail(send_sem, recv_sem)
    whole, cut = pl.ds(0, slab), tail_rows(slab)
    tail = pl.ds(slab - cut, cut)

    def send_own(name, q, to):
        rows = pl.ds(q * h, h)
        mail.send((name, q), own.at[rows], out.at[zp, y, c, rows], to)

    def send_on(name, zs, ys, rows, to):
        mail.send(name, out.at[zs, ys, c, rows], out.at[zs, ys, c, rows], to)

    def quarter(q):
        return pl.ds(q * h, h)

    def short(q):
        return pl.ds(q * h, h - cut if q == 3 else h)

    for q in (0, 2):
        send_own("r" if q == 0 else "l", q, to_r if q == 0 else to_l)
        send_own("z", q, to_z)
    for q in (1, 3):
        place(q)
        send_own("r" if q == 1 else "l", q, to_r if q == 1 else to_l)
        send_own("z", q, to_z)
    send_own("r", 2, to_r)
    send_own("l", 0, to_l)
    mail.send("c0", own, out.at[zp, y, c], to_c)
    own_copy = pltpu.make_async_copy(own, out.at[zp, y, c], own_sem)
    own_copy.start()
    mail.await_recv(("r", 0))
    send_on(("fr", 0), zp, yl, quarter(0), to_r)
    mail.await_recv(("l", 2))
    send_on(("fl", 2), zp, yr, quarter(2), to_l)
    send_own("r", 3, to_r)
    send_own("l", 1, to_l)
    mail.await_recv(("r", 1))
    send_on(("fr", 1), zp, yl, quarter(1), to_r)
    mail.await_recv(("l", 3))
    send_on(("fl", 3), zp, yr, quarter(3), to_l)
    send_on("tr", zp, yr, tail, to_z)
    for q in (0, 2):
        mail.await_recv(("z", q))
        send_on(("pr", q), zq, y, short(q), to_r)
        send_on(("pl", q), zq, y, short(q), to_l)
    mail.await_recv(("fr", 0))
    send_on(("zo", 0), zp, yo, quarter(0), to_z)
    mail.await_recv(("fl", 2))
    send_on(("zo", 2), zp, yo, quarter(2), to_z)
    for q in (1, 3):
        mail.await_recv(("z", q))
        send_on(("pr", q), zq, y, short(q), to_r)
        send_on(("pl", q), zq, y, short(q), to_l)
    send_on("c1", zq, y, whole, to_c)
    mail.await_recv(("r", 2), ("r", 3), ("l", 0), ("l", 1))
    send_on("tl", zp, yl, tail, to_z)
    send_on("c2", zp, yl, whole, to_c)
    send_on("c3", zp, yr, whole, to_c)
    mail.await_recv(("fr", 1))
    send_on(("zo", 1), zp, yo, quarter(1), to_z)
    mail.await_recv(("fl", 3))
    send_on(("zo", 3), zp, yo, quarter(3), to_z)
    send_on("c4", zp, yo, whole, to_c)
    last = []
    for q in (0, 2, 1, 3):
        for name, zs, ys in (("pr", zq, yl), ("pl", zq, yr), ("zo", zq, yo)):
            mail.await_recv((name, q))
            last.append(("c" + name, q))
            send_on(last[-1], zs, ys, quarter(q) if name == "zo" else short(q), to_c)
        if q == 1:
            for name, ys in (("tr", yr), ("tl", yl)):
                mail.await_recv(name)
                last.append("c" + name)
                send_on(last[-1], zq, ys, tail, to_c)
    own_copy.wait()
    mail.await_recv("c0", "c1", "c2", "c3", "c4", *last)
    mail.finish()


def col_gather(order, features):
    slab, width = features.shape
    vmem = pl.BlockSpec(memory_space=pltpu.VMEM)
    out = pl.pallas_call(
        gather_kernel,
        out_shape=jax.ShapeDtypeStruct((2, 4, 2, slab, width), features.dtype),
        in_specs=[vmem, vmem],
        out_specs=vmem,
        scratch_shapes=[
            pltpu.VMEM((slab, width), features.dtype),
            pltpu.SemaphoreType.DMA((49,)),
            pltpu.SemaphoreType.DMA((49,)),
            pltpu.SemaphoreType.DMA,
        ],
        compiler_params=pltpu.CompilerParams(
            collective_id=0, has_side_effects=True, vmem_limit_bytes=12 << 20
        ),
    )(order, features)
    return out.reshape(16, slab, width)


def sum_kernel(
    total, weight, out, mine, sib, both, z1, s2_l, s2_r, s3_l, s3_r, opp, s4b_l, s4b_r, s4a_l, s4a_r,
    c_r, c_l, z2, t_r, t_l, send_sem, recv_sem,
):
    slab = out.shape[0]
    h = slab // 2
    block = total.shape[1]
    count = slab // block
    me = lax.axis_index("col")
    zp, y, c = me // 8, (me // 2) % 4, me % 2
    yr, yl, yo, zq, d = (y + 1) % 4, (y + 3) % 4, (y + 2) % 4, 1 - zp, 1 - c
    to_r, to_l = {"col": zp * 8 + yr * 2 + c}, {"col": zp * 8 + yl * 2 + c}
    to_z, to_c = {"col": zq * 8 + y * 2 + c}, {"col": zp * 8 + y * 2 + d}
    a, b = pl.ds(0, h), pl.ds(h, h)
    cut = tail_rows(slab)
    head, tail = pl.ds(0, slab - cut), pl.ds(slab - cut, cut)
    dests = ((zq, yo), (zq, yr), (zq, yl), (zp, yr), (zp, yl), (zp, yo), (zq, y), (zp, y))
    greet((to_r, to_l, to_z, to_c))
    mail = Mail(send_sem, recv_sem)
    quarters = [pl.ds(q * (h // 2), h // 2) for q in range(4)]
    turns = (0, 2, 1, 3)

    def slab_of(i, core):
        zs, ys = dests[i]
        return (zs * 4 + ys) * 2 + core

    def give(i):
        round_slab(mine.at[i], total, slab_of(i, d))
        if i > 0:
            mail.send(("c", i), mine.at[i], sib.at[i], to_c)

    def join(i):
        if i > 0:
            mail.await_recv(("c", i))

        @pl.loop(0, count)
        def _(j):
            at = pl.ds(pl.multiple_of(j * block, block), block)
            both[i, at] = (
                total[slab_of(i, c) * count + j] + sib[i, at].astype(jnp.float32)
            ).astype(both.dtype)

    give(0)
    for q in turns:
        mail.send(("c0", q), mine.at[0, quarters[q]], sib.at[0, quarters[q]], to_c)
    for i in (1, 2):
        give(i)
    mail.await_recv(*(("c0", q) for q in turns))
    join(0)
    for q in turns:
        mail.send(("z1", q), both.at[0, quarters[q]], z1.at[quarters[q]], to_z)
    for i in (5, 3, 4, 6, 7):
        give(i)
    join(1)
    mail.send("s2r", both.at[1, head], s2_l, to_r)
    join(2)
    mail.send("s2l", both.at[2, head], s2_r, to_l)
    mail.send("tr", both.at[1, tail], t_r, to_z)
    mail.send("tl", both.at[2, tail], t_l, to_z)
    for i in (5, 3, 4, 6, 7):
        join(i)
    for q in turns:
        rows, half = quarters[q], quarters[q % 2]
        mail.await_recv(("z1", q))
        add_rows(opp.at[rows], (both.at[5, rows], z1.at[rows]))
        if q < 2:
            mail.send(("s3r", q), opp.at[rows], s3_l.at[half], to_r)
        else:
            mail.send(("s3l", q), opp.at[rows], s3_r.at[half], to_l)
    mail.await_recv("tr", "tl")
    add_rows(both.at[3, tail], (both.at[3, tail], t_r))
    add_rows(both.at[4, tail], (both.at[4, tail], t_l))
    mail.send("s4br", both.at[3, b], s4b_l, to_r)
    mail.send("s4bl", both.at[4, a], s4b_r, to_l)
    mail.await_recv("s2r", "s2l")
    add_rows(both.at[6, head], (both.at[6, head], s2_l, s2_r))
    mail.send("z2", both.at[6], z2, to_z)
    for q in turns:
        rows, half = quarters[q], quarters[q % 2]
        if q < 2:
            mail.await_recv(("s3r", q))
            add_rows(c_r.at[half], (both.at[3, rows], s3_l.at[half]))
            mail.send(("s4ar", q), c_r.at[half], s4a_l.at[half], to_r)
        else:
            mail.await_recv(("s3l", q))
            add_rows(c_l.at[half], (both.at[4, rows], s3_r.at[half]))
            mail.send(("s4al", q), c_l.at[half], s4a_r.at[half], to_l)
    mail.await_recv("s4bl", "s4br", "z2")
    for q in turns:
        rows, half = quarters[q], quarters[q % 2]
        mail.await_recv(("s4ar" if q < 2 else "s4al", q))
        near = (s4a_l, s4b_r) if q < 2 else (s4a_r, s4b_l)
        dense_relu(
            out.at[rows], (both.at[7, rows], near[0].at[half], near[1].at[half], z2.at[rows]), weight
        )
    mail.finish()


def col_sum(total, weight, slab):
    width = total.shape[2]
    dt, h, cut = weight.dtype, slab // 2, tail_rows(slab)
    vmem = pl.BlockSpec(memory_space=pltpu.VMEM)
    full, half = pltpu.VMEM((slab, width), dt), pltpu.VMEM((h, width), dt)
    return pl.pallas_call(
        sum_kernel,
        out_shape=jax.ShapeDtypeStruct((slab, width), dt),
        in_specs=[vmem, vmem],
        out_specs=vmem,
        scratch_shapes=(
            [pltpu.VMEM((8, slab, width), dt)] * 3
            + [full] + [pltpu.VMEM((slab - cut, width), dt)] * 2 + [half] * 2 + [full] + [half] * 6
            + [full] + [pltpu.VMEM((cut, width), dt)] * 2
            + [pltpu.SemaphoreType.DMA((30,))] * 2
        ),
        compiler_params=pltpu.CompilerParams(
            collective_id=2, has_side_effects=True, vmem_limit_bytes=20 << 20
        ),
    )(total, weight)


STEP = 32


def product_kernel(
    transposed, source_ref, target_ref, count_ref, panel, tiles, total
):
    slots = tiles.shape[0]
    blocks = panel.shape[0]
    live = count_ref[0, 0]

    @pl.loop(0, blocks)
    def _(g):
        total[g] = jnp.zeros_like(total[g])

    dims = (((0,), (0,)), ((), ())) if transposed else (((1,), (0,)), ((), ()))

    @pl.loop(0, slots // STEP)
    def _(step):
        first = step * STEP

        @pl.when(first < live)
        def _():
            products, targets = [], []
            for k in range(STEP):
                slot = first + k
                products.append(lax.dot_general(
                    tiles[slot], panel[source_ref[0, slot]], dims,
                    preferred_element_type=jnp.float32,
                ))
                targets.append(jnp.where(slot < live, target_ref[0, slot], blocks))
            for k in range(STEP):
                total[targets[k]] += products[k]


def block_product(panel, tiles, source_ids, target_ids, count, transposed):
    slots, block, _ = tiles.shape
    blocks, _, width = panel.shape
    smem = pl.BlockSpec(memory_space=pltpu.SMEM)
    vmem = pl.BlockSpec(memory_space=pltpu.VMEM)
    return pl.pallas_call(
        functools.partial(product_kernel, transposed),
        out_shape=jax.ShapeDtypeStruct((blocks + 1, block, width), jnp.float32),
        in_specs=[smem, smem, smem, vmem, vmem],
        out_specs=vmem,
        compiler_params=pltpu.CompilerParams(vmem_limit_bytes=26 << 20),
        cost_estimate=pl.CostEstimate(
            flops=2 * slots * block * block * width, transcendentals=0,
            bytes_accessed=2 * (tiles.size + 2 * panel.size),
        ),
    )(source_ids, target_ids, count, panel, tiles)


def on_device(
    features, node_order, block_rows, block_cols, block_counts, adjacency, weight_one, weight_two
):
    tiles = adjacency[0, 0]
    rows, cols = block_rows[0], block_cols[0]
    block, (slab, width) = tiles.shape[-1], features.shape
    row_panel = col_gather(node_order, features)
    partial_one = block_product(
        row_panel.reshape(-1, block, width), tiles, rows, cols, block_counts, True
    )
    col_panel = row_exchange(partial_one, weight_one, slab)
    partial_two = block_product(
        col_panel.reshape(-1, block, width), tiles, cols, rows, block_counts, False
    )
    return col_sum(partial_two, weight_two, slab)


def solution(mesh):
    in_specs = (
        P(("row", "col"), None),
        P(("row", "col"), None),
        P("row", "col", None),
        P("row", "col", None),
        P("row", "col"),
        P("row", "col", None, None, None),
        P(),
        P(),
    )
    out_specs = P(("row", "col"), None)
    return jax.shard_map(
        on_device, mesh=mesh, in_specs=in_specs, out_specs=out_specs, check_vma=False
    )
```

```python
import functools
import jax
import jax.numpy as jnp
from jax import lax
from jax.experimental import pallas as pl
from jax.experimental.pallas import tpu as pltpu
from jax.sharding import PartitionSpec as P

MESH = pl.DeviceIdType.MESH
PARTS = 4
ORDER = (
    ("r1o", 0), ("r1z", 0), ("r1x", 0), ("r1o", 2), ("r1z", 2), ("r2", 0), ("r1o", 1), ("r1o", 3),
    ("r1z", 1), ("r2", 2), ("r1z", 3), ("r3", 0), ("r1x", 2), ("r3", 2), ("r2", 1), ("r4", 0),
    ("r2", 3), ("r1x", 3), ("r5", 0), ("r4", 2), ("r3", 3), ("r1x", 1), ("d", 0), ("r5", 2),
    ("r3", 1), ("r4", 3), ("g3", 0), ("g2", 0), ("dx", 0), ("r5", 3), ("r4", 1), ("g3o", 0),
    ("d", 2), ("dx", 2), ("g4", 2), ("r5", 1), ("g4", 0), ("d", 3), ("dx", 3), ("g3", 2), ("g2", 2),
    ("d", 1), ("g3p", 0), ("g4", 3), ("g3", 3), ("g3o", 2), ("g2", 3), ("g2", 1), ("dx", 1),
    ("g3", 1), ("g5", 2), ("g5", 0), ("g4", 1), ("g3o", 3), ("g3o", 1), ("g4o", 2), ("g5", 3),
    ("g3p", 2), ("g5", 1), ("g4o", 0), ("g3p", 3), ("g3p", 1), ("g4o", 3), ("g4o", 1),
)


class Mail:
    def __init__(self, send_sem, recv_sem):
        self.send_sem, self.recv_sem, self.sent, self.arrived = send_sem, recv_sem, {}, set()

    def send(self, name, src, dst, device):
        slot = len(self.sent)
        copy = pltpu.make_async_remote_copy(
            src_ref=src, dst_ref=dst, send_sem=self.send_sem.at[slot],
            recv_sem=self.recv_sem.at[slot], device_id=device, device_id_type=MESH,
        )
        copy.start()
        self.sent[name] = copy

    def await_recv(self, *names):
        for name in names:
            if name not in self.arrived:
                self.sent[name].wait_recv()
                self.arrived.add(name)

    def finish(self):
        for copy in self.sent.values():
            copy.wait_send()


def greet(devices, meanwhile=None):
    barrier = pltpu.get_barrier_semaphore()
    for device in devices:
        pl.semaphore_signal(barrier, inc=1, device_id=device, device_id_type=MESH)
    if meanwhile is not None:
        meanwhile()
    pl.semaphore_wait(barrier, len(devices))


def add_rows(out, terms):
    rows = out.shape[0]
    step = next(s for s in (64, 48, 32, 16) if rows % s == 0)

    @pl.loop(0, rows // step)
    def _(i):
        at = pl.ds(pl.multiple_of(i * step, step), step)
        total = terms[0][at].astype(jnp.float32)
        for term in terms[1:]:
            total += term[at].astype(jnp.float32)
        out[at] = total.astype(out.dtype)


def round_slab(out, total, slab):
    block = total.shape[1]
    count = out.shape[0] // block

    @pl.loop(0, count)
    def _(j):
        at = pl.ds(pl.multiple_of(j * block, block), block)
        out[at] = total[slab * count + j].astype(out.dtype)


def dense_relu(out, terms, weight):
    total = terms[0][...].astype(jnp.float32)
    for term in terms[1:]:
        total += term[...].astype(jnp.float32)
    product = jnp.dot(total.astype(jnp.bfloat16), weight[...], preferred_element_type=jnp.float32)
    out[...] = jnp.maximum(product, 0.0).astype(out.dtype)


def row_kernel(
    total, weight, out, part, r1_l, r1_r, cz, r2_l, r2_r, r2o_l, r2o_r, cx_r, cx_l, r3m_l, r3m_r,
    r3b_l, r3a_r, r3a_l, r3b_r, sx, r4_l, r4_r, r5b_l, r5a_r, r5a_l, r5b_r, cs_r, cs_l, hid,
    send_sem, recv_sem, hid_sem,
):
    slab = part.shape[3]
    n = slab // PARTS
    h = n // 2
    me = lax.axis_index("row")
    z, x = me // 4, me % 4
    xr, xl, xo = (x + 1) % 4, (x + 3) % 4, (x + 2) % 4
    zr, zl, zo = (z + 1) % 4, (z + 3) % 4, (z + 2) % 4
    to_xr, to_xl = {"row": z * 4 + xr}, {"row": z * 4 + xl}
    to_zr, to_zl = {"row": zr * 4 + x}, {"row": zl * 4 + x}
    same, other = z % 2, 1 - z % 2

    def at(ref, zs, xs, rows):
        return ref.at[zs // 2, zs % 2, xs, rows]


    def round_x(*xs):
        for zs in (zr, zl, zo, z):
            for x_ in xs:
                round_slab(part.at[zs // 2, zs % 2, x_], total, zs * 4 + x_)

    greet((to_xr, to_xl, to_zr, to_zl), lambda: round_x(xo))
    mail = Mail(send_sem, recv_sem)

    def rows(p):
        return pl.ds(p * n, n), pl.ds(p * n, h), pl.ds(p * n + h, h)

    def r1z(p):
        n_, a, b = rows(p)
        mail.send(("r1r", p), at(part, zr, xo, n_), r1_l.at[p], to_zr)
        mail.send(("r1l", p), at(part, zl, xo, n_), r1_r.at[p], to_zl)

    def r1o(p):
        n_, a, b = rows(p)
        mail.send(("r2or", p), at(part, zo, xo, a), r2o_l.at[p], to_xr)
        mail.send(("r2ol", p), at(part, zo, xo, b), r2o_r.at[p], to_xl)

    def r1x(p):
        n_, a, b = rows(p)
        mail.send(("r3mr", p), part.at[:, other, xr, n_], r3m_l.at[p], to_xr)
        mail.send(("r3ml", p), part.at[:, other, xl, n_], r3m_r.at[p], to_xl)
        mail.send(("r3br", p), part.at[:, same, xr, b], r3b_l.at[p], to_xr)
        mail.send(("r3al", p), part.at[:, same, xl, a], r3a_r.at[p], to_xl)

    def r2(p):
        n_, a, b = rows(p)
        mail.await_recv(("r1r", p), ("r1l", p))
        add_rows(cz.at[p], (part.at[z // 2, same, xo, n_], r1_l.at[p], r1_r.at[p]))
        mail.send(("r2r", p), cz.at[p, pl.ds(0, h)], r2_l.at[p], to_xr)
        mail.send(("r2l", p), cz.at[p, pl.ds(h, h)], r2_r.at[p], to_xl)

    def r3(p):
        n_, a, b = rows(p)
        mail.await_recv(("r2r", p), ("r2or", p))
        add_rows(cx_r.at[p, z // 2], (part.at[z // 2, same, xr, a], r2_l.at[p]))
        add_rows(cx_r.at[p, zo // 2], (part.at[zo // 2, same, xr, a], r2o_l.at[p]))
        mail.send(("r3ar", p), cx_r.at[p], r3a_l.at[p], to_xr)
        mail.await_recv(("r2l", p), ("r2ol", p))
        add_rows(cx_l.at[p, z // 2], (part.at[z // 2, same, xl, b], r2_r.at[p]))
        add_rows(cx_l.at[p, zo // 2], (part.at[zo // 2, same, xl, b], r2o_r.at[p]))
        mail.send(("r3bl", p), cx_l.at[p], r3b_r.at[p], to_xl)

    def r4(p):
        n_, a, b = rows(p)
        first, second = pl.ds(0, h), pl.ds(h, h)
        mail.await_recv(("r3ar", p), ("r3al", p))
        for k in range(2):
            add_rows(sx.at[p, k, same, first], (part.at[k, same, x, a], r3a_l.at[p, k], r3a_r.at[p, k]))
        mail.send(("r4r", p), sx.at[p, zo // 2, same, first], r4_l.at[p], to_zr)
        mail.await_recv(("r3br", p), ("r3bl", p))
        for k in range(2):
            add_rows(sx.at[p, k, same, second], (part.at[k, same, x, b], r3b_l.at[p, k], r3b_r.at[p, k]))
        mail.send(("r4l", p), sx.at[p, zo // 2, same, second], r4_r.at[p], to_zl)
        mail.await_recv(("r3mr", p), ("r3ml", p))
        for k in range(2):
            add_rows(sx.at[p, k, other], (part.at[k, other, x, n_], r3m_l.at[p, k], r3m_r.at[p, k]))
        mail.send(("r5br", p), sx.at[p, zr // 2, other, second], r5b_l.at[p], to_zr)
        mail.send(("r5al", p), sx.at[p, zl // 2, other, first], r5a_r.at[p], to_zl)

    def r5(p):
        mail.await_recv(("r4r", p))
        add_rows(cs_r.at[p], (sx.at[p, zr // 2, other, pl.ds(0, h)], r4_l.at[p]))
        mail.send(("r5ar", p), cs_r.at[p], r5a_l.at[p], to_zr)
        mail.await_recv(("r4l", p))
        add_rows(cs_l.at[p], (sx.at[p, zl // 2, other, pl.ds(h, h)], r4_r.at[p]))
        mail.send(("r5bl", p), cs_l.at[p], r5b_r.at[p], to_zl)

    def dense(p):
        n_, a, b = rows(p)
        mine = sx.at[p, z // 2, same]
        mail.await_recv(("r5ar", p), ("r5al", p))
        dense_relu(hid.at[a], (mine.at[pl.ds(0, h)], r5a_l.at[p], r5a_r.at[p]), weight)
        mail.send(("g1ar", p), hid.at[a], at(out, z, x, a), to_zr)
        mail.await_recv(("r5br", p), ("r5bl", p))
        dense_relu(hid.at[b], (mine.at[pl.ds(h, h)], r5b_l.at[p], r5b_r.at[p]), weight)
        mail.send(("g1bl", p), hid.at[b], at(out, z, x, b), to_zl)
        mail.send(("g1br", p), hid.at[b], at(out, z, x, b), to_zr)
        mail.send(("g1al", p), hid.at[a], at(out, z, x, a), to_zl)
        pltpu.make_async_copy(hid.at[n_], at(out, z, x, n_), hid_sem.at[p]).start()

    def dense_x(p):
        n_, a, b = rows(p)
        mail.send(("g3ar", p), hid.at[a], at(out, z, x, a), to_xr)
        mail.send(("g3bl", p), hid.at[b], at(out, z, x, b), to_xl)
        mail.send(("g3br", p), hid.at[b], at(out, z, x, b), to_xr)
        mail.send(("g3al", p), hid.at[a], at(out, z, x, a), to_xl)

    def pass_on(name, p, zs, xs, rows_, to):
        mail.send((name, p), at(out, zs, xs, rows_), at(out, zs, xs, rows_), to)

    def g2(p):
        n_, a, b = rows(p)
        mail.await_recv(("g1ar", p))
        pass_on("g2r", p, zl, x, a, to_zr)
        mail.await_recv(("g1bl", p))
        pass_on("g2l", p, zr, x, b, to_zl)

    def g4(p):
        n_, a, b = rows(p)
        mail.await_recv(("g3ar", p))
        pass_on("g4r", p, z, xl, a, to_xr)
        mail.await_recv(("g3bl", p))
        pass_on("g4l", p, z, xr, b, to_xl)

    def g5(p):
        n_, a, b = rows(p)
        mail.await_recv(("g4r", p), ("g4l", p))
        pass_on("g5r", p, z, xo, n_, to_zr)
        pass_on("g5l", p, z, xo, n_, to_zl)

    def g3(p):
        n_, a, b = rows(p)
        mail.await_recv(("g1ar", p), ("g1bl", p), ("g1br", p), ("g1al", p))
        both = out.at[:, other, x, n_]
        mail.send(("g3mr", p), both, both, to_xr)
        mail.send(("g3ml", p), both, both, to_xl)

    def g3o(p):
        n_, a, b = rows(p)
        mail.await_recv(("g2r", p))
        pass_on("g3oar", p, zo, x, a, to_xr)
        mail.await_recv(("g2l", p))
        pass_on("g3obl", p, zo, x, b, to_xl)

    def g3p(p):
        n_, a, b = rows(p)
        pass_on("g3obr", p, zo, x, b, to_xr)
        pass_on("g3oal", p, zo, x, a, to_xl)

    def g4o(p):
        n_, a, b = rows(p)
        mail.await_recv(("g3oar", p))
        pass_on("g4or", p, zo, xl, a, to_xr)
        mail.await_recv(("g3obl", p))
        pass_on("g4ol", p, zo, xr, b, to_xl)

    def end(p):
        n_, a, b = rows(p)
        pltpu.make_async_copy(hid.at[n_], at(out, z, x, n_), hid_sem.at[p]).wait()
        mail.await_recv(*((name, p) for name in (
            "g3br", "g3al", "g3mr", "g3ml", "g3obr", "g3oal", "g4or", "g4ol", "g5r", "g5l"
        )))

    stages = dict(
        r1z=r1z, r1o=r1o, r1x=r1x, r2=r2, r3=r3, r4=r4, r5=r5, d=dense, dx=dense_x, g2=g2, g4=g4, g5=g5,
        g3=g3, g3o=g3o, g3p=g3p, g4o=g4o,
    )
    first_x = next(i for i, (name, _) in enumerate(ORDER) if name == "r1x")
    for i, (name, p) in enumerate(ORDER):
        if i == first_x:
            round_x(xr, xl)
        stages[name](p)
        if i == first_x:
            round_x(x)
    for p in range(PARTS):
        end(p)
    mail.finish()


def row_exchange(total, weight, slab):
    width = total.shape[2]
    n = slab // PARTS
    h = n // 2
    dt = weight.dtype
    vmem = pl.BlockSpec(memory_space=pltpu.VMEM)
    count = 40 * PARTS

    def buf(*lead):
        return [pltpu.VMEM((PARTS, *lead, width), dt)]

    out = pl.pallas_call(
        row_kernel,
        out_shape=jax.ShapeDtypeStruct((2, 2, 4, slab, width), dt),
        in_specs=[vmem, vmem],
        out_specs=vmem,
        scratch_shapes=(
            [pltpu.VMEM((2, 2, 4, slab, width), dt)]
            + buf(n) * 3 + buf(h) * 4 + buf(2, h) * 2 + buf(2, n) * 2 + buf(2, h) * 4
            + buf(2, 2, n) + buf(h) * 8
            + [pltpu.VMEM((slab, width), dt)]
            + [pltpu.SemaphoreType.DMA((count,))] * 2
            + [pltpu.SemaphoreType.DMA((PARTS,))]
        ),
        compiler_params=pltpu.CompilerParams(
            collective_id=1, has_side_effects=True, vmem_limit_bytes=20 << 20
        ),
    )(total, weight)
    return out.reshape(16, slab, width)


def tail_rows(slab):
    return max(slab // 96, 1) * 16


def gather_kernel(order, features, out, own, send_sem, recv_sem, own_sem):
    slab = features.shape[0]
    h = slab // 4
    me = lax.axis_index("col")
    zp, y, c = me // 8, (me // 2) % 4, me % 2
    yr, yl, yo, zq = (y + 1) % 4, (y + 3) % 4, (y + 2) % 4, 1 - zp
    to_r, to_l = {"col": zp * 8 + yr * 2 + c}, {"col": zp * 8 + yl * 2 + c}
    to_z, to_c = {"col": zq * 8 + y * 2 + c}, {"col": zp * 8 + y * 2 + 1 - c}

    def place(q):
        at = pl.ds(q * h, h)
        chosen = lax.broadcasted_iota(jnp.int32, (slab, h), 0) == order[:, at]
        own[at] = lax.dot_general(
            chosen.astype(features.dtype), features[...], (((0,), (0,)), ((), ())),
            preferred_element_type=jnp.float32,
        ).astype(own.dtype)

    def begin():
        for q in (0, 2):
            place(q)

    greet((to_r, to_l, to_z, to_c), begin)
    mail = Mail(send_sem, recv_sem)
    whole, cut = pl.ds(0, slab), tail_rows(slab)
    tail = pl.ds(slab - cut, cut)

    def send_own(name, q, to):
        rows = pl.ds(q * h, h)
        mail.send((name, q), own.at[rows], out.at[zp, y, c, rows], to)

    def send_on(name, zs, ys, rows, to):
        mail.send(name, out.at[zs, ys, c, rows], out.at[zs, ys, c, rows], to)

    def quarter(q):
        return pl.ds(q * h, h)

    def short(q):
        return pl.ds(q * h, h - cut if q == 3 else h)

    for q in (0, 2):
        send_own("r" if q == 0 else "l", q, to_r if q == 0 else to_l)
        send_own("z", q, to_z)
    for q in (1, 3):
        place(q)
        send_own("r" if q == 1 else "l", q, to_r if q == 1 else to_l)
        send_own("z", q, to_z)
    send_own("r", 2, to_r)
    send_own("l", 0, to_l)
    mail.send("c0", own, out.at[zp, y, c], to_c)
    own_copy = pltpu.make_async_copy(own, out.at[zp, y, c], own_sem)
    own_copy.start()
    mail.await_recv(("r", 0))
    send_on(("fr", 0), zp, yl, quarter(0), to_r)
    mail.await_recv(("l", 2))
    send_on(("fl", 2), zp, yr, quarter(2), to_l)
    send_own("r", 3, to_r)
    send_own("l", 1, to_l)
    mail.await_recv(("r", 1))
    send_on(("fr", 1), zp, yl, quarter(1), to_r)
    mail.await_recv(("l", 3))
    send_on(("fl", 3), zp, yr, quarter(3), to_l)
    send_on("tr", zp, yr, tail, to_z)
    for q in (0, 2):
        mail.await_recv(("z", q))
        send_on(("pr", q), zq, y, short(q), to_r)
        send_on(("pl", q), zq, y, short(q), to_l)
    mail.await_recv(("fr", 0))
    send_on(("zo", 0), zp, yo, quarter(0), to_z)
    mail.await_recv(("fl", 2))
    send_on(("zo", 2), zp, yo, quarter(2), to_z)
    for q in (1, 3):
        mail.await_recv(("z", q))
        send_on(("pr", q), zq, y, short(q), to_r)
        send_on(("pl", q), zq, y, short(q), to_l)
    send_on("c1", zq, y, whole, to_c)
    mail.await_recv(("r", 2), ("r", 3), ("l", 0), ("l", 1))
    send_on("tl", zp, yl, tail, to_z)
    send_on("c2", zp, yl, whole, to_c)
    send_on("c3", zp, yr, whole, to_c)
    mail.await_recv(("fr", 1))
    send_on(("zo", 1), zp, yo, quarter(1), to_z)
    mail.await_recv(("fl", 3))
    send_on(("zo", 3), zp, yo, quarter(3), to_z)
    send_on("c4", zp, yo, whole, to_c)
    last = []
    for q in (0, 2, 1, 3):
        for name, zs, ys in (("pr", zq, yl), ("pl", zq, yr), ("zo", zq, yo)):
            mail.await_recv((name, q))
            last.append(("c" + name, q))
            send_on(last[-1], zs, ys, quarter(q) if name == "zo" else short(q), to_c)
        if q == 1:
            for name, ys in (("tr", yr), ("tl", yl)):
                mail.await_recv(name)
                last.append("c" + name)
                send_on(last[-1], zq, ys, tail, to_c)
    own_copy.wait()
    mail.await_recv("c0", "c1", "c2", "c3", "c4", *last)
    mail.finish()


def col_gather(order, features):
    slab, width = features.shape
    vmem = pl.BlockSpec(memory_space=pltpu.VMEM)
    out = pl.pallas_call(
        gather_kernel,
        out_shape=jax.ShapeDtypeStruct((2, 4, 2, slab, width), features.dtype),
        in_specs=[vmem, vmem],
        out_specs=vmem,
        scratch_shapes=[
            pltpu.VMEM((slab, width), features.dtype),
            pltpu.SemaphoreType.DMA((49,)),
            pltpu.SemaphoreType.DMA((49,)),
            pltpu.SemaphoreType.DMA,
        ],
        compiler_params=pltpu.CompilerParams(
            collective_id=0, has_side_effects=True, vmem_limit_bytes=12 << 20
        ),
    )(order, features)
    return out.reshape(16, slab, width)


def sum_kernel(
    total, weight, out, mine, sib, both, z1, s2_l, s2_r, s3_l, s3_r, opp, s4b_l, s4b_r, s4a_l, s4a_r,
    c_r, c_l, z2, t_r, t_l, send_sem, recv_sem,
):
    slab = out.shape[0]
    h = slab // 2
    block = total.shape[1]
    count = slab // block
    me = lax.axis_index("col")
    zp, y, c = me // 8, (me // 2) % 4, me % 2
    yr, yl, yo, zq, d = (y + 1) % 4, (y + 3) % 4, (y + 2) % 4, 1 - zp, 1 - c
    to_r, to_l = {"col": zp * 8 + yr * 2 + c}, {"col": zp * 8 + yl * 2 + c}
    to_z, to_c = {"col": zq * 8 + y * 2 + c}, {"col": zp * 8 + y * 2 + d}
    a, b = pl.ds(0, h), pl.ds(h, h)
    cut = tail_rows(slab)
    head, tail = pl.ds(0, slab - cut), pl.ds(slab - cut, cut)
    dests = ((zq, yo), (zq, yr), (zq, yl), (zp, yr), (zp, yl), (zp, yo), (zq, y), (zp, y))
    greet((to_r, to_l, to_z, to_c))
    mail = Mail(send_sem, recv_sem)
    quarters = [pl.ds(q * (h // 2), h // 2) for q in range(4)]
    turns = (0, 2, 1, 3)

    def slab_of(i, core):
        zs, ys = dests[i]
        return (zs * 4 + ys) * 2 + core

    def give(i):
        round_slab(mine.at[i], total, slab_of(i, d))
        if i > 0:
            mail.send(("c", i), mine.at[i], sib.at[i], to_c)

    def join(i):
        if i > 0:
            mail.await_recv(("c", i))

        @pl.loop(0, count)
        def _(j):
            at = pl.ds(pl.multiple_of(j * block, block), block)
            both[i, at] = (
                total[slab_of(i, c) * count + j] + sib[i, at].astype(jnp.float32)
            ).astype(both.dtype)

    give(0)
    for q in turns:
        mail.send(("c0", q), mine.at[0, quarters[q]], sib.at[0, quarters[q]], to_c)
    for i in (1, 2):
        give(i)
    mail.await_recv(*(("c0", q) for q in turns))
    join(0)
    for q in turns:
        mail.send(("z1", q), both.at[0, quarters[q]], z1.at[quarters[q]], to_z)
    for i in (5, 3, 4, 6, 7):
        give(i)
    join(1)
    mail.send("s2r", both.at[1, head], s2_l, to_r)
    join(2)
    mail.send("s2l", both.at[2, head], s2_r, to_l)
    mail.send("tr", both.at[1, tail], t_r, to_z)
    mail.send("tl", both.at[2, tail], t_l, to_z)
    for i in (5, 3, 4, 6, 7):
        join(i)
    for q in turns:
        rows, half = quarters[q], quarters[q % 2]
        mail.await_recv(("z1", q))
        add_rows(opp.at[rows], (both.at[5, rows], z1.at[rows]))
        if q < 2:
            mail.send(("s3r", q), opp.at[rows], s3_l.at[half], to_r)
        else:
            mail.send(("s3l", q), opp.at[rows], s3_r.at[half], to_l)
    mail.await_recv("tr", "tl")
    add_rows(both.at[3, tail], (both.at[3, tail], t_r))
    add_rows(both.at[4, tail], (both.at[4, tail], t_l))
    mail.send("s4br", both.at[3, b], s4b_l, to_r)
    mail.send("s4bl", both.at[4, a], s4b_r, to_l)
    mail.await_recv("s2r", "s2l")
    add_rows(both.at[6, head], (both.at[6, head], s2_l, s2_r))
    mail.send("z2", both.at[6], z2, to_z)
    for q in turns:
        rows, half = quarters[q], quarters[q % 2]
        if q < 2:
            mail.await_recv(("s3r", q))
            add_rows(c_r.at[half], (both.at[3, rows], s3_l.at[half]))
            mail.send(("s4ar", q), c_r.at[half], s4a_l.at[half], to_r)
        else:
            mail.await_recv(("s3l", q))
            add_rows(c_l.at[half], (both.at[4, rows], s3_r.at[half]))
            mail.send(("s4al", q), c_l.at[half], s4a_r.at[half], to_l)
    mail.await_recv("s4bl", "s4br", "z2")
    for q in turns:
        rows, half = quarters[q], quarters[q % 2]
        mail.await_recv(("s4ar" if q < 2 else "s4al", q))
        near = (s4a_l, s4b_r) if q < 2 else (s4a_r, s4b_l)
        dense_relu(
            out.at[rows], (both.at[7, rows], near[0].at[half], near[1].at[half], z2.at[rows]), weight
        )
    mail.finish()


def col_sum(total, weight, slab):
    width = total.shape[2]
    dt, h, cut = weight.dtype, slab // 2, tail_rows(slab)
    vmem = pl.BlockSpec(memory_space=pltpu.VMEM)
    full, half = pltpu.VMEM((slab, width), dt), pltpu.VMEM((h, width), dt)
    return pl.pallas_call(
        sum_kernel,
        out_shape=jax.ShapeDtypeStruct((slab, width), dt),
        in_specs=[vmem, vmem],
        out_specs=vmem,
        scratch_shapes=(
            [pltpu.VMEM((8, slab, width), dt)] * 3
            + [full] + [pltpu.VMEM((slab - cut, width), dt)] * 2 + [half] * 2 + [full] + [half] * 6
            + [full] + [pltpu.VMEM((cut, width), dt)] * 2
            + [pltpu.SemaphoreType.DMA((30,))] * 2
        ),
        compiler_params=pltpu.CompilerParams(
            collective_id=2, has_side_effects=True, vmem_limit_bytes=20 << 20
        ),
    )(total, weight)


STEP = 64


def product_kernel(
    transposed, source_ref, target_ref, count_ref, panel, tiles, total
):
    slots = tiles.shape[0]
    blocks = panel.shape[0]
    live = count_ref[0, 0]

    @pl.loop(0, blocks)
    def _(g):
        total[g] = jnp.zeros_like(total[g])

    dims = (((0,), (0,)), ((), ())) if transposed else (((1,), (0,)), ((), ()))

    @pl.loop(0, slots // STEP)
    def _(step):
        first = step * STEP

        @pl.when(first < live)
        def _():
            products, targets = [], []
            for k in range(STEP):
                slot = first + k
                products.append(lax.dot_general(
                    tiles[slot], panel[source_ref[0, slot]], dims,
                    preferred_element_type=jnp.float32,
                ))
                targets.append(jnp.where(slot < live, target_ref[0, slot], blocks))
            for k in range(STEP):
                total[targets[k]] += products[k]


def block_product(panel, tiles, source_ids, target_ids, count, transposed):
    slots, block, _ = tiles.shape
    blocks, _, width = panel.shape
    smem = pl.BlockSpec(memory_space=pltpu.SMEM)
    vmem = pl.BlockSpec(memory_space=pltpu.VMEM)
    return pl.pallas_call(
        functools.partial(product_kernel, transposed),
        out_shape=jax.ShapeDtypeStruct((blocks + 1, block, width), jnp.float32),
        in_specs=[smem, smem, smem, vmem, vmem],
        out_specs=vmem,
        compiler_params=pltpu.CompilerParams(vmem_limit_bytes=26 << 20),
        cost_estimate=pl.CostEstimate(
            flops=2 * slots * block * block * width, transcendentals=0,
            bytes_accessed=2 * (tiles.size + 2 * panel.size),
        ),
    )(source_ids, target_ids, count, panel, tiles)


def on_device(
    features, node_order, block_rows, block_cols, block_counts, adjacency, weight_one, weight_two
):
    tiles = adjacency[0, 0]
    rows, cols = block_rows[0], block_cols[0]
    block, (slab, width) = tiles.shape[-1], features.shape
    row_panel = col_gather(node_order, features)
    partial_one = block_product(
        row_panel.reshape(-1, block, width), tiles, rows, cols, block_counts, True
    )
    col_panel = row_exchange(partial_one, weight_one, slab)
    partial_two = block_product(
        col_panel.reshape(-1, block, width), tiles, cols, rows, block_counts, False
    )
    return col_sum(partial_two, weight_two, slab)


def solution(mesh):
    in_specs = (
        P(("row", "col"), None),
        P(("row", "col"), None),
        P("row", "col", None),
        P("row", "col", None),
        P("row", "col"),
        P("row", "col", None, None, None),
        P(),
        P(),
    )
    out_specs = P(("row", "col"), None)
    return jax.shard_map(
        on_device, mesh=mesh, in_specs=in_specs, out_specs=out_specs, check_vma=False
    )
```
